256 devices in a mesh: gx: 4 (over y_hi, core), yz: 64 (over x, z, y_lo).
Axes of the slice: x: 4, y: 4 (y_hi: 2, y_lo: 2; y = y_hi * 2 + y_lo), z: 8, core: 2. Of those that a mesh axis runs over, the one named last changes fastest.
Arguments:
- prefill_tokens: bfloat16 [512, 18432], P('gx'), may hold values from -6 to 6
- prefill_lengths: int32 [4], P('gx'), may hold values from 1 to 128, as said below
- decode_tokens: bfloat16 [2, 256, 18432], P(None, None, ('gx', 'yz')), may hold values from -6 to 6
- cache_lengths: int32 [256], P(('gx', 'yz')), may hold values from 1 to 2048, as said below
- cache_keyvals: bfloat16 [256, 2048, 512], P(('gx', 'yz')), may hold values from -6 to 6
- query_weight: bfloat16 [18432, 12288], P('gx', 'yz')
- keyval_weight: bfloat16 [18432, 512], P('gx', 'yz')
- out_weight: bfloat16 [12288, 18432], P('yz', 'gx'), may hold values from -0.0546875 to 0.0546875
Outputs:
- prefill_out: bfloat16 [512, 18432], P('gx', 'yz')
- decode_out: bfloat16 [2, 256, 18432], P(None, None, ('gx', 'yz'))
The draws below stay inside these ranges and needn't reach their ends.
Inputs may be any that keep to these rules, and one draw needn't show every extreme that they name: `prefill_lengths`: some prefill sequence has exactly 128 valid positions. `cache_lengths`: some decode row has exactly 2048 valid cached positions.
All inputs are finite; a program needn't handle non-finite values.
Results may differ from the reference program's by a relative error of at most 0.015.
Values may be sent and summed in bfloat16 or wider, within the bound.
A program may use at most 128 MiB of HBM per device.

```python
import jax
import jax.numpy as jnp

D = 18432
HEADS = 48
HD = 256
QW = 12288
PLEN = 128
PSEQS = 4
PTOK = 512
STEPS = 2
ROWS = 256
CACHE = 2048


def head_block(key):
    return jax.random.normal(jax.random.fold_in(key, 101), (D, HD), jnp.float32) * D ** (-0.5)


def draw_query_weight(key, part):
    first_head = head_block(key)
    key = jax.random.fold_in(key, 2)
    others = jax.random.normal(key, (D, QW - HD), jnp.float32) * D ** (-0.5)
    return jnp.concatenate([first_head, others], axis=1).astype(jnp.bfloat16)


def draw_keyval_weight(key, part):
    key = jax.random.fold_in(key, 3)
    fresh_values = jax.random.normal(key, (D, 2 * HD), jnp.float32) * D ** (-0.5)
    return fresh_values.astype(jnp.bfloat16)


def draw_prefill_lengths(key, part):
    key = jax.random.fold_in(key, 4)
    uniform_draw = jax.random.randint(jax.random.fold_in(key, 1), (PSEQS,), 1, PLEN + 1)
    chosen = jax.random.randint(jax.random.fold_in(key, 2), (), 0, PSEQS)
    return jnp.where(jnp.arange(PSEQS) == chosen, PLEN, uniform_draw).astype(jnp.int32)


def draw_cache_lengths(key, part):
    key = jax.random.fold_in(key, 5)
    uniform_draw = jax.random.randint(jax.random.fold_in(key, 1), (ROWS,), 1, CACHE + 1)
    chosen = jax.random.randint(jax.random.fold_in(key, 2), (), 0, ROWS)
    return jnp.where(jnp.arange(ROWS) == chosen, CACHE, uniform_draw).astype(jnp.int32)


def block_scale(rng, extent, cuts, smallest, top_value):
    def one(axis_at, blocks):
        heights = jax.random.uniform(jax.random.fold_in(jax.random.fold_in(rng, 6), axis_at), (blocks,), jnp.float32, smallest / len(cuts), top_value / len(cuts))
        return jnp.repeat(jnp.exp(heights), extent[axis_at] // blocks).reshape((-1,) + (1,) * (len(extent) - axis_at - 1))

    level = one(*cuts[0])
    for cut in cuts[1:]:
        level = level * one(*cut)
    return level


def scatter_about(own_key, extent, scale, most, shards=(), kind=jnp.bfloat16):
    array = jax.random.normal(own_key, extent, jnp.float32) * scale
    if len(shards) > 0:
        array = block_scale(own_key, extent, shards, -0.22, 0.18) * array
    return jnp.clip(array, min=-most, max=most).astype(kind)


def setup_inputs(seed: int = 0) -> dict:
    key_list = jax.random.split(jax.random.key(seed), 9)
    prefill_tokens = scatter_about(key_list[0], (PTOK, D), 1.0, 6.0, ((0, 4),))
    prefill_lengths = draw_prefill_lengths(jax.random.fold_in(key_list[8], 71), 0)
    decode_tokens = scatter_about(key_list[2], (STEPS, ROWS, D), 1.0, 6.0, ((2, 256),))
    cache_lengths = draw_cache_lengths(jax.random.fold_in(key_list[8], 71), 0)
    cache_keyvals = scatter_about(key_list[4], (ROWS, CACHE, 2 * HD), 1.0, 6.0, ((0, 256),))
    query_weight = draw_query_weight(jax.random.fold_in(key_list[8], 71), 0)
    keyval_weight = draw_keyval_weight(jax.random.fold_in(key_list[8], 71), 0)
    out_weight = scatter_about(key_list[7], (QW, D), QW ** -0.5, 0.0546875, ((0, 64), (1, 4)))
    return {"prefill_tokens": prefill_tokens, "prefill_lengths": prefill_lengths, "decode_tokens": decode_tokens, "cache_lengths": cache_lengths, "cache_keyvals": cache_keyvals, "query_weight": query_weight, "keyval_weight": keyval_weight, "out_weight": out_weight}


def softmax_rounded(scores):
    peak_score = jnp.max(scores, axis=-1, keepdims=True)
    exponent = jnp.exp(scores - peak_score)
    return (exponent / jnp.sum(exponent, axis=-1, keepdims=True)).astype(jnp.bfloat16)


def reference(prefill_tokens, prefill_lengths, decode_tokens, cache_lengths, cache_keyvals, query_weight, keyval_weight, out_weight):
    score_scale = HD ** -0.5
    masked_score = -1e30
    pre_query = jnp.dot(prefill_tokens, query_weight, preferred_element_type=jnp.float32).astype(jnp.bfloat16)
    pre_keyval = jnp.dot(prefill_tokens, keyval_weight, preferred_element_type=jnp.float32).astype(jnp.bfloat16)
    seq_count = prefill_lengths.shape[0]
    queries = pre_query.reshape(seq_count, PLEN, HEADS, HD).astype(jnp.float32)
    keyvals = pre_keyval.reshape(seq_count, PLEN, 2 * HD).astype(jnp.float32)
    scores = jnp.einsum("sqhd,skd->sqhk", queries, keyvals[..., :HD]) * score_scale
    positions = jnp.arange(PLEN, dtype=jnp.int32)
    allowed = (positions[None, None, :] <= positions[None, :, None]) & (positions[None, None, :] < prefill_lengths[:, None, None])
    scores = jnp.where(allowed[:, :, None, :], scores, masked_score)
    pre_probs = softmax_rounded(scores)
    attended = jnp.einsum("sqhk,skd->sqhd", pre_probs.astype(jnp.float32), keyvals[..., HD:])
    attended = attended.astype(jnp.bfloat16).reshape(PTOK, QW)
    prefill_out = jnp.dot(attended, out_weight, preferred_element_type=jnp.float32).astype(jnp.bfloat16)

    cache_keys = cache_keyvals[:, :, :HD].astype(jnp.float32)
    cache_values = cache_keyvals[:, :, HD:].astype(jnp.float32)
    visible = jnp.arange(CACHE, dtype=jnp.int32)[None, :] < cache_lengths[:, None]
    fresh_list = []
    step_outputs = []
    for step_index in range(STEPS):
        dec_query = jnp.dot(decode_tokens[step_index], query_weight, preferred_element_type=jnp.float32).astype(jnp.bfloat16)
        dec_keyval = jnp.dot(decode_tokens[step_index], keyval_weight, preferred_element_type=jnp.float32).astype(jnp.bfloat16)
        fresh_list.append(dec_keyval)
        new_keyvals = jnp.stack(fresh_list, axis=1).astype(jnp.float32)
        row_queries = dec_query.reshape(ROWS, HEADS, HD).astype(jnp.float32)
        cache_scores = jnp.einsum("rhd,rld->rhl", row_queries, cache_keys) * score_scale
        cache_scores = jnp.where(visible[:, None, :], cache_scores, masked_score)
        fresh_scores = jnp.einsum("rhd,rnd->rhn", row_queries, new_keyvals[..., :HD]) * score_scale
        peak_score = jnp.maximum(jnp.max(cache_scores, axis=-1, keepdims=True), jnp.max(fresh_scores, axis=-1, keepdims=True))
        cache_exp = jnp.exp(cache_scores - peak_score)
        fresh_exp = jnp.exp(fresh_scores - peak_score)
        denominator = jnp.sum(cache_exp, axis=-1, keepdims=True) + jnp.sum(fresh_exp, axis=-1, keepdims=True)
        cache_probs = (cache_exp / denominator).astype(jnp.bfloat16)
        fresh_probs = (fresh_exp / denominator).astype(jnp.bfloat16)
        attended_rows = jnp.einsum("rhl,rld->rhd", cache_probs.astype(jnp.float32), cache_values)
        attended_rows = attended_rows + jnp.einsum("rhn,rnd->rhd", fresh_probs.astype(jnp.float32), new_keyvals[..., HD:])
        attended_rows = attended_rows.astype(jnp.bfloat16).reshape(ROWS, QW)
        step_outputs.append(jnp.dot(attended_rows, out_weight, preferred_element_type=jnp.float32).astype(jnp.bfloat16))
    return prefill_out, jnp.stack(step_outputs, axis=0)
```

```python
import functools
import heapq

import jax
import jax.numpy as jnp
from jax import lax
from jax.experimental import pallas as pl
from jax.experimental.pallas import tpu as pltpu
from jax.sharding import PartitionSpec as P

HEADS = 48
HD = 256
PLEN = 128
GX, X, Z, YL = 4, 4, 8, 2
BLK = 144
TOK = 1024
WIDTH = {"a": 640, "b": 384}
COLS = 192
KVC = 8
ROWS1 = 208
MESH = pl.DeviceIdType.MESH
F32 = jnp.float32
BF16 = jnp.bfloat16
FULL, UPPER, LOWER = (0, 144), (0, 80), (80, 64)


def steps_from(key):
    kind, xo, zo = key
    out = []
    if kind == "a":
        if xo == 0:
            if -3 < zo <= 0:
                out.append(("z+", FULL, ("a", 0, zo - 1)))
            if zo == -3:
                out.append(("z+", UPPER, ("a", 0, 4)))
            if 0 <= zo < 3:
                out.append(("z-", FULL, ("a", 0, zo + 1)))
            if zo == 3:
                out.append(("z-", LOWER, ("a", 0, 4)))
            out.append(("x+", FULL, ("a", -1, zo)))
            out.append(("x-", FULL, ("a", 1, zo)))
        elif xo == -1 and zo % 2 == 0:
            out.append(("x+", FULL, ("a", 2, zo)))
        elif xo == 1 and zo % 2 == 1:
            out.append(("x-", FULL, ("a", 2, zo)))
    else:
        if zo == 0:
            if xo == 0:
                out.append(("x+", FULL, ("b", -1, 0)))
                out.append(("x-", FULL, ("b", 1, 0)))
            elif xo == -1:
                out.append(("x+", UPPER, ("b", 2, 0)))
            elif xo == 1:
                out.append(("x-", LOWER, ("b", 2, 0)))
        if zo <= 0 and (zo > -3 or xo in (0, 2)):
            out.append(("z+", FULL, ("b", xo, zo - 1 if zo > -3 else 4)))
        if 0 <= zo <= 3 and (zo < 3 or xo in (-1, 1)):
            out.append(("z-", FULL, ("b", xo, zo + 1)))
    return out


def make_plan():
    free = {d: 0.0 for d in ("x+", "x-", "z+", "z-")}
    events, order, missing, pieces = [], [], {}, {}
    count = 0

    def leave(key, now):
        nonlocal count
        order.append(key)
        for d, rows, there in steps_from(key):
            free[d] = max(free[d], now) + WIDTH[key[0]] * rows[1] / 147456.0 * 2.95
            count += 1
            heapq.heappush(events, (free[d] + 1.0, count, there, (d, rows)))

    order_own = [("b", 0, 0), ("a", 0, 0)]
    for key in order_own:
        leave(key, 0.0)
    while events:
        now, _, key, piece = heapq.heappop(events)
        pieces.setdefault(key, []).append(piece)
        got = sum(p[1][1] for p in pieces[key])
        if got == BLK:
            leave(key, now)
    assert len(order) == 64
    return order, pieces


ORDER, PIECES = make_plan()
OPPOSITE = {"x+": "x-", "x-": "x+", "z+": "z-", "z-": "z+"}
SENDS = {}
for _key in ORDER:
    for _n, _step in enumerate(steps_from(_key)):
        SENDS[(_key, _n)] = len(SENDS)
NSEND = len(SENDS)
FILLS = {}
for _key in ORDER:
    for _n, (_d, _rows, _there) in enumerate(steps_from(_key)):
        FILLS[(_there, _rows)] = SENDS[(_key, _n)]
SLOTS = {k: [key for key in ORDER for _ in steps_from(key) if key[0] == k] for k in "ab"}


def place():
    gx = lax.axis_index("gx")
    yz = lax.axis_index("yz")
    return gx, yz // (Z * YL), (yz // YL) % Z, yz % YL


def device_at(gx, x, z, yl, d):
    dx = {"x+": 1, "x-": X - 1}.get(d, 0)
    dz = {"z+": 1, "z-": Z - 1}.get(d, 0)
    return (gx, ((x + dx) % X) * (Z * YL) + ((z + dz) % Z) * YL + yl)


def greet(gx, x, z, yl):
    barrier = pltpu.get_barrier_semaphore()
    yz = lax.axis_index("yz")
    for d in ("x+", "x-", "z+", "z-"):
        pl.semaphore_signal(barrier, inc=1, device_id=device_at(gx, x, z, yl, d), device_id_type=MESH)
    for g in range(1, GX):
        pl.semaphore_signal(barrier, inc=1, device_id=((gx + g) % GX, yz), device_id_type=MESH)
    pl.semaphore_wait(barrier, 4 + GX - 1)


def project_kernel(xa, xb, wq, wkv, out, ga, gb, w, acc, give, take, send, recv, rsend, rrecv):
    gx, x, z, yl = place()
    yz = lax.axis_index("yz")
    own = {"a": xa, "b": xb}
    held = {"a": ga, "b": gb}

    def slot(key, rows):
        kind, xo, zo = key
        first = pl.multiple_of(((z + zo) % Z) * BLK + rows[0], 16)
        return held[kind].at[(x + xo) % X, pl.ds(first, rows[1])]

    def copy(key, n):
        d, rows, there = steps_from(key)[n]
        k = SENDS[(key, n)]
        src = own[key[0]] if key[1:] == (0, 0) else slot(key, rows)
        return pltpu.make_async_remote_copy(
            src_ref=src,
            dst_ref=slot(key, rows),
            send_sem=send.at[k],
            recv_sem=recv.at[k],
            device_id=device_at(gx, x, z, yl, d),
            device_id_type=MESH,
        )

    def arrived(key):
        for _, rows in PIECES[key]:
            k = FILLS[(key, rows)]
            pltpu.make_async_remote_copy(
                src_ref=slot(key, rows),
                dst_ref=slot(key, rows),
                send_sem=send.at[k],
                recv_sem=recv.at[k],
                device_id=device_at(gx, x, z, yl, "x+"),
                device_id_type=MESH,
            ).wait_recv()

    greet(gx, x, z, yl)
    copies = []
    seen = {}

    def multiply(kind, xo):
        xx = (x + xo) % X
        lanes = slice(0, WIDTH["a"]) if kind == "a" else slice(WIDTH["a"], TOK)
        part = lax.dot_general(
            w[pl.ds(pl.multiple_of(xx * (Z * BLK), 128), Z * BLK), :],
            held[kind][xx],
            (((0,), (0,)), ((), ())),
            preferred_element_type=F32,
        )
        if (kind, "first") in seen:
            acc[:, lanes] += part
        else:
            acc[:, lanes] = part
            seen[(kind, "first")] = True

    for key in ORDER:
        kind, xo, zo = key
        if (xo, zo) != (0, 0):
            arrived(key)
        for n in range(len(steps_from(key))):
            c = copy(key, n)
            c.start()
            copies.append(c)
        if (xo, zo) == (0, 0):
            first = pl.multiple_of(z * BLK, 16)
            held[kind][x, pl.ds(first, BLK), :] = own[kind][...]
        if key == ("a", 0, 0):
            w[:, :COLS] = wq[...]
            w[:, COLS:] = jnp.zeros((wq.shape[0], 256 - COLS), BF16)
            w[:, COLS : COLS + KVC] = wkv[...]
        seen[(kind, xo)] = seen.get((kind, xo), 0) + 1
        if seen[(kind, xo)] == Z:
            multiply(kind, xo)

    for g in range(GX):
        give[g, :, :128] = acc[:ROWS1, g * 128 : g * 128 + 128].astype(give.dtype)
        give[g, :, 128:] = acc[:ROWS1, 512 + g * 128 : 640 + g * 128].astype(give.dtype)
    sums = []
    for s in range(1, GX):
        to = (gx + s) % GX
        c = pltpu.make_async_remote_copy(
            src_ref=give.at[to],
            dst_ref=take.at[s],
            send_sem=rsend.at[s],
            recv_sem=rrecv.at[s],
            device_id=(to, yz),
            device_id_type=MESH,
        )
        c.start()
        sums.append(c)
    for c in copies:
        c.wait_send()
    for c in sums:
        c.wait()
    total = give[gx].astype(F32)
    for s in range(1, GX):
        total = total + take[s].astype(F32)
    out[...] = total.astype(BF16)


def project(xa, xb, wq, wkv):
    depth = wq.shape[0]
    vmem = pl.BlockSpec(memory_space=pltpu.VMEM)
    return pl.pallas_call(
        project_kernel,
        out_shape=jax.ShapeDtypeStruct((ROWS1, 256), BF16),
        in_specs=[vmem] * 4,
        out_specs=vmem,
        scratch_shapes=[
            pltpu.VMEM((X, Z * BLK, WIDTH["a"]), BF16),
            pltpu.VMEM((X, Z * BLK, WIDTH["b"]), BF16),
            pltpu.VMEM((depth, 256), BF16),
            pltpu.VMEM((256, TOK), F32),
            pltpu.VMEM((GX, ROWS1, 256), F32),
            pltpu.VMEM((GX, ROWS1, 256), F32),
            pltpu.SemaphoreType.DMA((NSEND,)),
            pltpu.SemaphoreType.DMA((NSEND,)),
            pltpu.SemaphoreType.DMA((GX,)),
            pltpu.SemaphoreType.DMA((GX,)),
        ],
        compiler_params=pltpu.CompilerParams(
            collective_id=0, has_side_effects=True, vmem_limit_bytes=40 * 2**20
        ),
        name="gather_project",
    )(xa, xb, wq, wkv)


def output_kernel(att, wt, out_a, out_b, heads, dec, pa, pb, ra, rb, send, recv, hsend, hrecv):
    gx, x, z, yl = place()
    yz = lax.axis_index("yz")
    held = {"a": pa, "b": pb}
    landing = {"a": ra, "b": rb}
    where = {}
    used = {"a": 0, "b": 0}
    for key in ORDER:
        for n in range(len(steps_from(key))):
            where[(key, n)] = used[key[0]]
            used[key[0]] += 1

    greet(gx, x, z, yl)
    shares = []
    for s in range(1, GX):
        c = pltpu.make_async_remote_copy(
            src_ref=att,
            dst_ref=heads.at[s],
            send_sem=hsend.at[s],
            recv_sem=hrecv.at[s],
            device_id=((gx + s) % GX, yz),
            device_id_type=MESH,
        )
        c.start()
        shares.append(c)
    heads[0] = att[...]
    for c in shares:
        c.wait()
    for s in range(GX):
        lane = pl.multiple_of(((gx - s + GX) % GX) * 128, 128)
        dec[:, pl.ds(lane, 128)] = heads[s, :, :128]

    def terms(key):
        kind, xo, zo = key
        xx, zz = (x + xo) % X, (z + zo) % Z
        group = heads[(gx - xx + GX) % GX, :, 128:]

        def prefill(q):
            first = pl.multiple_of(zz * (4 * BLK) + q * BLK, 16)
            return jnp.dot(wt[pl.ds(first, BLK), :], group, preferred_element_type=F32)

        if kind == "a":
            first = pl.multiple_of((xx * Z + zz) * BLK, 16)
            return [
                (0, 512, jnp.dot(wt[pl.ds(first, BLK), :], dec[...], preferred_element_type=F32)),
                (512, 128, prefill(0)),
            ]
        return [(128 * q - 128, 128, prefill(q)) for q in (1, 2, 3)]

    copies = []
    for key in reversed(ORDER):
        kind, xo, zo = key
        last = (xo, zo) == (0, 0)
        xx, zz = (x + xo) % X, (z + zo) % Z
        local = terms(key)
        steps = steps_from(key)
        for n, (d, rows, there) in enumerate(steps):
            k = SENDS[(key, n)]
            spot = landing[kind].at[where[(key, n)], pl.ds(rows[0], rows[1])]
            pltpu.make_async_remote_copy(
                src_ref=spot,
                dst_ref=spot,
                send_sem=send.at[k],
                recv_sem=recv.at[k],
                device_id=device_at(gx, x, z, yl, d),
                device_id_type=MESH,
            ).wait_recv()
        for lane, width, value in local:
            pieces = [value[:80], value[80:]]
            for n, (d, rows, there) in enumerate(steps):
                for i, (r0, rn) in enumerate((UPPER, LOWER)):
                    if rows[0] <= r0 and r0 + rn <= rows[0] + rows[1]:
                        got = landing[kind][where[(key, n)], r0 : r0 + rn, lane : lane + width]
                        pieces[i] = pieces[i] + got.astype(F32)
            for i, (r0, rn) in enumerate((UPPER, LOWER)):
                if last:
                    target = {"a": out_a, "b": out_b}[kind]
                    target[r0 : r0 + rn, lane : lane + width] = pieces[i]
                else:
                    held[kind][xx * Z + zz, r0 : r0 + rn, lane : lane + width] = pieces[i].astype(BF16)
        if not last:
            for d, rows in PIECES[key]:
                k = FILLS[(key, rows)]
                source = [kn for kn, kk in SENDS.items() if kk == k][0]
                c = pltpu.make_async_remote_copy(
                    src_ref=held[kind].at[xx * Z + zz, pl.ds(rows[0], rows[1])],
                    dst_ref=landing[kind].at[where[source], pl.ds(rows[0], rows[1])],
                    send_sem=send.at[k],
                    recv_sem=recv.at[k],
                    device_id=device_at(gx, x, z, yl, OPPOSITE[d]),
                    device_id_type=MESH,
                )
                c.start()
                copies.append(c)
    for c in copies:
        c.wait_send()


def project_out(att, wt):
    vmem = pl.BlockSpec(memory_space=pltpu.VMEM)
    return pl.pallas_call(
        output_kernel,
        out_shape=(
            jax.ShapeDtypeStruct((BLK, WIDTH["a"]), F32),
            jax.ShapeDtypeStruct((BLK, WIDTH["b"]), F32),
        ),
        in_specs=[vmem] * 2,
        out_specs=(vmem, vmem),
        scratch_shapes=[
            pltpu.VMEM((GX, COLS, 256), BF16),
            pltpu.VMEM((COLS, 512), BF16),
            pltpu.VMEM((X * Z, BLK, WIDTH["a"]), BF16),
            pltpu.VMEM((X * Z, BLK, WIDTH["b"]), BF16),
            pltpu.VMEM((len(SLOTS["a"]), BLK, WIDTH["a"]), BF16),
            pltpu.VMEM((len(SLOTS["b"]), BLK, WIDTH["b"]), BF16),
            pltpu.SemaphoreType.DMA((NSEND,)),
            pltpu.SemaphoreType.DMA((NSEND,)),
            pltpu.SemaphoreType.DMA((GX,)),
            pltpu.SemaphoreType.DMA((GX,)),
        ],
        compiler_params=pltpu.CompilerParams(
            collective_id=1, has_side_effects=True, vmem_limit_bytes=48 * 2**20
        ),
        name="output_scatter",
    )(att, wt)


def attention_kernel(info, qd, fresh, cache, qp, kvt, od, op):
    scale = HD ** (-0.5)
    nt = (((1,), (1,)), ((), ()))
    length, prefill_length, first = info[0], info[1], info[2]
    q = qd[...]
    s = lax.dot_general(q, cache[:, :HD], nt, preferred_element_type=F32) * scale
    pos = lax.broadcasted_iota(jnp.int32, s.shape, 1)
    s = jnp.where(pos < length, s, -1e30)
    f = lax.dot_general(q, fresh[:, :HD], nt, preferred_element_type=F32) * scale
    step = lax.broadcasted_iota(jnp.int32, f.shape, 0) // HEADS
    new = lax.broadcasted_iota(jnp.int32, f.shape, 1)
    f = jnp.where(new <= step, f, -1e30)
    peak = jnp.maximum(jnp.max(s, axis=1, keepdims=True), jnp.max(f, axis=1, keepdims=True))
    es, ef = jnp.exp(s - peak), jnp.exp(f - peak)
    total = jnp.sum(es, axis=1, keepdims=True) + jnp.sum(ef, axis=1, keepdims=True)
    attended = jnp.dot((es / total).astype(BF16), cache[:, HD:], preferred_element_type=F32)
    attended += jnp.dot((ef / total).astype(BF16), fresh[:, HD:], preferred_element_type=F32)
    od[...] = attended.astype(BF16)

    s = jnp.dot(qp[...], kvt[:HD, :], preferred_element_type=F32) * scale
    query = first + lax.broadcasted_iota(jnp.int32, s.shape, 0) // HEADS
    pos = lax.broadcasted_iota(jnp.int32, s.shape, 1)
    s = jnp.where((pos <= query) & (pos < prefill_length), s, -1e30)
    e = jnp.exp(s - jnp.max(s, axis=1, keepdims=True))
    p = (e / jnp.sum(e, axis=1, keepdims=True)).astype(BF16)
    op[...] = lax.dot_general(p, kvt[HD:, :], nt, preferred_element_type=F32).astype(BF16)


def attend(info, qd, fresh, cache, qp, kvt):
    vmem = pl.BlockSpec(memory_space=pltpu.VMEM)
    shape = jax.ShapeDtypeStruct(qd.shape, BF16)
    return pl.pallas_call(
        attention_kernel,
        out_shape=(shape, shape),
        in_specs=[pl.BlockSpec(memory_space=pltpu.SMEM)] + [vmem] * 5,
        out_specs=(vmem, vmem),
        compiler_params=pltpu.CompilerParams(vmem_limit_bytes=32 * 2**20),
        name="attend",
    )(info, qd, fresh, cache, qp, kvt)


def body(
    prefill_tokens,
    prefill_lengths,
    decode_tokens,
    cache_lengths,
    cache_keyvals,
    query_weight,
    keyval_weight,
    out_weight,
):
    gx, x, z, yl = place()
    yz = lax.axis_index("yz")
    group = query_weight.shape[0]
    slices = [
        lax.dynamic_slice(prefill_tokens, (0, g * group + (x * Z + z) * BLK), (PLEN, BLK)).T
        for g in range(GX)
    ]
    pre = lax.all_to_all(jnp.stack(slices), "gx", split_axis=0, concat_axis=0, tiled=True)
    pre = pre.transpose(1, 0, 2).reshape(BLK, GX * PLEN)
    dec = decode_tokens.reshape(2, GX, 64, 72).transpose(3, 1, 0, 2).reshape(72, 512)
    other = lax.ppermute(dec, "yz", [(i, i ^ 1) for i in range(X * Z * YL)])
    dec = jnp.where(
        yl == 0, jnp.concatenate([dec, other], axis=0), jnp.concatenate([other, dec], axis=0)
    )
    xa = jnp.concatenate([dec, pre[:, : WIDTH["a"] - 512]], axis=1)
    xb = pre[:, WIDTH["a"] - 512 :]
    qkv = project(xa, xb, query_weight, keyval_weight)

    q = qkv[:COLS].T
    dq = q[:128].reshape(2, 64, COLS).transpose(1, 0, 2).reshape(64, 2 * COLS)
    pq = q[128:].reshape(64, 2 * COLS)
    kv = qkv[COLS : COLS + KVC]
    dkv = kv[:, :128].reshape(KVC, 2, 64).transpose(2, 1, 0).reshape(64, 2 * KVC)
    pkv = jnp.broadcast_to(kv[:, 128:].reshape(1, KVC * PLEN), (64, KVC * PLEN))
    pad = jnp.zeros((64, 112), BF16)
    sent = jnp.concatenate([pkv, dq, pq, dkv, pad], axis=1)
    got = lax.all_to_all(sent, "yz", split_axis=0, concat_axis=0, tiled=True)
    kvt = got[:, :1024].reshape(64 * KVC, PLEN)
    dq = got[:, 1024:1408].reshape(64, 2, COLS).transpose(1, 0, 2).reshape(2 * HEADS, HD)
    pq = got[:, 1408:1792].reshape(64, 2, COLS).transpose(1, 0, 2).reshape(2 * HEADS, HD)
    fresh = got[:, 1792:1808].reshape(64, 2, KVC).transpose(1, 0, 2).reshape(2, 64 * KVC)
    fresh = jnp.pad(fresh, ((0, 126), (0, 0)))
    info = jnp.stack([cache_lengths[0], prefill_lengths[0], yz * 2]).astype(jnp.int32)
    ad, ap = attend(info, dq, fresh, cache_keyvals[0], pq, kvt)

    ad = ad.reshape(2, 64, COLS).transpose(1, 0, 2).reshape(64, 2 * COLS)
    ap = ap.reshape(2, 64, COLS).transpose(1, 0, 2).reshape(64, 2 * COLS)
    got = lax.all_to_all(
        jnp.concatenate([ad, ap], axis=1), "yz", split_axis=0, concat_axis=0, tiled=True
    )
    ad = got[:, : 2 * COLS].reshape(64, 2, COLS).transpose(2, 1, 0).reshape(COLS, 128)
    ap = got[:, 2 * COLS :].reshape(PLEN, COLS).T
    out_a, out_b = project_out(jnp.concatenate([ad, ap], axis=1), out_weight.T)

    pre = jnp.concatenate([out_a[:, 512:], out_b], axis=1)
    dec = out_a[:, :512]
    swap = [(i, i ^ 1) for i in range(X * Z * YL)]
    dec_other = lax.ppermute(jnp.where(yl == 0, dec[72:], dec[:72]), "yz", swap)
    pre_other = lax.ppermute(jnp.where(yl == 0, pre[:, 256:], pre[:, :256]), "yz", swap)
    dec = jnp.where(yl == 0, dec[:72], dec[72:]) + dec_other
    pre = jnp.where(yl == 0, pre[:, :256], pre[:, 256:]) + pre_other
    decode_out = dec.reshape(72, GX, 2, 64).transpose(2, 1, 3, 0).reshape(2, 256, 72)
    turn = []
    for g in range(GX):
        for i in range(X * Z * YL):
            turn.append((g * 64 + i, (i // 16) * 64 + g * 16 + i % 16))
    pre = lax.ppermute(pre.astype(BF16), ("gx", "yz"), turn)
    prefill_out = pre.reshape(BLK, 2, PLEN).transpose(2, 1, 0).reshape(PLEN, 2 * BLK)
    return (prefill_out, decode_out.astype(BF16))


def solution(mesh):
    in_specs = (
        P("gx", None),
        P("gx"),
        P(None, None, ("gx", "yz")),
        P(("gx", "yz")),
        P(("gx", "yz"), None, None),
        P("gx", "yz"),
        P("gx", "yz"),
        P("yz", "gx"),
    )
    out_specs = (P("gx", "yz"), P(None, None, ("gx", "yz")))
    return jax.shard_map(body, mesh=mesh, in_specs=in_specs, out_specs=out_specs, check_vma=False)
```

```python
import heapq

import jax
import jax.numpy as jnp
from jax import lax
from jax.experimental import pallas as pl
from jax.experimental.pallas import tpu as pltpu
from jax.sharding import PartitionSpec as P

HEADS = 48
HD = 256
PLEN = 128
GX, X, Z, YL = 4, 4, 8, 2
BLK = 144
TOK = 512
WIDTH = {"pa": 256, "pb": 256, "da": 384, "db": 128}
START = {"pa": 0, "pb": 256, "da": 0, "db": 384}
KINDS = tuple(WIDTH)
COLS = 192
KVC = 8
ROWS1 = 208
MESH = pl.DeviceIdType.MESH
F32 = jnp.float32
BF16 = jnp.bfloat16
FULL, UPPER, LOWER = (0, 144), (0, 80), (80, 64)
OPPOSITE = {"x+": "x-", "x-": "x+", "z+": "z-", "z-": "z+"}


def steps_from(key):
    kind, xo, zo = key
    out = []
    if kind[1] == "a":
        if xo == 0:
            if -3 < zo <= 0:
                out.append(("z+", FULL, (kind, 0, zo - 1)))
            if zo == -3:
                out.append(("z+", UPPER, (kind, 0, 4)))
            if 0 <= zo < 3:
                out.append(("z-", FULL, (kind, 0, zo + 1)))
            if zo == 3:
                out.append(("z-", LOWER, (kind, 0, 4)))
            out.append(("x+", FULL, (kind, -1, zo)))
            out.append(("x-", FULL, (kind, 1, zo)))
        elif xo == -1 and zo % 2 == 0:
            out.append(("x+", FULL, (kind, 2, zo)))
        elif xo == 1 and zo % 2 == 1:
            out.append(("x-", FULL, (kind, 2, zo)))
    else:
        if zo == 0:
            if xo == 0:
                out.append(("x+", FULL, (kind, -1, 0)))
                out.append(("x-", FULL, (kind, 1, 0)))
            elif xo == -1:
                out.append(("x+", UPPER, (kind, 2, 0)))
            elif xo == 1:
                out.append(("x-", LOWER, (kind, 2, 0)))
        if zo <= 0 and (zo > -3 or xo in (0, 2)):
            out.append(("z+", FULL, (kind, xo, zo - 1 if zo > -3 else 4)))
        if 0 <= zo <= 3 and (zo < 3 or xo in (-1, 1)):
            out.append(("z-", FULL, (kind, xo, zo + 1)))
    return out


class Plan:
    def __init__(self, kinds):
        free = dict.fromkeys(OPPOSITE, 0.0)
        events, self.order, self.times, self.pieces = [], [], {}, {}
        self.sends, self.fills, self.source, self.where = {}, {}, {}, {}
        self.slots = dict.fromkeys(kinds, 0)

        def leave(key, now):
            self.order.append(key)
            self.times[key] = now
            for n, (d, rows, there) in enumerate(steps_from(key)):
                free[d] = max(free[d], now) + WIDTH[key[0]] * rows[1] * 4e-5
                k = len(self.sends)
                self.sends[(key, n)] = k
                self.fills[(there, rows)] = k
                self.source[k] = (key, n)
                self.where[(key, n)] = self.slots[key[0]]
                self.slots[key[0]] += 1
                heapq.heappush(events, (free[d] + 1.0, k, there, (d, rows)))

        for kind in kinds:
            leave((kind, 0, 0), 0.0)
        while events:
            now, _, key, piece = heapq.heappop(events)
            self.pieces.setdefault(key, []).append(piece)
            if sum(p[1][1] for p in self.pieces[key]) == BLK:
                leave(key, now)
        assert len(self.order) == X * Z * len(kinds)
        self.end = max(self.times.values())


IN = Plan(("pb", "pa", "db", "da"))
OUT = Plan(("db", "da", "pb", "pa"))
NSEND = len(IN.sends)


def place():
    gx = lax.axis_index("gx")
    yz = lax.axis_index("yz")
    return gx, yz // (Z * YL), (yz // YL) % Z, yz % YL


def flat(x, z, yl):
    return x * (Z * YL) + z * YL + yl


def copy_rows(move):
    def four(g, carry):
        for j in range(4):
            move(g // 4, (g % 4) * 2 + j // 2, j % 2, g, j)
        return carry

    lax.fori_loop(0, 16, four, 0)


def kernel(
    info, xpa, xpb, xda, xdb, wq, wkv, wt, cache,
    opa, opb, oda, odb,
    gpa, gpb, gda, gdb, w, accp, accd, takep, taked, tok, s1, r1, r2, qj, qh,
    kvown, k1, k2, att, heads, dec, ppa, ppb, pda, pdb, lpa, lpb, lda, ldb,
    send, recv, gsend, grecv, asend, arecv, ksend, krecv, hsend, hrecv, osend, orecv,
):
    gx, x, z, yl = place()
    yz = lax.axis_index("yz")
    own = dict(zip(KINDS, (xpa, xpb, xda, xdb)))
    got = dict(zip(KINDS, (gpa, gpb, gda, gdb)))
    result = dict(zip(KINDS, (opa, opb, oda, odb)))
    held = dict(zip(KINDS, (ppa, ppb, pda, pdb)))
    landing = dict(zip(KINDS, (lpa, lpb, lda, ldb)))
    acc = {"p": accp, "d": accd}
    take = {"p": takep, "d": taked}
    pending = []

    def near(d):
        dx = {"x+": 1, "x-": X - 1}.get(d, 0)
        dz = {"z+": 1, "z-": Z - 1}.get(d, 0)
        return (gx, flat((x + dx) % X, (z + dz) % Z, yl))

    z_peers = [(gx, flat(x, (z + s) % Z, yl)) for s in range(1, Z)]
    xy_peers = [(gx, flat((x + e // 2) % X, z, (yl + e) % YL)) for e in range(1, X * YL)]
    g_peers = [((gx + s) % GX, yz) for s in range(1, GX)]

    def remote(src, dst, ssem, rsem, device):
        return pltpu.make_async_remote_copy(
            src_ref=src, dst_ref=dst, send_sem=ssem, recv_sem=rsem, device_id=device, device_id_type=MESH
        )

    def start(src, dst, ssem, rsem, device):
        c = remote(src, dst, ssem, rsem, device)
        c.start()
        pending.append(c)

    def arrive(dst, ssem, rsem):
        remote(dst, dst, ssem, rsem, near("x+")).wait_recv()

    barrier = pltpu.get_barrier_semaphore()
    peers = z_peers + xy_peers + g_peers
    for peer in peers:
        pl.semaphore_signal(barrier, inc=1, device_id=peer, device_id_type=MESH)
    pl.semaphore_wait(barrier, len(peers))

    tok[...] = jnp.zeros(tok.shape, F32)
    qj[...] = jnp.zeros(qj.shape, F32)

    def slot(key, rows):
        kind, xo, zo = key
        first = pl.multiple_of(((z + zo) % Z) * BLK + rows[0], 16)
        return got[kind].at[(x + xo) % X, pl.ds(first, rows[1])]

    seen = {}

    def multiply(kind, xo):
        xx = (x + xo) % X
        part = lax.dot_general(
            w[pl.ds(pl.multiple_of(xx * (Z * BLK), 128), Z * BLK), :],
            got[kind][xx],
            (((0,), (0,)), ((), ())),
            preferred_element_type=F32,
        )
        lanes = slice(START[kind], START[kind] + WIDTH[kind])
        if kind in seen:
            acc[kind[0]][:, lanes] += part
        else:
            acc[kind[0]][:, lanes] = part
            seen[kind] = True

    def gather_node(key):
        kind, xo, zo = key
        mine = (xo, zo) == (0, 0)
        if not mine:
            for _, rows in IN.pieces[key]:
                k = IN.fills[(key, rows)]
                arrive(slot(key, rows), send.at[k], recv.at[k])
        for n, (d, rows, there) in enumerate(steps_from(key)):
            k = IN.sends[(key, n)]
            start(
                own[kind] if mine else slot(key, rows),
                slot(key, rows),
                send.at[k],
                recv.at[k],
                near(d),
            )
        if mine:
            first = pl.multiple_of(z * BLK, 16)
            got[kind][x, pl.ds(first, BLK), :] = own[kind][...]
        seen[(kind, xo)] = seen.get((kind, xo), 0) + 1
        if seen[(kind, xo)] == Z:
            multiply(kind, xo)

    def sum_start(f):
        for s in range(1, GX):
            to = (gx + s) % GX
            lane = pl.multiple_of(to * 128, 128)
            start(
                acc[f].at[pl.ds(0, ROWS1), pl.ds(lane, 128)],
                take[f].at[s - 1],
                gsend.at[n_of[f], s],
                grecv.at[n_of[f], s],
                g_peers[s - 1],
            )

    n_of = {"p": 0, "d": 1}

    def exchange_z(i):
        for s in range(1, Z):
            start(
                s1.at[i, :, (z + s) % Z],
                r1.at[i, :, z],
                asend.at[i, s],
                arecv.at[i, s],
                z_peers[s - 1],
            )
        r1[i, :, z] = s1[i, :, z]

    def exchange_xy(i):
        for s in range(1, Z):
            arrive(r1.at[i, :, (z + Z - s) % Z], asend.at[i, s], arecv.at[i, s])
        for e in range(1, X * YL):
            start(
                r1.at[i, (x + e // 2) % X, :, (yl + e) % YL],
                r2.at[i, x, :, yl],
                asend.at[i, Z + e],
                arecv.at[i, Z + e],
                xy_peers[e - 1],
            )
        r2[i, x, :, yl] = r1[i, x, :, yl]

    def exchange_end(i):
        for e in range(1, X * YL):
            arrive(
                r2.at[i, (x + X - e // 2) % X, :, (yl + e) % YL], asend.at[i, Z + e], arecv.at[i, Z + e]
            )

    def token(f, xx, zz, yy, t):
        r = flat(xx, zz, yy)
        return 2 * r + t if f == "p" else t * 64 + r

    def queries_start(f):
        for s in range(1, GX):
            arrive(take[f].at[s - 1], gsend.at[n_of[f], s], grecv.at[n_of[f], s])
        lane = pl.multiple_of(gx * 128, 128)
        total = acc[f][:ROWS1, pl.ds(lane, 128)]
        for s in range(1, GX):
            total = total + take[f][s - 1]
        total = total.astype(BF16).astype(F32)
        tok[:, :ROWS1] = total.T
        i = 2 * n_of[f]

        def pack(xx, zz, yy, g, j):
            for t in range(2):
                s1[i, xx, zz, yy, pl.ds(t, 1), :] = tok[pl.ds(token(f, xx, zz, yy, t), 1), :]

        copy_rows(pack)
        exchange_z(i)
        if f == "p":
            kvown[...] = total[COLS : COLS + KVC]
            for s in range(1, Z):
                start(kvown, k1.at[z], ksend.at[s], krecv.at[s], z_peers[s - 1])
            k1[z] = kvown[...]

    def queries_pass(f):
        exchange_xy(2 * n_of[f])
        if f == "p":
            for s in range(1, Z):
                arrive(k1.at[(z + Z - s) % Z], ksend.at[s], krecv.at[s])
            for e in range(1, X * YL):
                start(k1, k2.at[x, :, yl], ksend.at[Z + e], krecv.at[Z + e], xy_peers[e - 1])
            k2[x, :, yl] = k1[...]

    nt = (((1,), (1,)), ((), ()))
    scale = HD ** (-0.5)

    def attend(f):
        i = 2 * n_of[f]
        exchange_end(i)

        def unpack(xx, zz, yy, g, j):
            for t in range(2):
                qj[j, pl.ds(t * 16 + g, 1), :] = r2[i, xx, zz, yy, pl.ds(t, 1), :]

        copy_rows(unpack)
        qh[0:32, :192] = qj[0, :, :192]
        qh[0:32, 192:] = qj[1, :, :64]
        qh[32:64, :128] = qj[1, :, 64:192]
        qh[32:64, 128:] = qj[2, :, :128]
        qh[64:96, :64] = qj[2, :, 128:192]
        qh[64:96, 64:] = qj[3, :, :192]
        q32 = qh[...]
        q = q32.astype(BF16)
        if f == "p":
            for e in range(1, X * YL):
                arrive(k2.at[(x + X - e // 2) % X, :, (yl + e) % YL], ksend.at[Z + e], krecv.at[Z + e])
            kvt = k2[...].reshape(2 * HD, PLEN).astype(BF16)
            s = jnp.dot(q, kvt[:HD], preferred_element_type=F32) * scale
            query = 2 * yz + (lax.broadcasted_iota(jnp.int32, s.shape, 0) // 16) % 2
            pos = lax.broadcasted_iota(jnp.int32, s.shape, 1)
            s = jnp.where((pos <= query) & (pos < info[1]), s, -1e30)
            e = jnp.exp(s - jnp.max(s, axis=1, keepdims=True))
            probs = (e / jnp.sum(e, axis=1, keepdims=True)).astype(BF16)
            out = lax.dot_general(probs, kvt[HD:], nt, preferred_element_type=F32)
        else:
            row = lax.broadcasted_iota(jnp.int32, (KVC, 2 * HD), 0)
            lane = lax.broadcasted_iota(jnp.int32, (KVC, 2 * HD), 1)
            spread = (lane % KVC == row).astype(BF16)
            group = lax.broadcasted_iota(jnp.int32, (32, 2 * HD), 0) % 16
            holder = lax.broadcasted_iota(jnp.int32, (32, 2 * HD), 1) // KVC
            new = jnp.zeros((32, 2 * HD), F32)
            for j in range(4):
                wide = jnp.dot(
                    qj[j, :, COLS : COLS + KVC].astype(BF16), spread, preferred_element_type=F32
                )
                new = new + jnp.where(holder == 4 * group + j, wide, 0.0)
            new0 = jnp.sum(new[:16], axis=0, keepdims=True)
            new1 = jnp.sum(new[16:], axis=0, keepdims=True)
            s = lax.dot_general(q, cache[:, :HD], nt, preferred_element_type=F32) * scale
            pos = lax.broadcasted_iota(jnp.int32, s.shape, 1)
            s = jnp.where(pos < info[0], s, -1e30)
            f0 = jnp.sum(q32 * new0[:, :HD], axis=1, keepdims=True) * scale
            f1 = jnp.sum(q32 * new1[:, :HD], axis=1, keepdims=True) * scale
            step = (lax.broadcasted_iota(jnp.int32, f1.shape, 0) // 16) % 2
            f1 = jnp.where(step == 1, f1, -1e30)
            peak = jnp.maximum(jnp.max(s, axis=1, keepdims=True), jnp.maximum(f0, f1))
            es, e0, e1 = jnp.exp(s - peak), jnp.exp(f0 - peak), jnp.exp(f1 - peak)
            total = jnp.sum(es, axis=1, keepdims=True) + e0 + e1
            out = jnp.dot((es / total).astype(BF16), cache[:, HD:], preferred_element_type=F32)
            out = out + (e0 / total).astype(BF16).astype(F32) * new0[:, HD:]
            out = out + (e1 / total).astype(BF16).astype(F32) * new1[:, HD:]
        qh[...] = out.astype(BF16).astype(F32)
        qj[0, :, :192] = qh[0:32, :192]
        qj[1, :, :64] = qh[0:32, 192:]
        qj[1, :, 64:192] = qh[32:64, :128]
        qj[2, :, :128] = qh[32:64, 128:]
        qj[2, :, 128:192] = qh[64:96, :64]
        qj[3, :, :192] = qh[64:96, 64:]

        def pack(xx, zz, yy, g, j):
            for t in range(2):
                s1[i + 1, xx, zz, yy, pl.ds(t, 1), :] = qj[j, pl.ds(t * 16 + g, 1), :]

        copy_rows(pack)
        exchange_z(i + 1)

    def attended_pass(f):
        exchange_xy(2 * n_of[f] + 1)

    def attended_share(f):
        n = n_of[f]
        i = 2 * n + 1
        exchange_end(i)

        def unpack(xx, zz, yy, g, j):
            for t in range(2):
                tok[pl.ds(token(f, xx, zz, yy, t), 1), :] = r2[i, xx, zz, yy, pl.ds(t, 1), :]

        copy_rows(unpack)
        att[n] = tok[...].T[:COLS].astype(BF16)
        for s in range(1, GX):
            start(att.at[n], heads.at[n, s], hsend.at[n, s], hrecv.at[n, s], g_peers[s - 1])
        heads[n, 0] = att[n]

    def attended_end(f):
        n = n_of[f]
        for s in range(1, GX):
            arrive(heads.at[n, s], hsend.at[n, s], hrecv.at[n, s])
        if f == "d":
            for s in range(GX):
                lane = pl.multiple_of(((gx - s + GX) % GX) * 128, 128)
                dec[:, pl.ds(lane, 128)] = heads[n, s]

    def terms(key):
        kind, xo, zo = key
        xx, zz = (x + xo) % X, (z + zo) % Z
        if kind[0] == "d":
            first = pl.multiple_of((xx * Z + zz) * BLK, 16)
            lanes = slice(START[kind], START[kind] + WIDTH[kind])
            return jnp.dot(wt[pl.ds(first, BLK), :], dec[:, lanes], preferred_element_type=F32)
        group = heads[0, (gx - xx + GX) % GX]
        parts = []
        for q in range(START[kind] // 128, (START[kind] + WIDTH[kind]) // 128):
            first = pl.multiple_of(zz * (4 * BLK) + q * BLK, 16)
            parts.append(jnp.dot(wt[pl.ds(first, BLK), :], group, preferred_element_type=F32))
        return jnp.concatenate(parts, axis=1)

    def scatter_node(key):
        kind, xo, zo = key
        last = (xo, zo) == (0, 0)
        at = ((x + xo) % X) * Z + (z + zo) % Z
        local = terms(key)
        steps = steps_from(key)
        for n, (d, rows, there) in enumerate(steps):
            k = OUT.sends[(key, n)]
            spot = landing[kind].at[OUT.where[(key, n)], pl.ds(rows[0], rows[1])]
            arrive(spot, osend.at[k], orecv.at[k])
        halves = [local[:80], local[80:]]
        for n, (d, rows, there) in enumerate(steps):
            for i, (r0, rn) in enumerate((UPPER, LOWER)):
                if rows[0] <= r0 and r0 + rn <= rows[0] + rows[1]:
                    halves[i] = halves[i] + landing[kind][OUT.where[(key, n)], r0 : r0 + rn].astype(F32)
        for i, (r0, rn) in enumerate((UPPER, LOWER)):
            if last:
                result[kind][r0 : r0 + rn] = halves[i]
            else:
                held[kind][at, r0 : r0 + rn] = halves[i].astype(BF16)
        if not last:
            for d, rows in OUT.pieces[key]:
                k = OUT.fills[(key, rows)]
                start(
                    held[kind].at[at, pl.ds(rows[0], rows[1])],
                    landing[kind].at[OUT.where[OUT.source[k]], pl.ds(rows[0], rows[1])],
                    osend.at[k],
                    orecv.at[k],
                    near(OPPOSITE[d]),
                )

    middle = [sum_start, queries_start, queries_pass, attend, attended_pass, attended_share]

    prefill_done = max(IN.times[key] for key in IN.order if key[0][0] == "p")
    todo = [(prefill_done + 4.0 * n, step) for n, step in enumerate(middle)]
    for key in IN.order:
        while todo and IN.times[key] > todo[0][0]:
            todo.pop(0)[1]("p")
        gather_node(key)
        if key == ("da", 0, 0):
            w[:, :COLS] = wq[...]
            w[:, COLS:] = jnp.zeros((wq.shape[0], 256 - COLS), BF16)
            w[:, COLS : COLS + KVC] = wkv[...]
    sum_start("d")
    for _, step in todo:
        step("p")
    attended_end("p")

    todo = [(4.0 * n, step) for n, step in enumerate(middle)][1:]
    todo.append((24.0, attended_end))
    for key in reversed(OUT.order):
        while todo and (OUT.end - OUT.times[key] > todo[0][0] or key[0][0] == "d"):
            todo.pop(0)[1]("d")
        scatter_node(key)
    for c in pending:
        c.wait_send()


def run(info, xpa, xpb, xda, xdb, wq, wkv, wt, cache):
    vmem = pl.BlockSpec(memory_space=pltpu.VMEM)
    dma = pltpu.SemaphoreType.DMA
    return pl.pallas_call(
        kernel,
        out_shape=tuple(jax.ShapeDtypeStruct((BLK, WIDTH[k]), F32) for k in KINDS),
        in_specs=[pl.BlockSpec(memory_space=pltpu.SMEM)] + [vmem] * 8,
        out_specs=(vmem,) * 4,
        scratch_shapes=[pltpu.VMEM((X, Z * BLK, WIDTH[k]), BF16) for k in KINDS]
        + [
            pltpu.VMEM((wq.shape[0], 256), BF16),
            pltpu.VMEM((256, TOK), F32),
            pltpu.VMEM((256, TOK), F32),
            pltpu.VMEM((GX - 1, ROWS1, 128), F32),
            pltpu.VMEM((GX - 1, ROWS1, 128), F32),
            pltpu.VMEM((128, 256), F32),
            pltpu.VMEM((4, X, Z, YL, 2, 256), F32),
            pltpu.VMEM((4, X, Z, YL, 2, 256), F32),
            pltpu.VMEM((4, X, Z, YL, 2, 256), F32),
            pltpu.VMEM((4, 32, 256), F32),
            pltpu.VMEM((96, 256), F32),
            pltpu.VMEM((KVC, PLEN), F32),
            pltpu.VMEM((Z, KVC, PLEN), F32),
            pltpu.VMEM((X, Z, YL, KVC, PLEN), F32),
            pltpu.VMEM((2, COLS, 128), BF16),
            pltpu.VMEM((2, GX, COLS, 128), BF16),
            pltpu.VMEM((COLS, TOK), BF16),
        ]
        + [pltpu.VMEM((X * Z, BLK, WIDTH[k]), BF16) for k in KINDS]
        + [pltpu.VMEM((OUT.slots[k], BLK, WIDTH[k]), BF16) for k in KINDS]
        + [
            dma((NSEND,)),
            dma((NSEND,)),
            dma((2, GX)),
            dma((2, GX)),
            dma((4, 16)),
            dma((4, 16)),
            dma((16,)),
            dma((16,)),
            dma((2, GX)),
            dma((2, GX)),
            dma((NSEND,)),
            dma((NSEND,)),
        ],
        compiler_params=pltpu.CompilerParams(
            collective_id=0, has_side_effects=True, vmem_limit_bytes=58 * 2**20
        ),
        name="attention_block",
    )(info, xpa, xpb, xda, xdb, wq, wkv, wt, cache)


def body(
    prefill_tokens,
    prefill_lengths,
    decode_tokens,
    cache_lengths,
    cache_keyvals,
    query_weight,
    keyval_weight,
    out_weight,
):
    gx, x, z, yl = place()
    group = query_weight.shape[0]
    slices = [
        lax.dynamic_slice(prefill_tokens, (0, g * group + (x * Z + z) * BLK), (PLEN, BLK)).T
        for g in range(GX)
    ]
    pre = lax.all_to_all(jnp.stack(slices), "gx", split_axis=0, concat_axis=0, tiled=True)
    pre = pre.transpose(1, 0, 2).reshape(BLK, GX * PLEN)
    dec = decode_tokens.reshape(2, GX, 64, 72).transpose(3, 1, 0, 2).reshape(72, 512)
    other = lax.ppermute(dec, "yz", [(i, i ^ 1) for i in range(X * Z * YL)])
    dec = jnp.where(
        yl == 0, jnp.concatenate([dec, other], axis=0), jnp.concatenate([other, dec], axis=0)
    )
    split = WIDTH["pa"], WIDTH["da"]
    info = jnp.stack([cache_lengths[0], prefill_lengths[0]]).astype(jnp.int32)
    opa, opb, oda, odb = run(
        info,
        pre[:, : split[0]],
        pre[:, split[0] :],
        dec[:, : split[1]],
        dec[:, split[1] :],
        query_weight,
        keyval_weight,
        out_weight.T,
        cache_keyvals[0],
    )

    pre = jnp.concatenate([opa, opb], axis=1)
    dec = jnp.concatenate([oda, odb], axis=1)
    swap = [(i, i ^ 1) for i in range(X * Z * YL)]
    dec_other = lax.ppermute(jnp.where(yl == 0, dec[72:], dec[:72]), "yz", swap)
    pre_other = lax.ppermute(jnp.where(yl == 0, pre[:, 256:], pre[:, :256]), "yz", swap)
    dec = jnp.where(yl == 0, dec[:72], dec[72:]) + dec_other
    pre = jnp.where(yl == 0, pre[:, :256], pre[:, 256:]) + pre_other
    decode_out = dec.reshape(72, GX, 2, 64).transpose(2, 1, 3, 0).reshape(2, 256, 72)
    turn = []
    for g in range(GX):
        for i in range(X * Z * YL):
            turn.append((g * 64 + i, (i // 16) * 64 + g * 16 + i % 16))
    pre = lax.ppermute(pre.astype(BF16), ("gx", "yz"), turn)
    prefill_out = pre.reshape(BLK, 2, PLEN).transpose(2, 1, 0).reshape(PLEN, 2 * BLK)
    return (prefill_out, decode_out.astype(BF16))


def solution(mesh):
    in_specs = (
        P("gx", None),
        P("gx"),
        P(None, None, ("gx", "yz")),
        P(("gx", "yz")),
        P(("gx", "yz"), None, None),
        P("gx", "yz"),
        P("gx", "yz"),
        P("yz", "gx"),
    )
    out_specs = (P("gx", "yz"), P(None, None, ("gx", "yz")))
    return jax.shard_map(body, mesh=mesh, in_specs=in_specs, out_specs=out_specs, check_vma=False)
```

```python
import heapq

import jax
import jax.numpy as jnp
from jax import lax
from jax.experimental import pallas as pl
from jax.experimental.pallas import tpu as pltpu
from jax.sharding import PartitionSpec as P

HEADS = 48
HD = 256
PLEN = 128
GX, X, Z, YL = 4, 4, 8, 2
BLK = 144
TOK = 512
WIDTH_IN = {"pa": 128, "pb": 128, "da": 384, "db": 128}
WIDTH_OUT = {"pa": 256, "pb": 256, "da": 384, "db": 128}
START = {"pa": 0, "pb": 256, "da": 0, "db": 384}
KINDS = tuple(START)
COLS = 192
KVC = 8
ROWS1 = 208
MESH = pl.DeviceIdType.MESH
F32 = jnp.float32
BF16 = jnp.bfloat16
FULL, UPPER, LOWER = (0, 144), (0, 80), (80, 64)
OPPOSITE = {"x+": "x-", "x-": "x+", "z+": "z-", "z-": "z+"}


def steps_from(key):
    kind, xo, zo = key
    out = []
    if kind[1] == "a":
        if xo == 0:
            if -3 < zo <= 0:
                out.append(("z+", FULL, (kind, 0, zo - 1)))
            if zo == -3:
                out.append(("z+", UPPER, (kind, 0, 4)))
            if 0 <= zo < 3:
                out.append(("z-", FULL, (kind, 0, zo + 1)))
            if zo == 3:
                out.append(("z-", LOWER, (kind, 0, 4)))
            out.append(("x+", FULL, (kind, -1, zo)))
            out.append(("x-", FULL, (kind, 1, zo)))
        elif xo == -1 and zo % 2 == 0:
            out.append(("x+", FULL, (kind, 2, zo)))
        elif xo == 1 and zo % 2 == 1:
            out.append(("x-", FULL, (kind, 2, zo)))
    else:
        if zo == 0:
            if xo == 0:
                out.append(("x+", FULL, (kind, -1, 0)))
                out.append(("x-", FULL, (kind, 1, 0)))
            elif xo == -1:
                out.append(("x+", UPPER, (kind, 2, 0)))
            elif xo == 1:
                out.append(("x-", LOWER, (kind, 2, 0)))
        if zo <= 0 and (zo > -3 or xo in (0, 2)):
            out.append(("z+", FULL, (kind, xo, zo - 1 if zo > -3 else 4)))
        if 0 <= zo <= 3 and (zo < 3 or xo in (-1, 1)):
            out.append(("z-", FULL, (kind, xo, zo + 1)))
    return out


class Plan:
    def __init__(self, kinds, width, later):
        free = dict.fromkeys(OPPOSITE, 0.0)
        events, self.order, self.times, self.pieces = [], [], {}, {}
        self.sends, self.fills, self.source, self.where = {}, {}, {}, {}
        self.slots = dict.fromkeys(kinds, 0)

        def leave(key, now):
            self.order.append(key)
            self.times[key] = now
            for n, (d, rows, there) in enumerate(steps_from(key)):
                free[d] = max(free[d], now) + width[key[0]] * rows[1] * 4e-5
                k = len(self.sends)
                self.sends[(key, n)] = k
                self.fills[(there, rows)] = k
                self.source[k] = (key, n)
                self.where[(key, n)] = self.slots[key[0]]
                self.slots[key[0]] += 1
                heapq.heappush(events, (free[d] + 1.0, k, there, (d, rows)))

        for n, kind in enumerate(kinds):
            release = later if kind[0] != kinds[0][0] else 0.0
            heapq.heappush(events, (release, n - len(kinds), (kind, 0, 0), None))
        while events:
            now, _, key, piece = heapq.heappop(events)
            if piece is not None:
                self.pieces.setdefault(key, []).append(piece)
            if piece is None or sum(p[1][1] for p in self.pieces[key]) == BLK:
                leave(key, now)
        assert len(self.order) == X * Z * len(kinds)
        self.end = max(self.times.values())


IN = Plan(("pb", "pa", "db", "da"), WIDTH_IN, 12.0)
OUT = Plan(("db", "da", "pb", "pa"), WIDTH_OUT, 22.0)
NSEND = len(IN.sends)


def place():
    gx = lax.axis_index("gx")
    yz = lax.axis_index("yz")
    return gx, yz // (Z * YL), (yz // YL) % Z, yz % YL


def flat(x, z, yl):
    return x * (Z * YL) + z * YL + yl


def copy_rows(move):
    def four(g, carry):
        for j in range(4):
            move(g // 4, (g % 4) * 2 + j // 2, j % 2, g, j)
        return carry

    lax.fori_loop(0, 16, four, 0)


def kernel(
    info, dtok, wkv, ptok, wq, wo, cache_hbm,
    prefill_out, decode_out,
    gpa, gpb, gda, gdb, w, wov, wt, cache, tloc, win, winT, xpa, xpb, xda, xdb, dsend, drecv,
    accp, accd, takep, taked, tok, s1, r1, r2, qj, qh,
    kvown, k1, k2, att, heads, dec, dec2, ppa, ppb, pda, pdb, lpa, lpb, lda, ldb,
    opa, opb, oda, odb, psend, precv, dsend2, drecv2, pfin, pland,
    local, esend, erecv, send, recv, gsend, grecv, asend, arecv, ksend, krecv, hsend, hrecv,
    osend, orecv, fsend, frecv,
):
    gx, x, z, yl = place()
    yz = lax.axis_index("yz")
    core, y_hi = gx % 2, gx // 2
    own = dict(zip(KINDS, (xpa, xpb, xda, xdb)))
    got = dict(zip(KINDS, (gpa, gpb, gda, gdb)))
    result = dict(zip(KINDS, (opa, opb, oda, odb)))
    held = dict(zip(KINDS, (ppa, ppb, pda, pdb)))
    landing = dict(zip(KINDS, (lpa, lpb, lda, ldb)))
    acc = {"p": accp, "d": accd}
    take = {"p": takep, "d": taked}
    pending = []

    def near(d):
        dx = {"x+": 1, "x-": X - 1}.get(d, 0)
        dz = {"z+": 1, "z-": Z - 1}.get(d, 0)
        return (gx, flat((x + dx) % X, (z + dz) % Z, yl))

    z_peers = [(gx, flat(x, (z + s) % Z, yl)) for s in range(1, Z)]
    xy_peers = [(gx, flat((x + e // 2) % X, z, (yl + e) % YL)) for e in range(1, X * YL)]
    g_peers = [((gx + s) % GX, yz) for s in range(1, GX)]

    def remote(src, dst, ssem, rsem, device):
        return pltpu.make_async_remote_copy(
            src_ref=src, dst_ref=dst, send_sem=ssem, recv_sem=rsem, device_id=device, device_id_type=MESH
        )

    def start(src, dst, ssem, rsem, device):
        c = remote(src, dst, ssem, rsem, device)
        c.start()
        pending.append(c)

    def arrive(dst, ssem, rsem):
        remote(dst, dst, ssem, rsem, near("x+")).wait_recv()

    barrier = pltpu.get_barrier_semaphore()
    peers = z_peers + xy_peers + g_peers
    keeper = (x, flat(gx, z, yl))
    turned = x != gx
    for peer in peers:
        pl.semaphore_signal(barrier, inc=1, device_id=peer, device_id_type=MESH)

    @pl.when(turned)
    def _():
        pl.semaphore_signal(barrier, inc=1, device_id=keeper, device_id_type=MESH)

    group = wq.shape[1]
    edge = (x * Z + z) * BLK
    aligned = (edge // 128) * 128
    loads = []

    def load(src, dst):
        c = pltpu.make_async_copy(src, dst, local.at[len(loads)])
        c.start()
        loads.append(c)
        return c

    there = 1 - y_hi
    windows = []
    for c in range(2):
        lane = pl.multiple_of((2 * there + c) * group + aligned, 128)
        windows.append(load(ptok.at[:, pl.ds(lane, 256)], win.at[c]))
    w_load = load(wq, w.at[pl.ds(0, COLS)])
    mine_load = load(ptok.at[:, pl.ds(pl.multiple_of(gx * group, 128), group)], tloc.at[0])
    wo_load = load(wo, wov)
    cache_load = load(cache_hbm, cache)
    dsend[:72, :256] = dtok[0]
    dsend[:72, 256:] = dtok[1]
    dsend[72:, :] = jnp.zeros((8, TOK), BF16)
    tok[...] = jnp.zeros(tok.shape, F32)
    qj[...] = jnp.zeros(qj.shape, F32)
    for c in range(2):
        windows[c].wait()
        winT[c] = win[c].T
    pl.semaphore_wait(barrier, len(peers) + turned.astype(jnp.int32))

    partner = (gx, flat(x, z, 1 - yl))
    first = pl.multiple_of(edge - aligned, 16)
    landed = (xpa, xpb)
    for c in range(2):

        @pl.when(core == c)
        def _(c=c):
            for o in range(2):
                remote(
                    winT.at[o, pl.ds(first, BLK)],
                    landed[c],
                    esend.at[o],
                    erecv.at[c],
                    (2 * there + o, yz),
                ).start()

    start(dsend, drecv, esend.at[2], erecv.at[2], partner)
    lane = pl.multiple_of((gx + 1 - 2 * core) * group, 128)
    start(
        ptok.at[:, pl.ds(lane, group)], tloc.at[1], esend.at[3], erecv.at[3], (gx + 1 - 2 * core, yz)
    )

    def slot(key, rows):
        kind, xo, zo = key
        return got[kind].at[((x + xo) % X) * Z + (z + zo) % Z, pl.ds(rows[0], rows[1])]

    seen = {}

    def lanes_of(kind):
        if kind[0] == "p":
            return pl.ds(pl.multiple_of((2 * there + "ab".index(kind[1])) * 128, 128), 128)
        return slice(START[kind], START[kind] + WIDTH_IN[kind])

    def multiply(kind, xo):
        xx = (x + xo) % X
        part = jnp.dot(
            w[:, pl.ds(pl.multiple_of(xx * (Z * BLK), 128), Z * BLK)],
            got[kind][pl.ds(xx * Z, Z)].reshape(Z * BLK, WIDTH_IN[kind]),
            preferred_element_type=F32,
        )
        if kind in seen:
            acc[kind[0]][:, lanes_of(kind)] += part
        else:
            acc[kind[0]][:, lanes_of(kind)] = part
            seen[kind] = True

    def multiply_near(n):
        lanes = pl.ds(pl.multiple_of((gx if n == 0 else gx + 1 - 2 * core) * 128, 128), 128)
        acc["p"][:, lanes] = lax.dot_general(
            w[...], tloc[n], (((1,), (1,)), ((), ())), preferred_element_type=F32
        )

    def gather_node(key):
        kind, xo, zo = key
        mine = (xo, zo) == (0, 0)
        if not mine:
            for _, rows in IN.pieces[key]:
                k = IN.fills[(key, rows)]
                arrive(slot(key, rows), send.at[KINDS.index(kind)], recv.at[k])
        elif kind[0] == "p":
            c = "ab".index(kind[1])
            arrive(own[kind], esend.at[c], erecv.at[c])
        elif kind == "db":
            arrive(drecv, esend.at[2], erecv.at[2])
            one, two = dsend[:72].astype(F32), drecv[:72].astype(F32)
            both = jnp.where(
                yl == 0, jnp.concatenate([one, two], axis=0), jnp.concatenate([two, one], axis=0)
            ).astype(BF16)
            xda[...] = both[:, : WIDTH_IN["da"]]
            xdb[...] = both[:, WIDTH_IN["da"] :]
        for n, (d, rows, there) in enumerate(steps_from(key)):
            k = IN.sends[(key, n)]
            remote(
                own[kind] if mine else slot(key, rows),
                slot(key, rows),
                send.at[KINDS.index(kind)],
                recv.at[k],
                near(d),
            ).start()
        if mine:
            got[kind][x * Z + z] = own[kind][...]
        seen[(kind, xo)] = seen.get((kind, xo), 0) + 1
        if seen[(kind, xo)] == Z:
            multiply(kind, xo)

    def sum_start(f):
        if f == "d":
            rows = accd[...]
            for g in range(GX):
                accd[:, g * 128 : g * 128 + 64] = rows[:, g * 64 : g * 64 + 64]
                accd[:, g * 128 + 64 : g * 128 + 128] = rows[:, 256 + g * 64 : 320 + g * 64]
        for s in range(1, GX):
            to = (gx + s) % GX
            lane = pl.multiple_of(to * 128, 128)
            start(
                acc[f].at[pl.ds(0, ROWS1), pl.ds(lane, 128)],
                take[f].at[s - 1],
                gsend.at[n_of[f], s],
                grecv.at[n_of[f], s],
                g_peers[s - 1],
            )

    n_of = {"p": 0, "d": 1}

    def exchange_z(i):
        for s in range(1, Z):
            start(
                s1.at[i, :, (z + s) % Z],
                r1.at[i, :, z],
                asend.at[i, s],
                arecv.at[i, s],
                z_peers[s - 1],
            )
        r1[i, :, z] = s1[i, :, z]

    def exchange_xy(i):
        for s in range(1, Z):
            arrive(r1.at[i, :, (z + Z - s) % Z], asend.at[i, s], arecv.at[i, s])
        for e in range(1, X * YL):
            start(
                r1.at[i, (x + e // 2) % X, :, (yl + e) % YL],
                r2.at[i, x, :, yl],
                asend.at[i, Z + e],
                arecv.at[i, Z + e],
                xy_peers[e - 1],
            )
        r2[i, x, :, yl] = r1[i, x, :, yl]

    def exchange_end(i):
        for e in range(1, X * YL):
            arrive(
                r2.at[i, (x + X - e // 2) % X, :, (yl + e) % YL], asend.at[i, Z + e], arecv.at[i, Z + e]
            )

    def token(f, xx, zz, yy, t):
        r = flat(xx, zz, yy)
        return 2 * r + t if f == "p" else t * 64 + r

    def queries_start(f):
        for s in range(1, GX):
            arrive(take[f].at[s - 1], gsend.at[n_of[f], s], grecv.at[n_of[f], s])
        lane = pl.multiple_of(gx * 128, 128)
        total = acc[f][:ROWS1, pl.ds(lane, 128)]
        for s in range(1, GX):
            total = total + take[f][s - 1]
        total = total.astype(BF16).astype(F32)
        tok[:, :ROWS1] = total.T
        i = 2 * n_of[f]

        def pack(xx, zz, yy, g, j):
            for t in range(2):
                s1[i, xx, zz, yy, pl.ds(t, 1), :] = tok[pl.ds(token(f, xx, zz, yy, t), 1), :]

        copy_rows(pack)
        exchange_z(i)
        if f == "p":
            kvown[...] = total[COLS : COLS + KVC]
            for s in range(1, Z):
                start(kvown, k1.at[z], ksend.at[s], krecv.at[s], z_peers[s - 1])
            k1[z] = kvown[...]

    def queries_pass(f):
        exchange_xy(2 * n_of[f])
        if f == "p":
            for s in range(1, Z):
                arrive(k1.at[(z + Z - s) % Z], ksend.at[s], krecv.at[s])
            for e in range(1, X * YL):
                start(k1, k2.at[x, :, yl], ksend.at[Z + e], krecv.at[Z + e], xy_peers[e - 1])
            k2[x, :, yl] = k1[...]

    nt = (((1,), (1,)), ((), ()))
    scale = HD ** (-0.5)

    def attend(f):
        i = 2 * n_of[f]
        exchange_end(i)

        def unpack(xx, zz, yy, g, j):
            for t in range(2):
                qj[j, pl.ds(t * 16 + g, 1), :] = r2[i, xx, zz, yy, pl.ds(t, 1), :]

        copy_rows(unpack)
        qh[0:32, :192] = qj[0, :, :192]
        qh[0:32, 192:] = qj[1, :, :64]
        qh[32:64, :128] = qj[1, :, 64:192]
        qh[32:64, 128:] = qj[2, :, :128]
        qh[64:96, :64] = qj[2, :, 128:192]
        qh[64:96, 64:] = qj[3, :, :192]
        q32 = qh[...]
        q = q32.astype(BF16)
        if f == "p":
            for e in range(1, X * YL):
                arrive(k2.at[(x + X - e // 2) % X, :, (yl + e) % YL], ksend.at[Z + e], krecv.at[Z + e])
            kvt = k2[...].reshape(2 * HD, PLEN).astype(BF16)
            s = jnp.dot(q, kvt[:HD], preferred_element_type=F32) * scale
            query = 2 * yz + (lax.broadcasted_iota(jnp.int32, s.shape, 0) // 16) % 2
            pos = lax.broadcasted_iota(jnp.int32, s.shape, 1)
            s = jnp.where((pos <= query) & (pos < info[1]), s, -1e30)
            e = jnp.exp(s - jnp.max(s, axis=1, keepdims=True))
            probs = (e / jnp.sum(e, axis=1, keepdims=True)).astype(BF16)
            out = lax.dot_general(probs, kvt[HD:], nt, preferred_element_type=F32)
        else:
            row = lax.broadcasted_iota(jnp.int32, (KVC, 2 * HD), 0)
            lane = lax.broadcasted_iota(jnp.int32, (KVC, 2 * HD), 1)
            spread = (lane % KVC == row).astype(BF16)
            group = lax.broadcasted_iota(jnp.int32, (32, 2 * HD), 0) % 16
            holder = lax.broadcasted_iota(jnp.int32, (32, 2 * HD), 1) // KVC
            new = jnp.zeros((32, 2 * HD), F32)
            for j in range(4):
                wide = jnp.dot(
                    qj[j, :, COLS : COLS + KVC].astype(BF16), spread, preferred_element_type=F32
                )
                new = new + jnp.where(holder == 4 * group + j, wide, 0.0)
            new0 = jnp.sum(new[:16], axis=0, keepdims=True)
            new1 = jnp.sum(new[16:], axis=0, keepdims=True)
            s = lax.dot_general(q, cache[:, :HD], nt, preferred_element_type=F32) * scale
            pos = lax.broadcasted_iota(jnp.int32, s.shape, 1)
            s = jnp.where(pos < info[0], s, -1e30)
            f0 = jnp.sum(q32 * new0[:, :HD], axis=1, keepdims=True) * scale
            f1 = jnp.sum(q32 * new1[:, :HD], axis=1, keepdims=True) * scale
            step = (lax.broadcasted_iota(jnp.int32, f1.shape, 0) // 16) % 2
            f1 = jnp.where(step == 1, f1, -1e30)
            peak = jnp.maximum(jnp.max(s, axis=1, keepdims=True), jnp.maximum(f0, f1))
            es, e0, e1 = jnp.exp(s - peak), jnp.exp(f0 - peak), jnp.exp(f1 - peak)
            total = jnp.sum(es, axis=1, keepdims=True) + e0 + e1
            out = jnp.dot((es / total).astype(BF16), cache[:, HD:], preferred_element_type=F32)
            out = out + (e0 / total).astype(BF16).astype(F32) * new0[:, HD:]
            out = out + (e1 / total).astype(BF16).astype(F32) * new1[:, HD:]
        qh[...] = out.astype(BF16).astype(F32)
        qj[0, :, :192] = qh[0:32, :192]
        qj[1, :, :64] = qh[0:32, 192:]
        qj[1, :, 64:192] = qh[32:64, :128]
        qj[2, :, :128] = qh[32:64, 128:]
        qj[2, :, 128:192] = qh[64:96, :64]
        qj[3, :, :192] = qh[64:96, 64:]

        def pack(xx, zz, yy, g, j):
            for t in range(2):
                s1[i + 1, xx, zz, yy, pl.ds(t, 1), :] = qj[j, pl.ds(t * 16 + g, 1), :]

        copy_rows(pack)
        exchange_z(i + 1)

    def attended_pass(f):
        exchange_xy(2 * n_of[f] + 1)

    def attended_share(f):
        n = n_of[f]
        i = 2 * n + 1
        exchange_end(i)

        def unpack(xx, zz, yy, g, j):
            for t in range(2):
                tok[pl.ds(token(f, xx, zz, yy, t), 1), :] = r2[i, xx, zz, yy, pl.ds(t, 1), :]

        copy_rows(unpack)
        att[n] = tok[...].T[:COLS].astype(BF16)
        for s in range(1, GX):
            start(att.at[n], heads.at[n, s], hsend.at[n, s], hrecv.at[n, s], g_peers[s - 1])
        heads[n, 0] = att[n]

    def attended_end(f):
        n = n_of[f]
        for s in range(1, GX):
            arrive(heads.at[n, s], hsend.at[n, s], hrecv.at[n, s])
        if f == "d":
            for s in range(GX):
                lane = pl.multiple_of(((gx - s + GX) % GX) * 128, 128)
                dec2[:, pl.ds(lane, 128)] = heads[n, s]
            for g in range(GX):
                for t in range(2):
                    dec[:, t * 256 + g * 64 : t * 256 + g * 64 + 64] = dec2[
                        :, g * 128 + t * 64 : g * 128 + t * 64 + 64
                    ]

    def terms(key):
        kind, xo, zo = key
        xx, zz = (x + xo) % X, (z + zo) % Z
        if kind[0] == "d":
            first = pl.multiple_of((xx * Z + zz) * BLK, 16)
            lanes = slice(START[kind], START[kind] + WIDTH_OUT[kind])
            return jnp.dot(wt[pl.ds(first, BLK), :], dec[:, lanes], preferred_element_type=F32)
        group = heads[0, (gx - xx + GX) % GX]
        parts = []
        for q in range(START[kind] // 128, (START[kind] + WIDTH_OUT[kind]) // 128):
            first = pl.multiple_of(zz * (4 * BLK) + q * BLK, 16)
            parts.append(jnp.dot(wt[pl.ds(first, BLK), :], group, preferred_element_type=F32))
        return jnp.concatenate(parts, axis=1)

    def scatter_node(key):
        kind, xo, zo = key
        last = (xo, zo) == (0, 0)
        at = ((x + xo) % X) * Z + (z + zo) % Z
        local = terms(key)
        steps = steps_from(key)
        for n, (d, rows, there) in enumerate(steps):
            k = OUT.sends[(key, n)]
            spot = landing[kind].at[OUT.where[(key, n)], pl.ds(rows[0], rows[1])]
            arrive(spot, osend.at[KINDS.index(kind)], orecv.at[k])
        halves = [local[:80], local[80:]]
        for n, (d, rows, there) in enumerate(steps):
            for i, (r0, rn) in enumerate((UPPER, LOWER)):
                if rows[0] <= r0 and r0 + rn <= rows[0] + rows[1]:
                    halves[i] = halves[i] + landing[kind][OUT.where[(key, n)], r0 : r0 + rn].astype(F32)
        for i, (r0, rn) in enumerate((UPPER, LOWER)):
            if last:
                result[kind][r0 : r0 + rn] = halves[i]
            else:
                held[kind][at, r0 : r0 + rn] = halves[i].astype(BF16)
        if not last:
            for d, rows in OUT.pieces[key]:
                k = OUT.fills[(key, rows)]
                remote(
                    held[kind].at[at, pl.ds(rows[0], rows[1])],
                    landing[kind].at[OUT.where[OUT.source[k]], pl.ds(rows[0], rows[1])],
                    osend.at[KINDS.index(kind)],
                    orecv.at[k],
                    near(OPPOSITE[d]),
                ).start()

    middle = [sum_start, queries_start, queries_pass, attend, attended_pass, attended_share]

    def weights():
        w_load.wait()
        w[COLS:, :] = jnp.concatenate([wkv[...].astype(F32), jnp.zeros((8, group), F32)]).astype(BF16)
        mine_load.wait()
        multiply_near(0)
        wo_load.wait()
        for n in range(group // 512):
            wt[pl.ds(512 * n, 512), :] = wov[:, 512 * n : 512 * n + 512].T

    def sibling():
        arrive(tloc.at[1], esend.at[3], erecv.at[3])
        multiply_near(1)

    prefill_done = max(IN.times[key] for key in IN.order if key[0][0] == "p")
    todo = [(prefill_done + 3.0 * n, step) for n, step in enumerate(middle)]
    for n, key in enumerate(IN.order):
        while todo and IN.times[key] > todo[0][0]:
            todo.pop(0)[1]("p")
        gather_node(key)
        if n == 1:
            weights()
        if n == 12:
            sibling()
    sum_start("d")
    for _, step in todo:
        step("p")
    attended_end("p")

    cache_load.wait()
    todo = [(3.0 * n, step) for n, step in enumerate(middle)][1:]
    todo.append((18.0, attended_end))
    for key in reversed(OUT.order):
        while todo and (OUT.end - OUT.times[key] > todo[0][0] or key[0][0] == "d"):
            todo.pop(0)[1]("d")
        scatter_node(key)

    dec_sum = jnp.concatenate([oda[...], odb[...]], axis=1)
    dsend2[:72] = jnp.where(yl == 0, dec_sum[72:], dec_sum[:72]).astype(BF16)
    dsend2[72:] = jnp.zeros((8, TOK), BF16)
    psend[...] = jnp.where(yl == 0, opb[...], opa[...]).astype(BF16)
    start(psend, precv, fsend.at[0], frecv.at[0], partner)
    start(dsend2, drecv2, fsend.at[1], frecv.at[1], partner)
    arrive(precv, fsend.at[0], frecv.at[0])
    pre_sum = jnp.where(yl == 0, opa[...], opb[...]) + precv[...].astype(F32)
    for q in range(2):
        pfin[q * BLK : q * BLK + BLK] = pre_sum[:, q * 128 : q * 128 + 128].astype(BF16)

    @pl.when(turned)
    def _():
        remote(pfin, pland, fsend.at[2], frecv.at[2], keeper).start()

    arrive(drecv2, fsend.at[1], frecv.at[1])
    dec_sum = jnp.where(yl == 0, dec_sum[:72], dec_sum[72:]) + drecv2[:72].astype(F32)
    for t in range(2):
        decode_out[t] = dec_sum[:, t * 256 : t * 256 + 256].astype(BF16)

    @pl.when(turned)
    def _():
        remote(pfin, pland, fsend.at[2], frecv.at[2], keeper).wait()
        prefill_out[...] = pland[...]

    @pl.when(x == gx)
    def _():
        prefill_out[...] = pfin[...]

    for n, kind in enumerate(KINDS):
        sent = got[kind].at[pl.ds(0, X * Z - 1)]
        remote(sent, sent, send.at[n], recv.at[0], partner).wait_send()
        sent = held[kind].at[pl.ds(0, X * Z - 1)]
        remote(sent, sent, osend.at[n], orecv.at[0], partner).wait_send()
    for o in range(2):
        sent = winT.at[o, pl.ds(first, BLK)]
        remote(sent, sent, esend.at[o], erecv.at[o], partner).wait_send()
    for c in pending:
        c.wait_send()


def run(info, dtok, wkv, ptok, wq, wo, cache):
    vmem = pl.BlockSpec(memory_space=pltpu.VMEM)
    hbm = pl.BlockSpec(memory_space=pl.ANY)
    dma = pltpu.SemaphoreType.DMA
    group = wq.shape[1]

    def scratch(*shape, dtype=BF16):
        return pltpu.VMEM(shape, dtype)

    return pl.pallas_call(
        kernel,
        out_shape=(
            jax.ShapeDtypeStruct((2 * BLK, PLEN), BF16),
            jax.ShapeDtypeStruct((2, 72, 256), BF16),
        ),
        in_specs=[pl.BlockSpec(memory_space=pltpu.SMEM), vmem, vmem, hbm, hbm, hbm, hbm],
        out_specs=(vmem, vmem),
        scratch_shapes=[scratch(X * Z, BLK, WIDTH_IN[k]) for k in KINDS]
        + [
            scratch(ROWS1, group),
            scratch(COLS, group),
            scratch(group, COLS),
            scratch(*cache.shape),
            scratch(2, PLEN, group),
            scratch(2, PLEN, 256),
            scratch(2, 256, PLEN),
        ]
        + [scratch(BLK, WIDTH_IN[k]) for k in KINDS]
        + [
            scratch(80, TOK),
            scratch(80, TOK),
            scratch(ROWS1, TOK, dtype=F32),
            scratch(ROWS1, TOK, dtype=F32),
            scratch(GX - 1, ROWS1, 128, dtype=F32),
            scratch(GX - 1, ROWS1, 128, dtype=F32),
            scratch(128, 256, dtype=F32),
            scratch(4, X, Z, YL, 2, 256, dtype=F32),
            scratch(4, X, Z, YL, 2, 256, dtype=F32),
            scratch(4, X, Z, YL, 2, 256, dtype=F32),
            scratch(4, 32, 256, dtype=F32),
            scratch(96, 256, dtype=F32),
            scratch(KVC, PLEN, dtype=F32),
            scratch(Z, KVC, PLEN, dtype=F32),
            scratch(X, Z, YL, KVC, PLEN, dtype=F32),
            scratch(2, COLS, 128),
            scratch(2, GX, COLS, 128),
            scratch(COLS, TOK),
            scratch(COLS, TOK),
        ]
        + [scratch(X * Z, BLK, WIDTH_OUT[k]) for k in KINDS]
        + [scratch(OUT.slots[k], BLK, WIDTH_OUT[k]) for k in KINDS]
        + [scratch(BLK, WIDTH_OUT[k], dtype=F32) for k in KINDS]
        + [
            scratch(BLK, 256),
            scratch(BLK, 256),
            scratch(80, TOK),
            scratch(80, TOK),
            scratch(2 * BLK, PLEN),
            scratch(2 * BLK, PLEN),
            dma((8,)),
            dma((4,)),
            dma((4,)),
            dma((4,)),
            dma((NSEND,)),
            dma((2, GX)),
            dma((2, GX)),
            dma((4, 16)),
            dma((4, 16)),
            dma((16,)),
            dma((16,)),
            dma((2, GX)),
            dma((2, GX)),
            dma((4,)),
            dma((NSEND,)),
            dma((4,)),
            dma((4,)),
        ],
        compiler_params=pltpu.CompilerParams(
            collective_id=0, has_side_effects=True, vmem_limit_bytes=60 * 2**20
        ),
        name="attention_block",
    )(info, dtok, wkv, ptok, wq, wo, cache)


def body(
    prefill_tokens,
    prefill_lengths,
    decode_tokens,
    cache_lengths,
    cache_keyvals,
    query_weight,
    keyval_weight,
    out_weight,
):
    info = jnp.stack([cache_lengths[0], prefill_lengths[0]]).astype(jnp.int32)
    prefill_out, decode_out = run(
        info,
        decode_tokens.transpose(0, 2, 1),
        keyval_weight.T,
        prefill_tokens,
        query_weight.T,
        out_weight,
        cache_keyvals[0],
    )
    return (prefill_out.T, decode_out.transpose(0, 2, 1))


def solution(mesh):
    in_specs = (
        P("gx", None),
        P("gx"),
        P(None, None, ("gx", "yz")),
        P(("gx", "yz")),
        P(("gx", "yz"), None, None),
        P("gx", "yz"),
        P("gx", "yz"),
        P("yz", "gx"),
    )
    out_specs = (P("gx", "yz"), P(None, None, ("gx", "yz")))
    return jax.shard_map(body, mesh=mesh, in_specs=in_specs, out_specs=out_specs, check_vma=False)
```

```python
import heapq

import jax
import jax.numpy as jnp
from jax import lax
from jax.experimental import pallas as pl
from jax.experimental.pallas import tpu as pltpu
from jax.sharding import PartitionSpec as P

HEADS = 48
HD = 256
PLEN = 128
GX, X, Z, YL = 4, 4, 8, 2
BLK = 144
TOK = 512
WIDTH_IN = {"p0": 1024, "p1": 1024, "da": 128, "db": 384}
WIDTH_OUT = {"pa": 256, "pb": 256, "da": 384, "db": 128}
START_IN = {"da": 0, "db": 128}
START = {"pa": 0, "pb": 256, "da": 0, "db": 384}
KINDS = tuple(START)
KINDS_IN = tuple(WIDTH_IN)
SPAN = Z * BLK
COLS = 192
KVC = 8
ROWS1 = 208
MESH = pl.DeviceIdType.MESH
F32 = jnp.float32
BF16 = jnp.bfloat16
FULL, UPPER, LOWER = (0, 144), (0, 80), (80, 64)
OPPOSITE = {"x+": "x-", "x-": "x+", "z+": "z-", "z-": "z+"}


def steps_from(key):
    kind, xo, zo = key
    out = []
    if kind in ("p0", "p1"):
        if xo == 0:
            out.append(("x+", FULL, (kind, -1, 0)))
            out.append(("x-", FULL, (kind, 1, 0)))
        elif kind == "p0" and xo == -1:
            out.append(("x+", FULL, (kind, 2, 0)))
        elif kind == "p1" and xo == 1:
            out.append(("x-", FULL, (kind, 2, 0)))
    elif kind[1] == "a":
        if xo == 0:
            if -3 < zo <= 0:
                out.append(("z+", FULL, (kind, 0, zo - 1)))
            if zo == -3:
                out.append(("z+", UPPER, (kind, 0, 4)))
            if 0 <= zo < 3:
                out.append(("z-", FULL, (kind, 0, zo + 1)))
            if zo == 3:
                out.append(("z-", LOWER, (kind, 0, 4)))
            out.append(("x+", FULL, (kind, -1, zo)))
            out.append(("x-", FULL, (kind, 1, zo)))
        elif xo == -1 and zo % 2 == 0:
            out.append(("x+", FULL, (kind, 2, zo)))
        elif xo == 1 and zo % 2 == 1:
            out.append(("x-", FULL, (kind, 2, zo)))
    else:
        if zo == 0:
            if xo == 0:
                out.append(("x+", FULL, (kind, -1, 0)))
                out.append(("x-", FULL, (kind, 1, 0)))
            elif xo == -1:
                out.append(("x+", UPPER, (kind, 2, 0)))
            elif xo == 1:
                out.append(("x-", LOWER, (kind, 2, 0)))
        if zo <= 0 and (zo > -3 or xo in (0, 2)):
            out.append(("z+", FULL, (kind, xo, zo - 1 if zo > -3 else 4)))
        if 0 <= zo <= 3 and (zo < 3 or xo in (-1, 1)):
            out.append(("z-", FULL, (kind, xo, zo + 1)))
    return out


class Plan:
    def __init__(self, releases, width):
        free = dict.fromkeys(OPPOSITE, 0.0)
        events, self.order, self.times, self.pieces = [], [], {}, {}
        self.sends, self.fills, self.source, self.where = {}, {}, {}, {}
        self.slots = dict.fromkeys(releases, 0)

        def leave(key, now):
            self.order.append(key)
            self.times[key] = now
            for n, (d, rows, there) in enumerate(steps_from(key)):
                free[d] = max(free[d], now) + width[key[0]] * rows[1] * 4e-5
                k = len(self.sends)
                self.sends[(key, n)] = k
                self.fills[(there, rows)] = k
                self.source[k] = (key, n)
                self.where[(key, n)] = self.slots[key[0]]
                self.slots[key[0]] += 1
                heapq.heappush(events, (free[d] + 3.0, k, there, (d, rows)))

        for n, kind in enumerate(releases):
            heapq.heappush(events, (releases[kind], n - len(releases), (kind, 0, 0), None))
        while events:
            now, _, key, piece = heapq.heappop(events)
            if piece is not None:
                self.pieces.setdefault(key, []).append(piece)
            if piece is None or sum(p[1][1] for p in self.pieces[key]) == BLK:
                leave(key, now)
        self.end = max(self.times.values())


IN = Plan({"db": 0.0, "da": 0.0, "p0": 6.0, "p1": 12.0}, WIDTH_IN)
OUT = Plan({"db": 0.0, "da": 0.0, "pb": 10.0, "pa": 10.0}, WIDTH_OUT)
MIDDLE = (0.0, 4.5, 12.0, 21.5, 26.0)


def place():
    gx = lax.axis_index("gx")
    yz = lax.axis_index("yz")
    return gx, yz // (Z * YL), (yz // YL) % Z, yz % YL


def flat(x, z, yl):
    return x * (Z * YL) + z * YL + yl


def copy_rows(move):
    def four(g, carry):
        for j in range(4):
            move(4 * g + j, g, j)
        return carry

    lax.fori_loop(0, 16, four, 0)


def kernel(
    cache_length, prefill_length, dtok, wkv, ptok, wq, wo, cache_hbm,
    prefill_out, decode_out,
    gp0, gp1, gda, gdb, w, wov, wt, cache, tloc, xda, xdb, dsend, drecv,
    accp, accd, give, takep, taked, tok, s1, r2, qj, qh,
    kvown, k2, att, heads, dec, dec2, ppa, ppb, pda, pdb, lpa, lpb, lda, ldb,
    opa, opb, oda, odb, psend, precv, dsend2, drecv2, pfin, pland,
    local, esend, erecv, send, recv, gsend, grecv, asend, arecv, hsend, hrecv,
    osend, orecv, fsend, frecv,
):
    gx, x, z, yl = place()
    yz = lax.axis_index("yz")
    core, y_hi = gx % 2, gx // 2
    own = {"da": xda, "db": xdb}
    got = dict(zip(KINDS_IN, (gp0, gp1, gda, gdb)))
    result = dict(zip(KINDS, (opa, opb, oda, odb)))
    held = dict(zip(KINDS, (ppa, ppb, pda, pdb)))
    landing = dict(zip(KINDS, (lpa, lpb, lda, ldb)))
    acc = {"p": accp, "d": accd}
    take = {"p": takep, "d": taked}
    pending = []

    def near(d):
        dx = {"x+": 1, "x-": X - 1}.get(d, 0)
        dz = {"z+": 1, "z-": Z - 1}.get(d, 0)
        return (gx, flat((x + dx) % X, (z + dz) % Z, yl))

    g_peers = [((gx + s) % GX, yz) for s in range(1, GX)]
    there = 1 - y_hi
    across = [(2 * there + o, flat(x, z, 1 - yl)) for o in range(2)]
    many = X * Z * YL

    def remote(src, dst, ssem, rsem, device):
        return pltpu.make_async_remote_copy(
            src_ref=src, dst_ref=dst, send_sem=ssem, recv_sem=rsem, device_id=device, device_id_type=MESH
        )

    def start(src, dst, ssem, rsem, device):
        c = remote(src, dst, ssem, rsem, device)
        c.start()
        pending.append(c)

    def arrive(dst, ssem, rsem):
        remote(dst, dst, ssem, rsem, near("x+")).wait_recv()

    barrier = pltpu.get_barrier_semaphore()
    peers = g_peers + across
    keeper = (x, flat(gx, z, yl))
    turned = x != gx

    def greet(n, carry):
        pl.semaphore_signal(barrier, inc=1, device_id=(gx, (yz + n) % many), device_id_type=MESH)
        return carry

    lax.fori_loop(1, many, greet, 0)
    for peer in peers:
        pl.semaphore_signal(barrier, inc=1, device_id=peer, device_id_type=MESH)

    @pl.when(turned)
    def _():
        pl.semaphore_signal(barrier, inc=1, device_id=keeper, device_id_type=MESH)

    group = wq.shape[1]
    loads = []

    def load(src, dst):
        c = pltpu.make_async_copy(src, dst, local.at[len(loads)])
        c.start()
        loads.append(c)
        return c

    dsend[:72, :256] = dtok[0]
    dsend[:72, 256:] = dtok[1]
    dsend[72:, :] = jnp.zeros((8, TOK), BF16)
    pl.semaphore_wait(barrier, many - 1 + len(peers) + turned.astype(jnp.int32))

    partner = (gx, flat(x, z, 1 - yl))
    start(dsend, drecv, esend.at[2], erecv.at[2], partner)
    for c in range(2):

        @pl.when(core == c)
        def _(c=c):
            for o in range(2):
                lane = pl.multiple_of((2 * there + o) * group + x * SPAN, 128)
                remote(
                    ptok.at[:, pl.ds(lane, SPAN)],
                    got["p%d" % c].at[x],
                    esend.at[o],
                    erecv.at[c],
                    across[o],
                ).start()

    w_load = load(wq, w.at[pl.ds(0, COLS)])
    mine_load = load(ptok.at[:, pl.ds(pl.multiple_of(gx * group, 128), group)], tloc.at[0])
    sibling_gx = gx + 1 - 2 * core
    start(
        ptok.at[:, pl.ds(pl.multiple_of(sibling_gx * group, 128), group)],
        tloc.at[1],
        esend.at[3],
        erecv.at[3],
        (sibling_gx, yz),
    )
    wo_load = load(wo, wov)
    cache_load = load(cache_hbm, cache)
    tok[...] = jnp.zeros(tok.shape, F32)
    qj[...] = jnp.zeros(qj.shape, F32)

    def slot(key, rows):
        kind, xo, zo = key
        if kind[0] == "p":
            return got[kind].at[(x + xo) % X]
        return got[kind].at[((x + xo) % X) * Z + (z + zo) % Z, pl.ds(rows[0], rows[1])]

    seen = {}

    def multiply(kind, xo):
        xx = (x + xo) % X
        part_of_w = w[:, pl.ds(pl.multiple_of(xx * SPAN, 128), SPAN)]
        if kind[0] == "p":
            part = lax.dot_general(
                part_of_w, got[kind][xx], (((1,), (1,)), ((), ())), preferred_element_type=F32
            )
            lanes = pl.ds(pl.multiple_of((2 * there + int(kind[1])) * 128, 128), 128)
        else:
            block = got[kind][pl.ds(xx * Z, Z)].reshape(SPAN, WIDTH_IN[kind])
            part = jnp.dot(part_of_w, block, preferred_element_type=F32)
            lanes = slice(START_IN[kind], START_IN[kind] + WIDTH_IN[kind])
        if kind in seen:
            acc[kind[0]][:, lanes] += part
        else:
            acc[kind[0]][:, lanes] = part
            seen[kind] = True

    def multiply_near(n):
        lanes = pl.ds(pl.multiple_of((gx if n == 0 else sibling_gx) * 128, 128), 128)
        acc["p"][:, lanes] = lax.dot_general(
            w[...], tloc[n], (((1,), (1,)), ((), ())), preferred_element_type=F32
        )

    def gather_node(key):
        kind, xo, zo = key
        mine = (xo, zo) == (0, 0)
        if not mine:
            for _, rows in IN.pieces[key]:
                k = IN.fills[(key, rows)]
                arrive(slot(key, rows), send.at[KINDS_IN.index(kind)], recv.at[k])
        elif kind[0] == "p":
            c = int(kind[1])
            arrive(slot(key, FULL), esend.at[c], erecv.at[c])
        elif kind == "db":
            arrive(drecv, esend.at[2], erecv.at[2])
            one, two = dsend[:72].astype(F32), drecv[:72].astype(F32)
            both = jnp.where(
                yl == 0, jnp.concatenate([one, two], axis=0), jnp.concatenate([two, one], axis=0)
            ).astype(BF16)
            xda[...] = both[:, : WIDTH_IN["da"]]
            xdb[...] = both[:, WIDTH_IN["da"] :]
        for n, (d, rows, there) in enumerate(steps_from(key)):
            k = IN.sends[(key, n)]
            remote(
                own[kind] if mine and kind in own else slot(key, rows),
                slot(key, rows),
                send.at[KINDS_IN.index(kind)],
                recv.at[k],
                near(d),
            ).start()
        if mine and kind in own:
            got[kind][x * Z + z] = own[kind][...]
        seen[(kind, xo)] = seen.get((kind, xo), 0) + 1
        if seen[(kind, xo)] == (1 if kind[0] == "p" else Z):
            multiply(kind, xo)

    def sum_start(f):
        if f == "d":
            rows = accd[...]
            for g in range(GX):
                accd[:, g * 128 : g * 128 + 64] = rows[:, g * 64 : g * 64 + 64]
                accd[:, g * 128 + 64 : g * 128 + 128] = rows[:, 256 + g * 64 : 320 + g * 64]
        for g in range(GX):
            give[n_of[f], g] = acc[f][:, g * 128 : g * 128 + 128].astype(BF16)
        for s in range(1, GX):
            start(
                give.at[n_of[f], (gx + s) % GX],
                take[f].at[s - 1],
                gsend.at[n_of[f], s],
                grecv.at[n_of[f], s],
                g_peers[s - 1],
            )

    n_of = {"p": 0, "d": 1}

    def exchange_start(i, also=None):
        def one(n, carry):
            to = (yz + n) % many
            remote(s1.at[i, to], r2.at[i, yz], asend.at[i], arecv.at[i], (gx, to)).start()
            if also:
                remote(kvown, k2.at[yz], asend.at[4], arecv.at[4], (gx, to)).start()
            return carry

        lax.fori_loop(1, many, one, 0)
        r2[i, yz] = s1[i, yz]
        if also:
            k2[yz] = kvown[...]

    def exchange_end(i):
        arrive(r2.at[i, pl.ds(0, many - 1)], asend.at[i], arecv.at[i])

    def token(f, r, t):
        return 2 * r + t if f == "p" else t * 64 + r

    def queries_start(f):
        for s in range(1, GX):
            arrive(take[f].at[s - 1], gsend.at[n_of[f], s], grecv.at[n_of[f], s])
        lane = pl.multiple_of(gx * 128, 128)
        total = acc[f][:, pl.ds(lane, 128)]
        for s in range(1, GX):
            total = total + take[f][s - 1].astype(F32)
        total = total.astype(BF16).astype(F32)
        tok[:, :ROWS1] = total.T
        i = 2 * n_of[f]

        def pack(r, g, j):
            for t in range(2):
                s1[i, r, pl.ds(t, 1), :] = tok[pl.ds(token(f, r, t), 1), :]

        copy_rows(pack)
        if f == "p":
            kvown[...] = total[COLS : COLS + KVC]
        exchange_start(i, f == "p")

    nt = (((1,), (1,)), ((), ()))
    scale = HD ** (-0.5)

    def attend(f):
        i = 2 * n_of[f]
        exchange_end(i)

        def unpack(r, g, j):
            for t in range(2):
                qj[j, pl.ds(t * 16 + g, 1), :] = r2[i, r, pl.ds(t, 1), :]

        copy_rows(unpack)
        qh[0:32, :192] = qj[0, :, :192]
        qh[0:32, 192:] = qj[1, :, :64]
        qh[32:64, :128] = qj[1, :, 64:192]
        qh[32:64, 128:] = qj[2, :, :128]
        qh[64:96, :64] = qj[2, :, 128:192]
        qh[64:96, 64:] = qj[3, :, :192]
        q32 = qh[...]
        q = q32.astype(BF16)
        if f == "p":
            arrive(k2.at[pl.ds(0, many - 1)], asend.at[4], arecv.at[4])
            kvt = k2[...].reshape(2 * HD, PLEN).astype(BF16)
            s = jnp.dot(q, kvt[:HD], preferred_element_type=F32) * scale
            query = 2 * yz + (lax.broadcasted_iota(jnp.int32, s.shape, 0) // 16) % 2
            pos = lax.broadcasted_iota(jnp.int32, s.shape, 1)
            s = jnp.where((pos <= query) & (pos < prefill_length[0]), s, -1e30)
            e = jnp.exp(s - jnp.max(s, axis=1, keepdims=True))
            probs = (e / jnp.sum(e, axis=1, keepdims=True)).astype(BF16)
            out = lax.dot_general(probs, kvt[HD:], nt, preferred_element_type=F32)
        else:
            row = lax.broadcasted_iota(jnp.int32, (KVC, 2 * HD), 0)
            lane = lax.broadcasted_iota(jnp.int32, (KVC, 2 * HD), 1)
            spread = (lane % KVC == row).astype(BF16)
            group = lax.broadcasted_iota(jnp.int32, (32, 2 * HD), 0) % 16
            holder = lax.broadcasted_iota(jnp.int32, (32, 2 * HD), 1) // KVC
            new = jnp.zeros((32, 2 * HD), F32)
            for j in range(4):
                wide = jnp.dot(
                    qj[j, :, COLS : COLS + KVC].astype(BF16), spread, preferred_element_type=F32
                )
                new = new + jnp.where(holder == 4 * group + j, wide, 0.0)
            new0 = jnp.sum(new[:16], axis=0, keepdims=True)
            new1 = jnp.sum(new[16:], axis=0, keepdims=True)
            s = lax.dot_general(q, cache[:, :HD], nt, preferred_element_type=F32) * scale
            pos = lax.broadcasted_iota(jnp.int32, s.shape, 1)
            s = jnp.where(pos < cache_length[0], s, -1e30)
            f0 = jnp.sum(q32 * new0[:, :HD], axis=1, keepdims=True) * scale
            f1 = jnp.sum(q32 * new1[:, :HD], axis=1, keepdims=True) * scale
            step = (lax.broadcasted_iota(jnp.int32, f1.shape, 0) // 16) % 2
            f1 = jnp.where(step == 1, f1, -1e30)
            peak = jnp.maximum(jnp.max(s, axis=1, keepdims=True), jnp.maximum(f0, f1))
            es, e0, e1 = jnp.exp(s - peak), jnp.exp(f0 - peak), jnp.exp(f1 - peak)
            total = jnp.sum(es, axis=1, keepdims=True) + e0 + e1
            out = jnp.dot((es / total).astype(BF16), cache[:, HD:], preferred_element_type=F32)
            out = out + (e0 / total).astype(BF16).astype(F32) * new0[:, HD:]
            out = out + (e1 / total).astype(BF16).astype(F32) * new1[:, HD:]
        qh[...] = out.astype(BF16).astype(F32)
        qj[0, :, :192] = qh[0:32, :192]
        qj[1, :, :64] = qh[0:32, 192:]
        qj[1, :, 64:192] = qh[32:64, :128]
        qj[2, :, :128] = qh[32:64, 128:]
        qj[2, :, 128:192] = qh[64:96, :64]
        qj[3, :, :192] = qh[64:96, 64:]

        def pack(r, g, j):
            for t in range(2):
                s1[i + 1, r, pl.ds(t, 1), :] = qj[j, pl.ds(t * 16 + g, 1), :]

        copy_rows(pack)
        exchange_start(i + 1)

    def attended_share(f):
        n = n_of[f]
        i = 2 * n + 1
        exchange_end(i)

        def unpack(r, g, j):
            for t in range(2):
                tok[pl.ds(token(f, r, t), 1), :] = r2[i, r, pl.ds(t, 1), :]

        copy_rows(unpack)
        att[n] = tok[...].T[:COLS].astype(BF16)
        for s in range(1, GX):
            start(att.at[n], heads.at[n, s], hsend.at[n, s], hrecv.at[n, s], g_peers[s - 1])
        heads[n, 0] = att[n]

    def attended_end(f):
        n = n_of[f]
        for s in range(1, GX):
            arrive(heads.at[n, s], hsend.at[n, s], hrecv.at[n, s])
        if f == "d":
            for s in range(GX):
                lane = pl.multiple_of(((gx - s + GX) % GX) * 128, 128)
                dec2[:, pl.ds(lane, 128)] = heads[n, s]
            for g in range(GX):
                for t in range(2):
                    dec[:, t * 256 + g * 64 : t * 256 + g * 64 + 64] = dec2[
                        :, g * 128 + t * 64 : g * 128 + t * 64 + 64
                    ]

    def terms(key):
        kind, xo, zo = key
        xx, zz = (x + xo) % X, (z + zo) % Z
        if kind[0] == "d":
            first = pl.multiple_of((xx * Z + zz) * BLK, 16)
            lanes = slice(START[kind], START[kind] + WIDTH_OUT[kind])
            return jnp.dot(wt[pl.ds(first, BLK), :], dec[:, lanes], preferred_element_type=F32)
        group = heads[0, (gx - xx + GX) % GX]
        parts = []
        for q in range(START[kind] // 128, (START[kind] + WIDTH_OUT[kind]) // 128):
            first = pl.multiple_of(zz * (4 * BLK) + q * BLK, 16)
            parts.append(jnp.dot(wt[pl.ds(first, BLK), :], group, preferred_element_type=F32))
        return jnp.concatenate(parts, axis=1)

    def scatter_node(key):
        kind, xo, zo = key
        last = (xo, zo) == (0, 0)
        at = ((x + xo) % X) * Z + (z + zo) % Z
        local = terms(key)
        steps = steps_from(key)
        for n, (d, rows, there) in enumerate(steps):
            k = OUT.sends[(key, n)]
            spot = landing[kind].at[OUT.where[(key, n)], pl.ds(rows[0], rows[1])]
            arrive(spot, osend.at[KINDS.index(kind)], orecv.at[k])
        halves = [local[:80], local[80:]]
        for n, (d, rows, there) in enumerate(steps):
            for i, (r0, rn) in enumerate((UPPER, LOWER)):
                if rows[0] <= r0 and r0 + rn <= rows[0] + rows[1]:
                    halves[i] = halves[i] + landing[kind][OUT.where[(key, n)], r0 : r0 + rn].astype(F32)
        for i, (r0, rn) in enumerate((UPPER, LOWER)):
            if last:
                result[kind][r0 : r0 + rn] = halves[i]
            else:
                held[kind][at, r0 : r0 + rn] = halves[i].astype(BF16)
        if not last:
            for d, rows in OUT.pieces[key]:
                k = OUT.fills[(key, rows)]
                remote(
                    held[kind].at[at, pl.ds(rows[0], rows[1])],
                    landing[kind].at[OUT.where[OUT.source[k]], pl.ds(rows[0], rows[1])],
                    osend.at[KINDS.index(kind)],
                    orecv.at[k],
                    near(OPPOSITE[d]),
                ).start()

    def prefill_halves():
        psend[...] = jnp.where(yl == 0, opb[...], opa[...]).astype(BF16)
        start(psend, precv, fsend.at[0], frecv.at[0], partner)

    def prefill_turn():
        arrive(precv, fsend.at[0], frecv.at[0])
        pre_sum = jnp.where(yl == 0, opa[...], opb[...]) + precv[...].astype(F32)
        for q in range(2):
            pfin[q * BLK : q * BLK + BLK] = pre_sum[:, q * 128 : q * 128 + 128].astype(BF16)

        @pl.when(turned)
        def _():
            remote(pfin, pland, fsend.at[2], frecv.at[2], keeper).start()

    def prefill_end():
        @pl.when(turned)
        def _():
            remote(pfin, pland, fsend.at[2], frecv.at[2], keeper).wait()
            prefill_out[...] = pland[...]

        @pl.when(x == gx)
        def _():
            prefill_out[...] = pfin[...]

    def weights():
        w_load.wait()
        w[COLS:, :] = jnp.concatenate([wkv[...].astype(F32), jnp.zeros((8, group), F32)]).astype(BF16)
        mine_load.wait()
        multiply_near(0)

    def turn_weights():
        wo_load.wait()
        for n in range(group // 512):
            wt[pl.ds(512 * n, 512), :] = wov[:, 512 * n : 512 * n + 512].T

    def sibling():
        arrive(tloc.at[1], esend.at[3], erecv.at[3])
        multiply_near(1)
        cache_load.wait()

    middle = (sum_start, queries_start, attend, attended_share, attended_end)
    todo = [(IN.times[key], gather_node, key) for key in IN.order]
    todo.append((1.5, lambda _: weights(), None))
    todo.append((9.0, lambda _: sibling(), None))
    ends = {}
    for f in "pd":
        ready = max(IN.times[key] for key in IN.order if key[0][0] == f) + 0.5
        todo += [(ready + MIDDLE[n], step, f) for n, step in enumerate(middle)]
        ends[f] = ready + MIDDLE[-1]
        if f == "p":
            todo.append((ready + MIDDLE[1] + 0.1, lambda _: turn_weights(), None))
    begin = ends["p"] + 0.1
    out_times = {key: begin + OUT.end - OUT.times[key] for key in OUT.order}
    first_d = min(t for key, t in out_times.items() if key[0][0] == "d")
    shift = max(0.0, ends["d"] + 0.1 - first_d)
    for key in reversed(OUT.order):
        todo.append((out_times[key] + (shift if key[0][0] == "d" else 0.0), scatter_node, key))
    last_p = max(t for key, t in out_times.items() if key[0][0] == "p")
    todo.append((last_p + 0.1, lambda _: prefill_halves(), None))
    todo.append((last_p + 6.0, lambda _: prefill_turn(), None))
    for _, step, what in sorted(todo, key=lambda entry: entry[0]):
        step(what)

    dec_sum = jnp.concatenate([oda[...], odb[...]], axis=1)
    dsend2[:72] = jnp.where(yl == 0, dec_sum[72:], dec_sum[:72]).astype(BF16)
    dsend2[72:] = jnp.zeros((8, TOK), BF16)
    start(dsend2, drecv2, fsend.at[1], frecv.at[1], partner)
    prefill_end()
    arrive(drecv2, fsend.at[1], frecv.at[1])
    dec_sum = jnp.where(yl == 0, dec_sum[:72], dec_sum[72:]) + drecv2[:72].astype(F32)
    for t in range(2):
        decode_out[t] = dec_sum[:, t * 256 : t * 256 + 256].astype(BF16)

    for n, kind in enumerate(KINDS_IN):
        sent = got[kind].at[pl.ds(0, 3 if kind[0] == "p" else X * Z - 1)]
        remote(sent, sent, send.at[n], recv.at[0], partner).wait_send()
    for n, kind in enumerate(KINDS):
        sent = held[kind].at[pl.ds(0, X * Z - 1)]
        remote(sent, sent, osend.at[n], orecv.at[0], partner).wait_send()
    for o in range(2):
        sent = got["p0"].at[0]
        remote(sent, sent, esend.at[o], erecv.at[o], partner).wait_send()
    for i in range(4):
        sent = s1.at[i, pl.ds(0, many - 1)]
        remote(sent, sent, asend.at[i], arecv.at[i], partner).wait_send()
    sent = k2.at[pl.ds(0, many - 1)]
    remote(sent, sent, asend.at[4], arecv.at[4], partner).wait_send()
    for c in pending:
        c.wait_send()


def run(cache_length, prefill_length, dtok, wkv, ptok, wq, wo, cache):
    vmem = pl.BlockSpec(memory_space=pltpu.VMEM)
    hbm = pl.BlockSpec(memory_space=pl.ANY)
    dma = pltpu.SemaphoreType.DMA
    group = wq.shape[1]

    def scratch(*shape, dtype=BF16):
        return pltpu.VMEM(shape, dtype)

    return pl.pallas_call(
        kernel,
        out_shape=(
            jax.ShapeDtypeStruct((2 * BLK, PLEN), BF16),
            jax.ShapeDtypeStruct((2, 72, 256), BF16),
        ),
        in_specs=[pl.BlockSpec(memory_space=pltpu.SMEM)] * 2 + [vmem, vmem, hbm, hbm, hbm, hbm],
        out_specs=(vmem, vmem),
        scratch_shapes=[
            scratch(X, PLEN, SPAN),
            scratch(X, PLEN, SPAN),
            scratch(X * Z, BLK, WIDTH_IN["da"]),
            scratch(X * Z, BLK, WIDTH_IN["db"]),
            scratch(ROWS1, group),
            scratch(COLS, group),
            scratch(group, COLS),
            scratch(*cache.shape),
            scratch(2, PLEN, group),
            scratch(BLK, WIDTH_IN["da"]),
            scratch(BLK, WIDTH_IN["db"]),
            scratch(80, TOK),
            scratch(80, TOK),
            scratch(ROWS1, TOK, dtype=F32),
            scratch(ROWS1, TOK, dtype=F32),
            scratch(2, GX, ROWS1, 128),
            scratch(GX - 1, ROWS1, 128),
            scratch(GX - 1, ROWS1, 128),
            scratch(128, 256, dtype=F32),
            scratch(4, X * Z * YL, 2, 256, dtype=F32),
            scratch(4, X * Z * YL, 2, 256, dtype=F32),
            scratch(4, 32, 256, dtype=F32),
            scratch(96, 256, dtype=F32),
            scratch(KVC, PLEN, dtype=F32),
            scratch(X * Z * YL, KVC, PLEN, dtype=F32),
            scratch(2, COLS, 128),
            scratch(2, GX, COLS, 128),
            scratch(COLS, TOK),
            scratch(COLS, TOK),
        ]
        + [scratch(X * Z, BLK, WIDTH_OUT[k]) for k in KINDS]
        + [scratch(OUT.slots[k], BLK, WIDTH_OUT[k]) for k in KINDS]
        + [scratch(BLK, WIDTH_OUT[k], dtype=F32) for k in KINDS]
        + [
            scratch(BLK, 256),
            scratch(BLK, 256),
            scratch(80, TOK),
            scratch(80, TOK),
            scratch(2 * BLK, PLEN),
            scratch(2 * BLK, PLEN),
            dma((4,)),
            dma((4,)),
            dma((4,)),
            dma((4,)),
            dma((len(IN.sends),)),
            dma((2, GX)),
            dma((2, GX)),
            dma((5,)),
            dma((5,)),
            dma((2, GX)),
            dma((2, GX)),
            dma((4,)),
            dma((len(OUT.sends),)),
            dma((3,)),
            dma((3,)),
        ],
        compiler_params=pltpu.CompilerParams(
            collective_id=0, has_side_effects=True, vmem_limit_bytes=60 * 2**20
        ),
        name="attention_block",
    )(cache_length, prefill_length, dtok, wkv, ptok, wq, wo, cache)


def body(
    prefill_tokens,
    prefill_lengths,
    decode_tokens,
    cache_lengths,
    cache_keyvals,
    query_weight,
    keyval_weight,
    out_weight,
):
    prefill_out, decode_out = run(
        cache_lengths,
        prefill_lengths,
        decode_tokens.transpose(0, 2, 1),
        keyval_weight.T,
        prefill_tokens,
        query_weight.T,
        out_weight,
        cache_keyvals[0],
    )
    return (prefill_out.T, decode_out.transpose(0, 2, 1))


def solution(mesh):
    in_specs = (
        P("gx", None),
        P("gx"),
        P(None, None, ("gx", "yz")),
        P(("gx", "yz")),
        P(("gx", "yz"), None, None),
        P("gx", "yz"),
        P("gx", "yz"),
        P("yz", "gx"),
    )
    out_specs = (P("gx", "yz"), P(None, None, ("gx", "yz")))
    return jax.shard_map(body, mesh=mesh, in_specs=in_specs, out_specs=out_specs, check_vma=False)
```

```python
import heapq

import jax
import jax.numpy as jnp
from jax import lax
from jax.experimental import pallas as pl
from jax.experimental.pallas import tpu as pltpu
from jax.sharding import PartitionSpec as P

HEADS = 48
HD = 256
PLEN = 128
GX, X, Z, YL = 4, 4, 8, 2
BLK = 144
TOK = 512
WIDTH_IN = {"p0": 1024, "p1": 1024, "da": 128, "db": 384}
WIDTH_OUT = {"pa": 256, "pb": 256, "da": 384, "db": 128}
START_IN = {"da": 0, "db": 128}
START = {"pa": 0, "pb": 256, "da": 0, "db": 384}
KINDS = tuple(START)
KINDS_IN = tuple(WIDTH_IN)
FAR = {"p0": 21.0, "p1": 27.0}
SPAN = Z * BLK
COLS = 192
KVC = 8
ROWS1 = 208
MESH = pl.DeviceIdType.MESH
F32 = jnp.float32
BF16 = jnp.bfloat16
FULL, UPPER, LOWER = (0, 144), (0, 80), (80, 64)
OPPOSITE = {"x+": "x-", "x-": "x+", "z+": "z-", "z-": "z+"}


def steps_from(key):
    kind, xo, zo = key
    out = []
    if kind in ("p0", "p1"):
        if xo == 0:
            out.append(("x+", FULL, (kind, -1, 0)))
            out.append(("x-", FULL, (kind, 1, 0)))
    elif kind[1] == "a":
        if xo == 0:
            if -3 < zo <= 0:
                out.append(("z+", FULL, (kind, 0, zo - 1)))
            if zo == -3:
                out.append(("z+", UPPER, (kind, 0, 4)))
            if 0 <= zo < 3:
                out.append(("z-", FULL, (kind, 0, zo + 1)))
            if zo == 3:
                out.append(("z-", LOWER, (kind, 0, 4)))
            out.append(("x+", FULL, (kind, -1, zo)))
            out.append(("x-", FULL, (kind, 1, zo)))
        elif xo == -1 and zo % 2 == 0:
            out.append(("x+", FULL, (kind, 2, zo)))
        elif xo == 1 and zo % 2 == 1:
            out.append(("x-", FULL, (kind, 2, zo)))
    else:
        if zo == 0:
            if xo == 0:
                out.append(("x+", FULL, (kind, -1, 0)))
                out.append(("x-", FULL, (kind, 1, 0)))
            elif xo == -1:
                out.append(("x+", UPPER, (kind, 2, 0)))
            elif xo == 1:
                out.append(("x-", LOWER, (kind, 2, 0)))
        if zo <= 0 and (zo > -3 or xo in (0, 2)):
            out.append(("z+", FULL, (kind, xo, zo - 1 if zo > -3 else 4)))
        if 0 <= zo <= 3 and (zo < 3 or xo in (-1, 1)):
            out.append(("z-", FULL, (kind, xo, zo + 1)))
    return out


class Plan:
    def __init__(self, releases, width):
        free = dict.fromkeys(OPPOSITE, 0.0)
        events, self.order, self.times, self.pieces = [], [], {}, {}
        self.sends, self.fills, self.source, self.where = {}, {}, {}, {}
        self.slots = dict.fromkeys(releases, 0)

        def leave(key, now):
            self.order.append(key)
            self.times[key] = now
            for n, (d, rows, there) in enumerate(steps_from(key)):
                free[d] = max(free[d], now) + width[key[0]] * rows[1] * 4e-5
                k = len(self.sends)
                self.sends[(key, n)] = k
                self.fills[(there, rows)] = k
                self.source[k] = (key, n)
                self.where[(key, n)] = self.slots[key[0]]
                self.slots[key[0]] += 1
                heapq.heappush(events, (free[d] + 3.0, k, there, (d, rows)))

        for n, kind in enumerate(releases):
            heapq.heappush(events, (releases[kind], n - len(releases), (kind, 0, 0), None))
            if kind in FAR:
                heapq.heappush(events, (FAR[kind], n - len(releases), (kind, 2, 0), None))
        while events:
            now, _, key, piece = heapq.heappop(events)
            if piece is not None:
                self.pieces.setdefault(key, []).append(piece)
            if piece is None or sum(p[1][1] for p in self.pieces[key]) == BLK:
                leave(key, now)
        self.end = max(self.times.values())


IN = Plan({"db": 0.0, "da": 0.0, "p0": 9.0, "p1": 15.0}, WIDTH_IN)
OUT = Plan({"db": 0.0, "da": 0.0, "pb": 20.0, "pa": 20.0}, WIDTH_OUT)
MIDDLE = {"p": (0.0, 4.5, 8.5, 13.0, 18.0, 22.0), "d": (0.0, 4.5, 10.5, 15.5, 23.5, 28.5, 33.0)}
QUAD = 4


def place():
    gx = lax.axis_index("gx")
    yz = lax.axis_index("yz")
    return gx, yz // (Z * YL), (yz // YL) % Z, yz % YL


def flat(x, z, yl):
    return x * (Z * YL) + z * YL + yl


def copy_rows(move):
    def four(g, carry):
        for j in range(QUAD):
            move(g // 4, (g % 4) * 2 + j // 2, j % 2, g, j)
        return carry

    lax.fori_loop(0, 16, four, 0)


def kernel(
    cache_length, prefill_length, dtok, wkv, ptok, wq, wo, cache_hbm,
    prefill_out, decode_out,
    gp0, gp1, gda, gdb, w, wov, wt, cache, tloc, xda, xdb, dsend, drecv,
    accp, accd, give, takep, taked, tok, tokp, backp, s1, r1, r2, qj, qjp, qh,
    kvown, k1, k2, att, heads, dec, dec2, ppa, ppb, pda, pdb, lpa, lpb, lda, ldb,
    opa, opb, oda, odb, psend, precv, dsend2, drecv2, pfin, pland,
    local, esend, erecv, send, recv, gsend, grecv, asend, arecv, ksend, krecv, qsend, qrecv, hsend, hrecv,
    osend, orecv, fsend, frecv,
):
    gx, x, z, yl = place()
    yz = lax.axis_index("yz")
    core, y_hi = gx % 2, gx // 2
    own = {"da": xda, "db": xdb}
    got = dict(zip(KINDS_IN, (gp0, gp1, gda, gdb)))
    result = dict(zip(KINDS, (opa, opb, oda, odb)))
    held = dict(zip(KINDS, (ppa, ppb, pda, pdb)))
    landing = dict(zip(KINDS, (lpa, lpb, lda, ldb)))
    acc = {"p": accp, "d": accd}
    take = {"p": takep, "d": taked}
    pending = []

    def near(d):
        dx = {"x+": 1, "x-": X - 1}.get(d, 0)
        dz = {"z+": 1, "z-": Z - 1}.get(d, 0)
        return (gx, flat((x + dx) % X, (z + dz) % Z, yl))

    g_peers = [((gx + s) % GX, yz) for s in range(1, GX)]
    there = 1 - y_hi
    across = [(2 * there + o, flat(x, z, 1 - yl)) for o in range(2)]
    z_peers = [(gx, flat(x, (z + s) % Z, yl)) for s in range(1, Z)]
    xy_peers = [(gx, flat((x + e // 2) % X, z, (yl + e) % YL)) for e in range(1, X * YL)]
    quad_first = (yz // QUAD) * QUAD
    place_in_quad = yz % QUAD
    quad_peers = [(gx, quad_first + (place_in_quad + s) % QUAD) for s in range(1, QUAD)]
    diagonal = (gx, flat(x, z + 1 - 2 * (z % 2), 1 - yl))

    def remote(src, dst, ssem, rsem, device):
        return pltpu.make_async_remote_copy(
            src_ref=src, dst_ref=dst, send_sem=ssem, recv_sem=rsem, device_id=device, device_id_type=MESH
        )

    def start(src, dst, ssem, rsem, device):
        c = remote(src, dst, ssem, rsem, device)
        c.start()
        pending.append(c)

    def arrive(dst, ssem, rsem):
        remote(dst, dst, ssem, rsem, near("x+")).wait_recv()

    barrier = pltpu.get_barrier_semaphore()
    peers = z_peers + xy_peers + [diagonal] + g_peers + across
    keeper = (x, flat(gx, z, yl))
    turned = x != gx

    for peer in peers:
        pl.semaphore_signal(barrier, inc=1, device_id=peer, device_id_type=MESH)

    @pl.when(turned)
    def _():
        pl.semaphore_signal(barrier, inc=1, device_id=keeper, device_id_type=MESH)

    group = wq.shape[1]
    loads = []

    def load(src, dst):
        c = pltpu.make_async_copy(src, dst, local.at[len(loads)])
        c.start()
        loads.append(c)
        return c

    dsend[:72, :256] = dtok[0]
    dsend[:72, 256:] = dtok[1]
    dsend[72:, :] = jnp.zeros((8, TOK), BF16)
    pl.semaphore_wait(barrier, len(peers) + turned.astype(jnp.int32))

    partner = (gx, flat(x, z, 1 - yl))
    start(dsend, drecv, esend.at[2], erecv.at[2], partner)
    for c in range(2):

        @pl.when(core == c)
        def _(c=c):
            for far in range(2):
                xx = (x + 2 * far) % X
                for o in range(2):
                    lane = pl.multiple_of((2 * there + o) * group + xx * SPAN, 128)
                    remote(
                        ptok.at[:, pl.ds(lane, SPAN)],
                        got["p%d" % c].at[xx],
                        esend.at[4 * far + o],
                        erecv.at[4 * far + c],
                        across[o],
                    ).start()

    w_load = load(wq, w.at[pl.ds(0, COLS)])
    mine_load = load(ptok.at[:, pl.ds(pl.multiple_of(gx * group, 128), group)], tloc.at[0])
    sibling_gx = gx + 1 - 2 * core
    start(
        ptok.at[:, pl.ds(pl.multiple_of(sibling_gx * group, 128), group)],
        tloc.at[1],
        esend.at[3],
        erecv.at[3],
        (sibling_gx, yz),
    )
    wo_load = load(wo, wov)
    cache_load = load(cache_hbm, cache)
    for ref in (tok, tokp, qj):
        ref[...] = jnp.zeros(ref.shape, F32)

    def slot(key, rows):
        kind, xo, zo = key
        if kind[0] == "p":
            return got[kind].at[(x + xo) % X]
        return got[kind].at[((x + xo) % X) * Z + (z + zo) % Z, pl.ds(rows[0], rows[1])]

    seen = {}

    def multiply(kind, xo):
        xx = (x + xo) % X
        part_of_w = w[:, pl.ds(pl.multiple_of(xx * SPAN, 128), SPAN)]
        if kind[0] == "p":
            part = lax.dot_general(
                part_of_w, got[kind][xx], (((1,), (1,)), ((), ())), preferred_element_type=F32
            )
            lanes = pl.ds(pl.multiple_of((2 * there + int(kind[1])) * 128, 128), 128)
        else:
            block = got[kind][pl.ds(xx * Z, Z)].reshape(SPAN, WIDTH_IN[kind])
            part = jnp.dot(part_of_w, block, preferred_element_type=F32)
            lanes = slice(START_IN[kind], START_IN[kind] + WIDTH_IN[kind])
        if kind in seen:
            acc[kind[0]][:, lanes] += part
        else:
            acc[kind[0]][:, lanes] = part
            seen[kind] = True

    def multiply_near(n):
        lanes = pl.ds(pl.multiple_of((gx if n == 0 else sibling_gx) * 128, 128), 128)
        acc["p"][:, lanes] = lax.dot_general(
            w[...], tloc[n], (((1,), (1,)), ((), ())), preferred_element_type=F32
        )

    def gather_node(key):
        kind, xo, zo = key
        mine = (xo, zo) == (0, 0)
        if xo == 2 and kind in FAR:
            c = 4 + int(kind[1])
            arrive(slot(key, FULL), esend.at[c], erecv.at[c])
        elif not mine:
            for _, rows in IN.pieces[key]:
                k = IN.fills[(key, rows)]
                arrive(slot(key, rows), send.at[KINDS_IN.index(kind)], recv.at[k])
        elif kind[0] == "p":
            c = int(kind[1])
            arrive(slot(key, FULL), esend.at[c], erecv.at[c])
        elif kind == "db":
            arrive(drecv, esend.at[2], erecv.at[2])
            one, two = dsend[:72].astype(F32), drecv[:72].astype(F32)
            both = jnp.where(
                yl == 0, jnp.concatenate([one, two], axis=0), jnp.concatenate([two, one], axis=0)
            ).astype(BF16)
            xda[...] = both[:, : WIDTH_IN["da"]]
            xdb[...] = both[:, WIDTH_IN["da"] :]
        for n, (d, rows, there) in enumerate(steps_from(key)):
            k = IN.sends[(key, n)]
            remote(
                own[kind] if mine and kind in own else slot(key, rows),
                slot(key, rows),
                send.at[KINDS_IN.index(kind)],
                recv.at[k],
                near(d),
            ).start()
        if mine and kind in own:
            got[kind][x * Z + z] = own[kind][...]
        seen[(kind, xo)] = seen.get((kind, xo), 0) + 1
        if seen[(kind, xo)] == (1 if kind[0] == "p" else Z):
            multiply(kind, xo)

    def sum_start(f):
        if f == "d":
            rows = accd[...]
            for g in range(GX):
                accd[:, g * 128 : g * 128 + 64] = rows[:, g * 64 : g * 64 + 64]
                accd[:, g * 128 + 64 : g * 128 + 128] = rows[:, 256 + g * 64 : 320 + g * 64]
        for g in range(GX):
            give[n_of[f], g] = acc[f][:, g * 128 : g * 128 + 128].astype(BF16)
        for s in range(1, GX):
            start(
                give.at[n_of[f], (gx + s) % GX],
                take[f].at[s - 1],
                gsend.at[n_of[f], s],
                grecv.at[n_of[f], s],
                g_peers[s - 1],
            )

    n_of = {"p": 0, "d": 1}

    def exchange_z(i):
        for s in range(1, Z):
            start(
                s1.at[i, :, (z + s) % Z],
                r1.at[i, :, z],
                asend.at[i, s],
                arecv.at[i, s],
                z_peers[s - 1],
            )
        r1[i, :, z] = s1[i, :, z]

    def exchange_xy(i):
        for s in range(1, Z):
            arrive(r1.at[i, :, (z + Z - s) % Z], asend.at[i, s], arecv.at[i, s])
        for e in range(1, X * YL):
            start(
                r1.at[i, (x + e // 2) % X, :, (yl + e) % YL],
                r2.at[i, x, :, yl],
                asend.at[i, Z + e],
                arecv.at[i, Z + e],
                xy_peers[e - 1],
            )
        r2[i, x, :, yl] = r1[i, x, :, yl]

    def exchange_end(i):
        for e in range(1, X * YL):
            arrive(
                r2.at[i, (x + X - e // 2) % X, :, (yl + e) % YL], asend.at[i, Z + e], arecv.at[i, Z + e]
            )

    def queries_start(f):
        for s in range(1, GX):
            arrive(take[f].at[s - 1], gsend.at[n_of[f], s], grecv.at[n_of[f], s])
        lane = pl.multiple_of(gx * 128, 128)
        total = acc[f][:, pl.ds(lane, 128)]
        for s in range(1, GX):
            total = total + take[f][s - 1].astype(F32)
        total = total.astype(BF16).astype(F32)
        if f == "p":
            tokp[:, :ROWS1] = total.T
            for s in range(1, QUAD):
                to = (place_in_quad + s) % QUAD
                start(
                    tokp.at[pl.ds(pl.multiple_of(32 * to, 32), 32)],
                    qjp.at[place_in_quad],
                    qsend.at[0, s],
                    qrecv.at[0, s],
                    quad_peers[s - 1],
                )
            qjp[place_in_quad] = tokp[pl.ds(pl.multiple_of(32 * place_in_quad, 32), 32), :]
            kvown[...] = total[COLS : COLS + KVC]
            for s in range(1, Z):
                start(kvown, k1.at[z], ksend.at[s], krecv.at[s], z_peers[s - 1])
            k1[z] = kvown[...]
            return
        tok[:, :ROWS1] = total.T

        def pack(xx, zz, yy, g, j):
            r = flat(xx, zz, yy)
            for t in range(2):
                s1[0, xx, zz, yy, pl.ds(t, 1), :] = tok[pl.ds(t * 64 + r, 1), :]

        copy_rows(pack)
        exchange_z(0)

    def queries_pass(f):
        if f == "d":
            exchange_xy(0)
            return
        for s in range(1, Z):
            arrive(k1.at[(z + Z - s) % Z], ksend.at[s], krecv.at[s])
        for e in range(1, X * YL):
            start(k1, k2.at[x, :, yl], ksend.at[Z + e], krecv.at[Z + e], xy_peers[e - 1])
        k2[x, :, yl] = k1[...]

    nt = (((1,), (1,)), ((), ()))
    scale = HD ** (-0.5)

    def attend(f):
        if f == "p":
            for s in range(1, QUAD):
                arrive(
                    qjp.at[(place_in_quad + QUAD - s) % QUAD], qsend.at[0, s], qrecv.at[0, s]
                )
            piece = qjp
        else:
            exchange_end(0)

            def unpack(xx, zz, yy, g, j):
                for t in range(2):
                    qj[j, pl.ds(t * 16 + g, 1), :] = r2[0, xx, zz, yy, pl.ds(t, 1), :]

            copy_rows(unpack)
            piece = qj
        qh[0:32, :192] = piece[0, :, :192]
        qh[0:32, 192:] = piece[1, :, :64]
        qh[32:64, :128] = piece[1, :, 64:192]
        qh[32:64, 128:] = piece[2, :, :128]
        qh[64:96, :64] = piece[2, :, 128:192]
        qh[64:96, 64:] = piece[3, :, :192]
        q32 = qh[...]
        q = q32.astype(BF16)
        if f == "p":
            for e in range(1, X * YL):
                arrive(k2.at[(x + X - e // 2) % X, :, (yl + e) % YL], ksend.at[Z + e], krecv.at[Z + e])
            kvt = k2[...].reshape(2 * HD, PLEN).astype(BF16)
            s = jnp.dot(q, kvt[:HD], preferred_element_type=F32) * scale
            query = 32 * place_in_quad + lax.broadcasted_iota(jnp.int32, s.shape, 0) % 32
            pos = lax.broadcasted_iota(jnp.int32, s.shape, 1)
            s = jnp.where((pos <= query) & (pos < prefill_length[0]), s, -1e30)
            e = jnp.exp(s - jnp.max(s, axis=1, keepdims=True))
            probs = (e / jnp.sum(e, axis=1, keepdims=True)).astype(BF16)
            out = lax.dot_general(probs, kvt[HD:], nt, preferred_element_type=F32)
        else:
            row = lax.broadcasted_iota(jnp.int32, (KVC, 2 * HD), 0)
            lane = lax.broadcasted_iota(jnp.int32, (KVC, 2 * HD), 1)
            spread = (lane % KVC == row).astype(BF16)
            group = lax.broadcasted_iota(jnp.int32, (32, 2 * HD), 0) % 16
            holder = lax.broadcasted_iota(jnp.int32, (32, 2 * HD), 1) // KVC
            new = jnp.zeros((32, 2 * HD), F32)
            for j in range(4):
                wide = jnp.dot(
                    qj[j, :, COLS : COLS + KVC].astype(BF16), spread, preferred_element_type=F32
                )
                new = new + jnp.where(holder == 4 * group + j, wide, 0.0)
            new0 = jnp.sum(new[:16], axis=0, keepdims=True)
            new1 = jnp.sum(new[16:], axis=0, keepdims=True)
            s = lax.dot_general(q, cache[:, :HD], nt, preferred_element_type=F32) * scale
            pos = lax.broadcasted_iota(jnp.int32, s.shape, 1)
            s = jnp.where(pos < cache_length[0], s, -1e30)
            f0 = jnp.sum(q32 * new0[:, :HD], axis=1, keepdims=True) * scale
            f1 = jnp.sum(q32 * new1[:, :HD], axis=1, keepdims=True) * scale
            step = (lax.broadcasted_iota(jnp.int32, f1.shape, 0) // 16) % 2
            f1 = jnp.where(step == 1, f1, -1e30)
            peak = jnp.maximum(jnp.max(s, axis=1, keepdims=True), jnp.maximum(f0, f1))
            es, e0, e1 = jnp.exp(s - peak), jnp.exp(f0 - peak), jnp.exp(f1 - peak)
            total = jnp.sum(es, axis=1, keepdims=True) + e0 + e1
            out = jnp.dot((es / total).astype(BF16), cache[:, HD:], preferred_element_type=F32)
            out = out + (e0 / total).astype(BF16).astype(F32) * new0[:, HD:]
            out = out + (e1 / total).astype(BF16).astype(F32) * new1[:, HD:]
        qh[...] = out.astype(BF16).astype(F32)
        piece[0, :, :192] = qh[0:32, :192]
        piece[1, :, :64] = qh[0:32, 192:]
        piece[1, :, 64:192] = qh[32:64, :128]
        piece[2, :, :128] = qh[32:64, 128:]
        piece[2, :, 128:192] = qh[64:96, :64]
        piece[3, :, :192] = qh[64:96, 64:]

        if f == "p":
            for s in range(1, QUAD):
                start(
                    piece.at[(place_in_quad + s) % QUAD],
                    backp.at[pl.ds(pl.multiple_of(32 * place_in_quad, 32), 32)],
                    qsend.at[1, s],
                    qrecv.at[1, s],
                    quad_peers[s - 1],
                )
            backp[pl.ds(pl.multiple_of(32 * place_in_quad, 32), 32), :] = piece[place_in_quad]
            return

        def pack(xx, zz, yy, g, j):
            for t in range(2):
                s1[1, xx, zz, yy, pl.ds(t, 1), :] = qj[j, pl.ds(t * 16 + g, 1), :]

        copy_rows(pack)
        exchange_z(1)

    def attended_pass(f):
        exchange_xy(1)

    def attended_share(f):
        n = n_of[f]
        if f == "p":
            for s in range(1, QUAD):
                first = 32 * ((place_in_quad + QUAD - s) % QUAD)
                arrive(
                    backp.at[pl.ds(pl.multiple_of(first, 32), 32)], qsend.at[1, s], qrecv.at[1, s]
                )
            att[n] = backp[...].T[:COLS].astype(BF16)
        else:
            exchange_end(1)

            def unpack(xx, zz, yy, g, j):
                r = flat(xx, zz, yy)
                for t in range(2):
                    tok[pl.ds(t * 64 + r, 1), :] = r2[1, xx, zz, yy, pl.ds(t, 1), :]

            copy_rows(unpack)
            att[n] = tok[...].T[:COLS].astype(BF16)
        for s in range(1, GX):
            start(att.at[n], heads.at[n, s], hsend.at[n, s], hrecv.at[n, s], g_peers[s - 1])
        heads[n, 0] = att[n]

    def attended_end(f):
        n = n_of[f]
        for s in range(1, GX):
            arrive(heads.at[n, s], hsend.at[n, s], hrecv.at[n, s])
        if f == "d":
            for s in range(GX):
                lane = pl.multiple_of(((gx - s + GX) % GX) * 128, 128)
                dec2[:, pl.ds(lane, 128)] = heads[n, s]
            for g in range(GX):
                for t in range(2):
                    dec[:, t * 256 + g * 64 : t * 256 + g * 64 + 64] = dec2[
                        :, g * 128 + t * 64 : g * 128 + t * 64 + 64
                    ]

    def terms(key):
        kind, xo, zo = key
        xx, zz = (x + xo) % X, (z + zo) % Z
        if kind[0] == "d":
            first = pl.multiple_of((xx * Z + zz) * BLK, 16)
            lanes = slice(START[kind], START[kind] + WIDTH_OUT[kind])
            return jnp.dot(wt[pl.ds(first, BLK), :], dec[:, lanes], preferred_element_type=F32)
        group = heads[0, (gx - xx + GX) % GX]
        parts = []
        for q in range(START[kind] // 128, (START[kind] + WIDTH_OUT[kind]) // 128):
            first = pl.multiple_of(zz * (4 * BLK) + q * BLK, 16)
            parts.append(jnp.dot(wt[pl.ds(first, BLK), :], group, preferred_element_type=F32))
        return jnp.concatenate(parts, axis=1)

    def scatter_node(key):
        kind, xo, zo = key
        last = (xo, zo) == (0, 0)
        at = ((x + xo) % X) * Z + (z + zo) % Z
        local = terms(key)
        steps = steps_from(key)
        for n, (d, rows, there) in enumerate(steps):
            k = OUT.sends[(key, n)]
            spot = landing[kind].at[OUT.where[(key, n)], pl.ds(rows[0], rows[1])]
            arrive(spot, osend.at[KINDS.index(kind)], orecv.at[k])
        halves = [local[:80], local[80:]]
        for n, (d, rows, there) in enumerate(steps):
            for i, (r0, rn) in enumerate((UPPER, LOWER)):
                if rows[0] <= r0 and r0 + rn <= rows[0] + rows[1]:
                    halves[i] = halves[i] + landing[kind][OUT.where[(key, n)], r0 : r0 + rn].astype(F32)
        for i, (r0, rn) in enumerate((UPPER, LOWER)):
            if last:
                result[kind][r0 : r0 + rn] = halves[i]
            else:
                held[kind][at, r0 : r0 + rn] = halves[i].astype(BF16)
        if not last:
            for d, rows in OUT.pieces[key]:
                k = OUT.fills[(key, rows)]
                remote(
                    held[kind].at[at, pl.ds(rows[0], rows[1])],
                    landing[kind].at[OUT.where[OUT.source[k]], pl.ds(rows[0], rows[1])],
                    osend.at[KINDS.index(kind)],
                    orecv.at[k],
                    near(OPPOSITE[d]),
                ).start()

    def prefill_halves():
        psend[...] = jnp.where(yl == 0, opb[...], opa[...]).astype(BF16)
        start(psend, precv, fsend.at[0], frecv.at[0], partner)

    def prefill_turn():
        arrive(precv, fsend.at[0], frecv.at[0])
        pre_sum = jnp.where(yl == 0, opa[...], opb[...]) + precv[...].astype(F32)
        for q in range(2):
            pfin[q * BLK : q * BLK + BLK] = pre_sum[:, q * 128 : q * 128 + 128].astype(BF16)

        @pl.when(turned)
        def _():
            remote(pfin, pland, fsend.at[2], frecv.at[2], keeper).start()

    def prefill_end():
        @pl.when(turned)
        def _():
            remote(pfin, pland, fsend.at[2], frecv.at[2], keeper).wait()
            prefill_out[...] = pland[...]

        @pl.when(x == gx)
        def _():
            prefill_out[...] = pfin[...]

    def weights():
        w_load.wait()
        w[COLS:, :] = jnp.concatenate([wkv[...].astype(F32), jnp.zeros((8, group), F32)]).astype(BF16)
        mine_load.wait()
        multiply_near(0)

    def turn_weights():
        wo_load.wait()
        for n in range(group // 512):
            wt[pl.ds(512 * n, 512), :] = wov[:, 512 * n : 512 * n + 512].T

    def sibling():
        arrive(tloc.at[1], esend.at[3], erecv.at[3])
        multiply_near(1)
        cache_load.wait()

    middle = {
        "p": (sum_start, queries_start, queries_pass, attend, attended_share, attended_end),
        "d": (
            sum_start,
            queries_start,
            queries_pass,
            attend,
            attended_pass,
            attended_share,
            attended_end,
        ),
    }
    todo = [(IN.times[key], gather_node, key) for key in IN.order]
    todo.append((1.5, lambda _: weights(), None))
    todo.append((9.0, lambda _: sibling(), None))
    ends = {}
    for f in "pd":
        ready = max(IN.times[key] for key in IN.order if key[0][0] == f) + 0.5
        todo += [(ready + after, step, f) for after, step in zip(MIDDLE[f], middle[f])]
        ends[f] = ready + MIDDLE[f][-1]
        if f == "p":
            todo.append((ready + MIDDLE["p"][1] + 0.1, lambda _: turn_weights(), None))
    begin = ends["p"] + 0.1
    out_times = {key: begin + OUT.end - OUT.times[key] for key in OUT.order}
    first_d = min(t for key, t in out_times.items() if key[0][0] == "d")
    shift = max(0.0, ends["d"] + 0.1 - first_d)
    for key in reversed(OUT.order):
        todo.append((out_times[key] + (shift if key[0][0] == "d" else 0.0), scatter_node, key))
    last_p = max(t for key, t in out_times.items() if key[0][0] == "p")
    todo.append((last_p + 0.1, lambda _: prefill_halves(), None))
    todo.append((last_p + 6.0, lambda _: prefill_turn(), None))
    for _, step, what in sorted(todo, key=lambda entry: entry[0]):
        step(what)

    dec_sum = jnp.concatenate([oda[...], odb[...]], axis=1)
    dsend2[:72] = jnp.where(yl == 0, dec_sum[72:], dec_sum[:72]).astype(BF16)
    dsend2[72:] = jnp.zeros((8, TOK), BF16)
    start(dsend2, drecv2, fsend.at[1], frecv.at[1], partner)
    prefill_end()
    arrive(drecv2, fsend.at[1], frecv.at[1])
    dec_sum = jnp.where(yl == 0, dec_sum[:72], dec_sum[72:]) + drecv2[:72].astype(F32)
    for t in range(2):
        decode_out[t] = dec_sum[:, t * 256 : t * 256 + 256].astype(BF16)

    for n, kind in enumerate(KINDS_IN):
        sent = got[kind].at[pl.ds(0, 2 if kind[0] == "p" else X * Z - 1)]
        remote(sent, sent, send.at[n], recv.at[0], partner).wait_send()
    for n, kind in enumerate(KINDS):
        sent = held[kind].at[pl.ds(0, X * Z - 1)]
        remote(sent, sent, osend.at[n], orecv.at[0], partner).wait_send()
    for o in (0, 1, 4, 5):
        sent = got["p0"].at[0]
        remote(sent, sent, esend.at[o], erecv.at[o], partner).wait_send()
    for c in pending:
        c.wait_send()


def run(cache_length, prefill_length, dtok, wkv, ptok, wq, wo, cache):
    vmem = pl.BlockSpec(memory_space=pltpu.VMEM)
    hbm = pl.BlockSpec(memory_space=pl.ANY)
    dma = pltpu.SemaphoreType.DMA
    group = wq.shape[1]

    def scratch(*shape, dtype=BF16):
        return pltpu.VMEM(shape, dtype)

    return pl.pallas_call(
        kernel,
        out_shape=(
            jax.ShapeDtypeStruct((2 * BLK, PLEN), BF16),
            jax.ShapeDtypeStruct((2, 72, 256), BF16),
        ),
        in_specs=[pl.BlockSpec(memory_space=pltpu.SMEM)] * 2 + [vmem, vmem, hbm, hbm, hbm, hbm],
        out_specs=(vmem, vmem),
        scratch_shapes=[
            scratch(X, PLEN, SPAN),
            scratch(X, PLEN, SPAN),
            scratch(X * Z, BLK, WIDTH_IN["da"]),
            scratch(X * Z, BLK, WIDTH_IN["db"]),
            scratch(ROWS1, group),
            scratch(COLS, group),
            scratch(group, COLS),
            scratch(*cache.shape),
            scratch(2, PLEN, group),
            scratch(BLK, WIDTH_IN["da"]),
            scratch(BLK, WIDTH_IN["db"]),
            scratch(80, TOK),
            scratch(80, TOK),
            scratch(ROWS1, TOK, dtype=F32),
            scratch(ROWS1, TOK, dtype=F32),
            scratch(2, GX, ROWS1, 128),
            scratch(GX - 1, ROWS1, 128),
            scratch(GX - 1, ROWS1, 128),
            scratch(128, 256, dtype=F32),
            scratch(128, 256, dtype=F32),
            scratch(128, 256, dtype=F32),
            scratch(2, X, Z, YL, 2, 256, dtype=F32),
            scratch(2, X, Z, YL, 2, 256, dtype=F32),
            scratch(2, X, Z, YL, 2, 256, dtype=F32),
            scratch(QUAD, 32, 256, dtype=F32),
            scratch(QUAD, 32, 256, dtype=F32),
            scratch(96, 256, dtype=F32),
            scratch(KVC, PLEN, dtype=F32),
            scratch(Z, KVC, PLEN, dtype=F32),
            scratch(X, Z, YL, KVC, PLEN, dtype=F32),
            scratch(2, COLS, 128),
            scratch(2, GX, COLS, 128),
            scratch(COLS, TOK),
            scratch(COLS, TOK),
        ]
        + [scratch(X * Z, BLK, WIDTH_OUT[k]) for k in KINDS]
        + [scratch(OUT.slots[k], BLK, WIDTH_OUT[k]) for k in KINDS]
        + [scratch(BLK, WIDTH_OUT[k], dtype=F32) for k in KINDS]
        + [
            scratch(BLK, 256),
            scratch(BLK, 256),
            scratch(80, TOK),
            scratch(80, TOK),
            scratch(2 * BLK, PLEN),
            scratch(2 * BLK, PLEN),
            dma((4,)),
            dma((6,)),
            dma((6,)),
            dma((4,)),
            dma((len(IN.sends),)),
            dma((2, GX)),
            dma((2, GX)),
            dma((2, 16)),
            dma((2, 16)),
            dma((16,)),
            dma((16,)),
            dma((2, QUAD)),
            dma((2, QUAD)),
            dma((2, GX)),
            dma((2, GX)),
            dma((4,)),
            dma((len(OUT.sends),)),
            dma((3,)),
            dma((3,)),
        ],
        compiler_params=pltpu.CompilerParams(
            collective_id=0, has_side_effects=True, vmem_limit_bytes=56 * 2**20
        ),
        name="attention_block",
    )(cache_length, prefill_length, dtok, wkv, ptok, wq, wo, cache)


def body(
    prefill_tokens,
    prefill_lengths,
    decode_tokens,
    cache_lengths,
    cache_keyvals,
    query_weight,
    keyval_weight,
    out_weight,
):
    prefill_out, decode_out = run(
        cache_lengths,
        prefill_lengths,
        decode_tokens.transpose(0, 2, 1),
        keyval_weight.T,
        prefill_tokens,
        query_weight.T,
        out_weight,
        cache_keyvals[0],
    )
    return (prefill_out.T, decode_out.transpose(0, 2, 1))


def solution(mesh):
    in_specs = (
        P("gx", None),
        P("gx"),
        P(None, None, ("gx", "yz")),
        P(("gx", "yz")),
        P(("gx", "yz"), None, None),
        P("gx", "yz"),
        P("gx", "yz"),
        P("yz", "gx"),
    )
    out_specs = (P("gx", "yz"), P(None, None, ("gx", "yz")))
    return jax.shard_map(body, mesh=mesh, in_specs=in_specs, out_specs=out_specs, check_vma=False)
```

```python
import heapq

import jax
import jax.numpy as jnp
from jax import lax
from jax.experimental import pallas as pl
from jax.experimental.pallas import tpu as pltpu
from jax.sharding import PartitionSpec as P

HEADS = 48
HD = 256
PLEN = 128
GX, X, Z, YL = 4, 4, 8, 2
BLK = 144
TOK = 512
WIDTH_IN = {"p0": 1024, "p1": 1024, "da": 128, "db": 384}
WIDTH_OUT = {"pa": 256, "pb": 256, "da": 384, "db": 128}
START_IN = {"da": 0, "db": 128}
START = {"pa": 0, "pb": 256, "da": 0, "db": 384}
KINDS = tuple(START)
KINDS_IN = tuple(WIDTH_IN)
FAR = {"p0": 21.0, "p1": 27.0}
SPAN = Z * BLK
COLS = 192
KVC = 8
ROWS1 = 208
MESH = pl.DeviceIdType.MESH
F32 = jnp.float32
BF16 = jnp.bfloat16
FULL, UPPER, LOWER = (0, 144), (0, 80), (80, 64)
OPPOSITE = {"x+": "x-", "x-": "x+", "z+": "z-", "z-": "z+"}


def steps_from(key):
    kind, xo, zo = key
    out = []
    if kind in ("p0", "p1"):
        if xo == 0:
            out.append(("x+", FULL, (kind, -1, 0)))
            out.append(("x-", FULL, (kind, 1, 0)))
    elif kind[1] == "a":
        if xo == 0:
            if -3 < zo <= 0:
                out.append(("z+", FULL, (kind, 0, zo - 1)))
            if zo == -3:
                out.append(("z+", UPPER, (kind, 0, 4)))
            if 0 <= zo < 3:
                out.append(("z-", FULL, (kind, 0, zo + 1)))
            if zo == 3:
                out.append(("z-", LOWER, (kind, 0, 4)))
            out.append(("x+", FULL, (kind, -1, zo)))
            out.append(("x-", FULL, (kind, 1, zo)))
        elif xo == -1 and zo % 2 == 0:
            out.append(("x+", FULL, (kind, 2, zo)))
        elif xo == 1 and zo % 2 == 1:
            out.append(("x-", FULL, (kind, 2, zo)))
    else:
        if zo == 0:
            if xo == 0:
                out.append(("x+", FULL, (kind, -1, 0)))
                out.append(("x-", FULL, (kind, 1, 0)))
            elif xo == -1:
                out.append(("x+", UPPER, (kind, 2, 0)))
            elif xo == 1:
                out.append(("x-", LOWER, (kind, 2, 0)))
        if zo <= 0 and (zo > -3 or xo in (0, 2)):
            out.append(("z+", FULL, (kind, xo, zo - 1 if zo > -3 else 4)))
        if 0 <= zo <= 3 and (zo < 3 or xo in (-1, 1)):
            out.append(("z-", FULL, (kind, xo, zo + 1)))
    return out


class Plan:
    def __init__(self, releases, width):
        free = dict.fromkeys(OPPOSITE, 0.0)
        events, self.order, self.times, self.pieces = [], [], {}, {}
        self.sends, self.fills, self.source, self.where = {}, {}, {}, {}
        self.slots = dict.fromkeys(releases, 0)

        def leave(key, now):
            self.order.append(key)
            self.times[key] = now
            for n, (d, rows, there) in enumerate(steps_from(key)):
                free[d] = max(free[d], now) + width[key[0]] * rows[1] * 4e-5
                k = len(self.sends)
                self.sends[(key, n)] = k
                self.fills[(there, rows)] = k
                self.source[k] = (key, n)
                self.where[(key, n)] = self.slots[key[0]]
                self.slots[key[0]] += 1
                heapq.heappush(events, (free[d] + 3.0, k, there, (d, rows)))

        for n, kind in enumerate(releases):
            heapq.heappush(events, (releases[kind], n - len(releases), (kind, 0, 0), None))
            if kind in FAR:
                heapq.heappush(events, (FAR[kind], n - len(releases), (kind, 2, 0), None))
        while events:
            now, _, key, piece = heapq.heappop(events)
            if piece is not None:
                self.pieces.setdefault(key, []).append(piece)
            if piece is None or sum(p[1][1] for p in self.pieces[key]) == BLK:
                leave(key, now)
        self.end = max(self.times.values())


IN = Plan({"db": 0.0, "da": 0.0, "p0": 9.0, "p1": 15.0}, WIDTH_IN)
OUT = Plan({"db": 0.0, "da": 0.0, "pb": 28.0, "pa": 28.0}, WIDTH_OUT)
MIDDLE = {"p": (0.0, 4.5, 8.5, 13.0, 18.0, 22.0), "d": (0.0, 4.5, 10.5, 15.5, 23.5, 28.5, 33.0)}
QUAD = 4


def place():
    gx = lax.axis_index("gx")
    yz = lax.axis_index("yz")
    return gx, yz // (Z * YL), (yz // YL) % Z, yz % YL


def flat(x, z, yl):
    return x * (Z * YL) + z * YL + yl


def copy_rows(move):
    def four(g, carry):
        for j in range(QUAD):
            move(g // 4, (g % 4) * 2 + j // 2, j % 2, g, j)
        return carry

    lax.fori_loop(0, 16, four, 0)


def kernel(
    cache_length, prefill_length, dtok, wkv, ptok, wq, wo, cache_hbm,
    prefill_out, decode_out,
    gp0, gp1, gda, gdb, w, wov, wt, cache, tloc, xda, xdb, dsend, drecv,
    accp, accd, give, takep, taked, tok, tokp, backp, s1, r1, r2, qj, qjp, qh,
    kvown, k1, k2, att, heads, dec, dec2, ppa, ppb, pda, pdb, lpa, lpb, lda, ldb,
    opa, opb, oda, odb, psend, precv, dsend2, drecv2, pfin, pland,
    local, esend, erecv, send, recv, gsend, grecv, asend, arecv, ksend, krecv, qsend, qrecv, hsend, hrecv,
    osend, orecv, fsend, frecv,
):
    gx, x, z, yl = place()
    yz = lax.axis_index("yz")
    core, y_hi = gx % 2, gx // 2
    own = {"da": xda, "db": xdb}
    got = dict(zip(KINDS_IN, (gp0, gp1, gda, gdb)))
    result = dict(zip(KINDS, (opa, opb, oda, odb)))
    held = dict(zip(KINDS, (ppa, ppb, pda, pdb)))
    landing = dict(zip(KINDS, (lpa, lpb, lda, ldb)))
    acc = {"p": accp, "d": accd}
    take = {"p": takep, "d": taked}
    pending = []

    def near(d):
        dx = {"x+": 1, "x-": X - 1}.get(d, 0)
        dz = {"z+": 1, "z-": Z - 1}.get(d, 0)
        return (gx, flat((x + dx) % X, (z + dz) % Z, yl))

    g_peers = [((gx + s) % GX, yz) for s in range(1, GX)]
    there = 1 - y_hi
    across = [(2 * there + o, flat(x, z, 1 - yl)) for o in range(2)]
    z_peers = [(gx, flat(x, (z + s) % Z, yl)) for s in range(1, Z)]
    xy_peers = [(gx, flat((x + e // 2) % X, z, (yl + e) % YL)) for e in range(1, X * YL)]
    quad_first = (yz // QUAD) * QUAD
    place_in_quad = yz % QUAD
    quad_peers = [(gx, quad_first + (place_in_quad + s) % QUAD) for s in range(1, QUAD)]
    diagonal = (gx, flat(x, z + 1 - 2 * (z % 2), 1 - yl))

    def remote(src, dst, ssem, rsem, device):
        return pltpu.make_async_remote_copy(
            src_ref=src, dst_ref=dst, send_sem=ssem, recv_sem=rsem, device_id=device, device_id_type=MESH
        )

    def start(src, dst, ssem, rsem, device):
        c = remote(src, dst, ssem, rsem, device)
        c.start()
        pending.append(c)

    def arrive(dst, ssem, rsem):
        remote(dst, dst, ssem, rsem, near("x+")).wait_recv()

    barrier = pltpu.get_barrier_semaphore()
    peers = z_peers + xy_peers + [diagonal] + g_peers + across
    keeper = (x, flat(gx, z, yl))
    turned = x != gx

    for peer in peers:
        pl.semaphore_signal(barrier, inc=1, device_id=peer, device_id_type=MESH)

    @pl.when(turned)
    def _():
        pl.semaphore_signal(barrier, inc=1, device_id=keeper, device_id_type=MESH)

    group = wq.shape[1]
    loads = []

    def load(src, dst):
        c = pltpu.make_async_copy(src, dst, local.at[len(loads)])
        c.start()
        loads.append(c)
        return c

    dsend[:72, :256] = dtok[0]
    dsend[:72, 256:] = dtok[1]
    dsend[72:, :] = jnp.zeros((8, TOK), BF16)
    pl.semaphore_wait(barrier, len(peers) + turned.astype(jnp.int32))

    partner = (gx, flat(x, z, 1 - yl))
    start(dsend, drecv, esend.at[2], erecv.at[2], partner)
    for c in range(2):

        @pl.when(core == c)
        def _(c=c):
            for far in range(2):
                xx = (x + 2 * far) % X
                for o in range(2):
                    lane = pl.multiple_of((2 * there + o) * group + xx * SPAN, 128)
                    remote(
                        ptok.at[:, pl.ds(lane, SPAN)],
                        got["p%d" % c].at[xx],
                        esend.at[4 * far + o],
                        erecv.at[4 * far + c],
                        across[o],
                    ).start()

    w_load = load(wq, w.at[pl.ds(0, COLS)])
    mine_load = load(ptok.at[:, pl.ds(pl.multiple_of(gx * group, 128), group)], tloc.at[0])
    sibling_gx = gx + 1 - 2 * core
    start(
        ptok.at[:, pl.ds(pl.multiple_of(sibling_gx * group, 128), group)],
        tloc.at[1],
        esend.at[3],
        erecv.at[3],
        (sibling_gx, yz),
    )
    wo_load = load(wo, wov)
    cache_load = load(cache_hbm, cache)
    for ref in (tok, tokp, qj):
        ref[...] = jnp.zeros(ref.shape, F32)

    def slot(key, rows):
        kind, xo, zo = key
        if kind[0] == "p":
            return got[kind].at[(x + xo) % X]
        return got[kind].at[((x + xo) % X) * Z + (z + zo) % Z, pl.ds(rows[0], rows[1])]

    seen = {}

    def multiply(kind, xo):
        xx = (x + xo) % X
        part_of_w = w[:, pl.ds(pl.multiple_of(xx * SPAN, 128), SPAN)]
        if kind[0] == "p":
            part = lax.dot_general(
                part_of_w, got[kind][xx], (((1,), (1,)), ((), ())), preferred_element_type=F32
            )
            lanes = pl.ds(pl.multiple_of((2 * there + int(kind[1])) * 128, 128), 128)
        else:
            block = got[kind][pl.ds(xx * Z, Z)].reshape(SPAN, WIDTH_IN[kind])
            part = jnp.dot(part_of_w, block, preferred_element_type=F32)
            lanes = slice(START_IN[kind], START_IN[kind] + WIDTH_IN[kind])
        if kind in seen:
            acc[kind[0]][:, lanes] += part
        else:
            acc[kind[0]][:, lanes] = part
            seen[kind] = True

    def multiply_near(n):
        lanes = pl.ds(pl.multiple_of((gx if n == 0 else sibling_gx) * 128, 128), 128)
        acc["p"][:, lanes] = lax.dot_general(
            w[...], tloc[n], (((1,), (1,)), ((), ())), preferred_element_type=F32
        )

    def gather_node(key):
        kind, xo, zo = key
        mine = (xo, zo) == (0, 0)
        if xo == 2 and kind in FAR:
            c = 4 + int(kind[1])
            arrive(slot(key, FULL), esend.at[c], erecv.at[c])
        elif not mine:
            for _, rows in IN.pieces[key]:
                k = IN.fills[(key, rows)]
                arrive(slot(key, rows), send.at[KINDS_IN.index(kind)], recv.at[k])
        elif kind[0] == "p":
            c = int(kind[1])
            arrive(slot(key, FULL), esend.at[c], erecv.at[c])
        elif kind == "db":
            arrive(drecv, esend.at[2], erecv.at[2])
            one, two = dsend[:72].astype(F32), drecv[:72].astype(F32)
            both = jnp.where(
                yl == 0, jnp.concatenate([one, two], axis=0), jnp.concatenate([two, one], axis=0)
            ).astype(BF16)
            xda[...] = both[:, : WIDTH_IN["da"]]
            xdb[...] = both[:, WIDTH_IN["da"] :]
        for n, (d, rows, there) in enumerate(steps_from(key)):
            k = IN.sends[(key, n)]
            remote(
                own[kind] if mine and kind in own else slot(key, rows),
                slot(key, rows),
                send.at[KINDS_IN.index(kind)],
                recv.at[k],
                near(d),
            ).start()
        if mine and kind in own:
            got[kind][x * Z + z] = own[kind][...]
        seen[(kind, xo)] = seen.get((kind, xo), 0) + 1
        if seen[(kind, xo)] == (1 if kind[0] == "p" else Z):
            multiply(kind, xo)

    def sum_start(f):
        if f == "d":
            rows = accd[...]
            for g in range(GX):
                accd[:, g * 128 : g * 128 + 64] = rows[:, g * 64 : g * 64 + 64]
                accd[:, g * 128 + 64 : g * 128 + 128] = rows[:, 256 + g * 64 : 320 + g * 64]
        for g in range(GX):
            give[n_of[f], g] = acc[f][:, g * 128 : g * 128 + 128].astype(BF16)
        for s in range(1, GX):
            start(
                give.at[n_of[f], (gx + s) % GX],
                take[f].at[s - 1],
                gsend.at[n_of[f], s],
                grecv.at[n_of[f], s],
                g_peers[s - 1],
            )

    n_of = {"p": 0, "d": 1}

    def exchange_z(i):
        for s in range(1, Z):
            start(
                s1.at[i, :, (z + s) % Z],
                r1.at[i, :, z],
                asend.at[i, s],
                arecv.at[i, s],
                z_peers[s - 1],
            )
        r1[i, :, z] = s1[i, :, z]

    def exchange_xy(i):
        for s in range(1, Z):
            arrive(r1.at[i, :, (z + Z - s) % Z], asend.at[i, s], arecv.at[i, s])
        for e in range(1, X * YL):
            start(
                r1.at[i, (x + e // 2) % X, :, (yl + e) % YL],
                r2.at[i, x, :, yl],
                asend.at[i, Z + e],
                arecv.at[i, Z + e],
                xy_peers[e - 1],
            )
        r2[i, x, :, yl] = r1[i, x, :, yl]

    def exchange_end(i):
        for e in range(1, X * YL):
            arrive(
                r2.at[i, (x + X - e // 2) % X, :, (yl + e) % YL], asend.at[i, Z + e], arecv.at[i, Z + e]
            )

    def queries_start(f):
        for s in range(1, GX):
            arrive(take[f].at[s - 1], gsend.at[n_of[f], s], grecv.at[n_of[f], s])
        lane = pl.multiple_of(gx * 128, 128)
        total = acc[f][:, pl.ds(lane, 128)]
        for s in range(1, GX):
            total = total + take[f][s - 1].astype(F32)
        total = total.astype(BF16).astype(F32)
        if f == "p":
            tokp[:, :ROWS1] = total.T
            for s in range(1, QUAD):
                to = (place_in_quad + s) % QUAD
                start(
                    tokp.at[pl.ds(pl.multiple_of(32 * to, 32), 32)],
                    qjp.at[place_in_quad],
                    qsend.at[0, s],
                    qrecv.at[0, s],
                    quad_peers[s - 1],
                )
            qjp[place_in_quad] = tokp[pl.ds(pl.multiple_of(32 * place_in_quad, 32), 32), :]
            kvown[...] = total[COLS : COLS + KVC]
            for s in range(1, Z):
                start(kvown, k1.at[z], ksend.at[s], krecv.at[s], z_peers[s - 1])
            k1[z] = kvown[...]
            return
        tok[:, :ROWS1] = total.T

        def pack(xx, zz, yy, g, j):
            r = flat(xx, zz, yy)
            for t in range(2):
                s1[0, xx, zz, yy, pl.ds(t, 1), :] = tok[pl.ds(t * 64 + r, 1), :]

        copy_rows(pack)
        exchange_z(0)

    def queries_pass(f):
        if f == "d":
            exchange_xy(0)
            return
        for s in range(1, Z):
            arrive(k1.at[(z + Z - s) % Z], ksend.at[s], krecv.at[s])
        for e in range(1, X * YL):
            start(k1, k2.at[x, :, yl], ksend.at[Z + e], krecv.at[Z + e], xy_peers[e - 1])
        k2[x, :, yl] = k1[...]

    nt = (((1,), (1,)), ((), ()))
    scale = HD ** (-0.5)

    def attend(f):
        if f == "p":
            for s in range(1, QUAD):
                arrive(
                    qjp.at[(place_in_quad + QUAD - s) % QUAD], qsend.at[0, s], qrecv.at[0, s]
                )
            piece = qjp
        else:
            exchange_end(0)

            def unpack(xx, zz, yy, g, j):
                for t in range(2):
                    qj[j, pl.ds(t * 16 + g, 1), :] = r2[0, xx, zz, yy, pl.ds(t, 1), :]

            copy_rows(unpack)
            piece = qj
        qh[0:32, :192] = piece[0, :, :192]
        qh[0:32, 192:] = piece[1, :, :64]
        qh[32:64, :128] = piece[1, :, 64:192]
        qh[32:64, 128:] = piece[2, :, :128]
        qh[64:96, :64] = piece[2, :, 128:192]
        qh[64:96, 64:] = piece[3, :, :192]
        q32 = qh[...]
        q = q32.astype(BF16)
        if f == "p":
            for e in range(1, X * YL):
                arrive(k2.at[(x + X - e // 2) % X, :, (yl + e) % YL], ksend.at[Z + e], krecv.at[Z + e])
            kvt = k2[...].reshape(2 * HD, PLEN).astype(BF16)
            s = jnp.dot(q, kvt[:HD], preferred_element_type=F32) * scale
            query = 32 * place_in_quad + lax.broadcasted_iota(jnp.int32, s.shape, 0) % 32
            pos = lax.broadcasted_iota(jnp.int32, s.shape, 1)
            s = jnp.where((pos <= query) & (pos < prefill_length[0]), s, -1e30)
            e = jnp.exp(s - jnp.max(s, axis=1, keepdims=True))
            probs = (e / jnp.sum(e, axis=1, keepdims=True)).astype(BF16)
            out = lax.dot_general(probs, kvt[HD:], nt, preferred_element_type=F32)
        else:
            row = lax.broadcasted_iota(jnp.int32, (KVC, 2 * HD), 0)
            lane = lax.broadcasted_iota(jnp.int32, (KVC, 2 * HD), 1)
            spread = (lane % KVC == row).astype(BF16)
            group = lax.broadcasted_iota(jnp.int32, (32, 2 * HD), 0) % 16
            holder = lax.broadcasted_iota(jnp.int32, (32, 2 * HD), 1) // KVC
            new = jnp.zeros((32, 2 * HD), F32)
            for j in range(4):
                wide = jnp.dot(
                    qj[j, :, COLS : COLS + KVC].astype(BF16), spread, preferred_element_type=F32
                )
                new = new + jnp.where(holder == 4 * group + j, wide, 0.0)
            new0 = jnp.sum(new[:16], axis=0, keepdims=True)
            new1 = jnp.sum(new[16:], axis=0, keepdims=True)
            s = lax.dot_general(q, cache[:, :HD], nt, preferred_element_type=F32) * scale
            pos = lax.broadcasted_iota(jnp.int32, s.shape, 1)
            s = jnp.where(pos < cache_length[0], s, -1e30)
            f0 = jnp.sum(q32 * new0[:, :HD], axis=1, keepdims=True) * scale
            f1 = jnp.sum(q32 * new1[:, :HD], axis=1, keepdims=True) * scale
            step = (lax.broadcasted_iota(jnp.int32, f1.shape, 0) // 16) % 2
            f1 = jnp.where(step == 1, f1, -1e30)
            peak = jnp.maximum(jnp.max(s, axis=1, keepdims=True), jnp.maximum(f0, f1))
            es, e0, e1 = jnp.exp(s - peak), jnp.exp(f0 - peak), jnp.exp(f1 - peak)
            total = jnp.sum(es, axis=1, keepdims=True) + e0 + e1
            out = jnp.dot((es / total).astype(BF16), cache[:, HD:], preferred_element_type=F32)
            out = out + (e0 / total).astype(BF16).astype(F32) * new0[:, HD:]
            out = out + (e1 / total).astype(BF16).astype(F32) * new1[:, HD:]
        qh[...] = out.astype(BF16).astype(F32)
        piece[0, :, :192] = qh[0:32, :192]
        piece[1, :, :64] = qh[0:32, 192:]
        piece[1, :, 64:192] = qh[32:64, :128]
        piece[2, :, :128] = qh[32:64, 128:]
        piece[2, :, 128:192] = qh[64:96, :64]
        piece[3, :, :192] = qh[64:96, 64:]

        if f == "p":
            for s in range(1, QUAD):
                start(
                    piece.at[(place_in_quad + s) % QUAD],
                    backp.at[pl.ds(pl.multiple_of(32 * place_in_quad, 32), 32)],
                    qsend.at[1, s],
                    qrecv.at[1, s],
                    quad_peers[s - 1],
                )
            backp[pl.ds(pl.multiple_of(32 * place_in_quad, 32), 32), :] = piece[place_in_quad]
            return

        def pack(xx, zz, yy, g, j):
            for t in range(2):
                s1[1, xx, zz, yy, pl.ds(t, 1), :] = qj[j, pl.ds(t * 16 + g, 1), :]

        copy_rows(pack)
        exchange_z(1)

    def attended_pass(f):
        exchange_xy(1)

    def attended_share(f):
        n = n_of[f]
        if f == "p":
            for s in range(1, QUAD):
                first = 32 * ((place_in_quad + QUAD - s) % QUAD)
                arrive(
                    backp.at[pl.ds(pl.multiple_of(first, 32), 32)], qsend.at[1, s], qrecv.at[1, s]
                )
            att[n] = backp[...].T[:COLS].astype(BF16)
        else:
            exchange_end(1)

            def unpack(xx, zz, yy, g, j):
                r = flat(xx, zz, yy)
                for t in range(2):
                    tok[pl.ds(t * 64 + r, 1), :] = r2[1, xx, zz, yy, pl.ds(t, 1), :]

            copy_rows(unpack)
            att[n] = tok[...].T[:COLS].astype(BF16)
        for s in range(1, GX):
            start(att.at[n], heads.at[n, s], hsend.at[n, s], hrecv.at[n, s], g_peers[s - 1])
        heads[n, 0] = att[n]

    def attended_end(f):
        n = n_of[f]
        for s in range(1, GX):
            arrive(heads.at[n, s], hsend.at[n, s], hrecv.at[n, s])
        if f == "d":
            for s in range(GX):
                lane = pl.multiple_of(((gx - s + GX) % GX) * 128, 128)
                dec2[:, pl.ds(lane, 128)] = heads[n, s]
            for g in range(GX):
                for t in range(2):
                    dec[:, t * 256 + g * 64 : t * 256 + g * 64 + 64] = dec2[
                        :, g * 128 + t * 64 : g * 128 + t * 64 + 64
                    ]

    def terms(key):
        kind, xo, zo = key
        xx, zz = (x + xo) % X, (z + zo) % Z
        if kind[0] == "d":
            first = pl.multiple_of((xx * Z + zz) * BLK, 16)
            lanes = slice(START[kind], START[kind] + WIDTH_OUT[kind])
            return jnp.dot(wt[pl.ds(first, BLK), :], dec[:, lanes], preferred_element_type=F32)
        group = heads[0, (gx - xx + GX) % GX]
        parts = []
        for q in range(START[kind] // 128, (START[kind] + WIDTH_OUT[kind]) // 128):
            first = pl.multiple_of(zz * (4 * BLK) + q * BLK, 16)
            parts.append(jnp.dot(wt[pl.ds(first, BLK), :], group, preferred_element_type=F32))
        return jnp.concatenate(parts, axis=1)

    def scatter_node(key):
        kind, xo, zo = key
        last = (xo, zo) == (0, 0)
        at = ((x + xo) % X) * Z + (z + zo) % Z
        local = terms(key)
        steps = steps_from(key)
        for n, (d, rows, there) in enumerate(steps):
            k = OUT.sends[(key, n)]
            spot = landing[kind].at[OUT.where[(key, n)], pl.ds(rows[0], rows[1])]
            arrive(spot, osend.at[KINDS.index(kind)], orecv.at[k])
        halves = [local[:80], local[80:]]
        for n, (d, rows, there) in enumerate(steps):
            for i, (r0, rn) in enumerate((UPPER, LOWER)):
                if rows[0] <= r0 and r0 + rn <= rows[0] + rows[1]:
                    halves[i] = halves[i] + landing[kind][OUT.where[(key, n)], r0 : r0 + rn].astype(F32)
        for i, (r0, rn) in enumerate((UPPER, LOWER)):
            if last:
                result[kind][r0 : r0 + rn] = halves[i]
            else:
                held[kind][at, r0 : r0 + rn] = halves[i].astype(BF16)
        if not last:
            for d, rows in OUT.pieces[key]:
                k = OUT.fills[(key, rows)]
                remote(
                    held[kind].at[at, pl.ds(rows[0], rows[1])],
                    landing[kind].at[OUT.where[OUT.source[k]], pl.ds(rows[0], rows[1])],
                    osend.at[KINDS.index(kind)],
                    orecv.at[k],
                    near(OPPOSITE[d]),
                ).start()

    def prefill_halves():
        psend[...] = jnp.where(yl == 0, opb[...], opa[...]).astype(BF16)
        start(psend, precv, fsend.at[0], frecv.at[0], partner)

    def prefill_turn():
        arrive(precv, fsend.at[0], frecv.at[0])
        pre_sum = jnp.where(yl == 0, opa[...], opb[...]) + precv[...].astype(F32)
        for q in range(2):
            pfin[q * BLK : q * BLK + BLK] = pre_sum[:, q * 128 : q * 128 + 128].astype(BF16)

        @pl.when(turned)
        def _():
            remote(pfin, pland, fsend.at[2], frecv.at[2], keeper).start()

    def prefill_end():
        @pl.when(turned)
        def _():
            remote(pfin, pland, fsend.at[2], frecv.at[2], keeper).wait()
            prefill_out[...] = pland[...]

        @pl.when(x == gx)
        def _():
            prefill_out[...] = pfin[...]

    def weights():
        w_load.wait()
        w[COLS:, :] = jnp.concatenate([wkv[...].astype(F32), jnp.zeros((8, group), F32)]).astype(BF16)
        mine_load.wait()
        multiply_near(0)

    def turn_weights():
        wo_load.wait()
        for n in range(group // 512):
            wt[pl.ds(512 * n, 512), :] = wov[:, 512 * n : 512 * n + 512].T

    def sibling():
        arrive(tloc.at[1], esend.at[3], erecv.at[3])
        multiply_near(1)
        cache_load.wait()

    middle = {
        "p": (sum_start, queries_start, queries_pass, attend, attended_share, attended_end),
        "d": (
            sum_start,
            queries_start,
            queries_pass,
            attend,
            attended_pass,
            attended_share,
            attended_end,
        ),
    }
    todo = [(IN.times[key], gather_node, key) for key in IN.order]
    todo.append((1.5, lambda _: weights(), None))
    todo.append((9.0, lambda _: sibling(), None))
    ends = {}
    for f in "pd":
        ready = max(IN.times[key] for key in IN.order if key[0][0] == f) + 0.5
        todo += [(ready + after, step, f) for after, step in zip(MIDDLE[f], middle[f])]
        ends[f] = ready + MIDDLE[f][-1]
        if f == "p":
            todo.append((ready + MIDDLE["p"][1] + 0.1, lambda _: turn_weights(), None))
    begin = ends["p"] + 0.1
    out_times = {key: begin + OUT.end - OUT.times[key] for key in OUT.order}
    first_d = min(t for key, t in out_times.items() if key[0][0] == "d")
    shift = max(0.0, ends["d"] + 0.1 - first_d)
    for key in reversed(OUT.order):
        todo.append((out_times[key] + (shift if key[0][0] == "d" else 0.0), scatter_node, key))
    last_p = max(t for key, t in out_times.items() if key[0][0] == "p")
    todo.append((last_p + 0.1, lambda _: prefill_halves(), None))
    todo.append((last_p + 6.0, lambda _: prefill_turn(), None))
    for _, step, what in sorted(todo, key=lambda entry: entry[0]):
        step(what)

    dec_sum = jnp.concatenate([oda[...], odb[...]], axis=1)
    dsend2[:72] = jnp.where(yl == 0, dec_sum[72:], dec_sum[:72]).astype(BF16)
    dsend2[72:] = jnp.zeros((8, TOK), BF16)
    start(dsend2, drecv2, fsend.at[1], frecv.at[1], partner)
    prefill_end()
    arrive(drecv2, fsend.at[1], frecv.at[1])
    dec_sum = jnp.where(yl == 0, dec_sum[:72], dec_sum[72:]) + drecv2[:72].astype(F32)
    for t in range(2):
        decode_out[t] = dec_sum[:, t * 256 : t * 256 + 256].astype(BF16)

    for n, kind in enumerate(KINDS_IN):
        sent = got[kind].at[pl.ds(0, 2 if kind[0] == "p" else X * Z - 1)]
        remote(sent, sent, send.at[n], recv.at[0], partner).wait_send()
    for n, kind in enumerate(KINDS):
        sent = held[kind].at[pl.ds(0, X * Z - 1)]
        remote(sent, sent, osend.at[n], orecv.at[0], partner).wait_send()
    for o in (0, 1, 4, 5):
        sent = got["p0"].at[0]
        remote(sent, sent, esend.at[o], erecv.at[o], partner).wait_send()
    for c in pending:
        c.wait_send()


def run(cache_length, prefill_length, dtok, wkv, ptok, wq, wo, cache):
    vmem = pl.BlockSpec(memory_space=pltpu.VMEM)
    hbm = pl.BlockSpec(memory_space=pl.ANY)
    dma = pltpu.SemaphoreType.DMA
    group = wq.shape[1]

    def scratch(*shape, dtype=BF16):
        return pltpu.VMEM(shape, dtype)

    return pl.pallas_call(
        kernel,
        out_shape=(
            jax.ShapeDtypeStruct((2 * BLK, PLEN), BF16),
            jax.ShapeDtypeStruct((2, 72, 256), BF16),
        ),
        in_specs=[pl.BlockSpec(memory_space=pltpu.SMEM)] * 2 + [vmem, vmem, hbm, hbm, hbm, hbm],
        out_specs=(vmem, vmem),
        scratch_shapes=[
            scratch(X, PLEN, SPAN),
            scratch(X, PLEN, SPAN),
            scratch(X * Z, BLK, WIDTH_IN["da"]),
            scratch(X * Z, BLK, WIDTH_IN["db"]),
            scratch(ROWS1, group),
            scratch(COLS, group),
            scratch(group, COLS),
            scratch(*cache.shape),
            scratch(2, PLEN, group),
            scratch(BLK, WIDTH_IN["da"]),
            scratch(BLK, WIDTH_IN["db"]),
            scratch(80, TOK),
            scratch(80, TOK),
            scratch(ROWS1, TOK, dtype=F32),
            scratch(ROWS1, TOK, dtype=F32),
            scratch(2, GX, ROWS1, 128),
            scratch(GX - 1, ROWS1, 128),
            scratch(GX - 1, ROWS1, 128),
            scratch(128, 256, dtype=F32),
            scratch(128, 256, dtype=F32),
            scratch(128, 256, dtype=F32),
            scratch(2, X, Z, YL, 2, 256, dtype=F32),
            scratch(2, X, Z, YL, 2, 256, dtype=F32),
            scratch(2, X, Z, YL, 2, 256, dtype=F32),
            scratch(QUAD, 32, 256, dtype=F32),
            scratch(QUAD, 32, 256, dtype=F32),
            scratch(96, 256, dtype=F32),
            scratch(KVC, PLEN, dtype=F32),
            scratch(Z, KVC, PLEN, dtype=F32),
            scratch(X, Z, YL, KVC, PLEN, dtype=F32),
            scratch(2, COLS, 128),
            scratch(2, GX, COLS, 128),
            scratch(COLS, TOK),
            scratch(COLS, TOK),
        ]
        + [scratch(X * Z, BLK, WIDTH_OUT[k]) for k in KINDS]
        + [scratch(OUT.slots[k], BLK, WIDTH_OUT[k]) for k in KINDS]
        + [scratch(BLK, WIDTH_OUT[k], dtype=F32) for k in KINDS]
        + [
            scratch(BLK, 256),
            scratch(BLK, 256),
            scratch(80, TOK),
            scratch(80, TOK),
            scratch(2 * BLK, PLEN),
            scratch(2 * BLK, PLEN),
            dma((4,)),
            dma((6,)),
            dma((6,)),
            dma((4,)),
            dma((len(IN.sends),)),
            dma((2, GX)),
            dma((2, GX)),
            dma((2, 16)),
            dma((2, 16)),
            dma((16,)),
            dma((16,)),
            dma((2, QUAD)),
            dma((2, QUAD)),
            dma((2, GX)),
            dma((2, GX)),
            dma((4,)),
            dma((len(OUT.sends),)),
            dma((3,)),
            dma((3,)),
        ],
        compiler_params=pltpu.CompilerParams(
            collective_id=0, has_side_effects=True, vmem_limit_bytes=56 * 2**20
        ),
        name="attention_block",
    )(cache_length, prefill_length, dtok, wkv, ptok, wq, wo, cache)


def body(
    prefill_tokens,
    prefill_lengths,
    decode_tokens,
    cache_lengths,
    cache_keyvals,
    query_weight,
    keyval_weight,
    out_weight,
):
    prefill_out, decode_out = run(
        cache_lengths,
        prefill_lengths,
        decode_tokens.transpose(0, 2, 1),
        keyval_weight.T,
        prefill_tokens,
        query_weight.T,
        out_weight,
        cache_keyvals[0],
    )
    return (prefill_out.T, decode_out.transpose(0, 2, 1))


def solution(mesh):
    in_specs = (
        P("gx", None),
        P("gx"),
        P(None, None, ("gx", "yz")),
        P(("gx", "yz")),
        P(("gx", "yz"), None, None),
        P("gx", "yz"),
        P("gx", "yz"),
        P("yz", "gx"),
    )
    out_specs = (P("gx", "yz"), P(None, None, ("gx", "yz")))
    return jax.shard_map(body, mesh=mesh, in_specs=in_specs, out_specs=out_specs, check_vma=False)
```

```python
import heapq

import jax
import jax.numpy as jnp
from jax import lax
from jax.experimental import pallas as pl
from jax.experimental.pallas import tpu as pltpu
from jax.sharding import PartitionSpec as P

HEADS = 48
HD = 256
PLEN = 128
GX, X, Z, YL = 4, 4, 8, 2
BLK = 144
TOK = 512
WIDTH_IN = {"p0": 1024, "p1": 1024, "da": 128, "db": 384}
WIDTH_OUT = {"pa": 256, "pb": 256, "da": 384, "db": 128}
START_IN = {"da": 0, "db": 128}
START = {"pa": 0, "pb": 256, "da": 0, "db": 384}
KINDS = tuple(START)
KINDS_IN = tuple(WIDTH_IN)
FAR = {"p0": 21.0, "p1": 27.0}
SPAN = Z * BLK
COLS = 192
KVC = 8
ROWS1 = 208
MESH = pl.DeviceIdType.MESH
F32 = jnp.float32
BF16 = jnp.bfloat16
FULL, UPPER, LOWER = (0, 144), (0, 80), (80, 64)
OPPOSITE = {"x+": "x-", "x-": "x+", "z+": "z-", "z-": "z+"}


def steps_from(key):
    kind, xo, zo = key
    out = []
    if kind in ("p0", "p1"):
        if xo == 0:
            out.append(("x+", FULL, (kind, -1, 0)))
            out.append(("x-", FULL, (kind, 1, 0)))
    elif kind[1] == "a":
        if xo == 0:
            if -3 < zo <= 0:
                out.append(("z+", FULL, (kind, 0, zo - 1)))
            if zo == -3:
                out.append(("z+", UPPER, (kind, 0, 4)))
            if 0 <= zo < 3:
                out.append(("z-", FULL, (kind, 0, zo + 1)))
            if zo == 3:
                out.append(("z-", LOWER, (kind, 0, 4)))
            out.append(("x+", FULL, (kind, -1, zo)))
            out.append(("x-", FULL, (kind, 1, zo)))
        elif xo == -1 and zo % 2 == 0:
            out.append(("x+", FULL, (kind, 2, zo)))
        elif xo == 1 and zo % 2 == 1:
            out.append(("x-", FULL, (kind, 2, zo)))
    else:
        if zo == 0:
            if xo == 0:
                out.append(("x+", FULL, (kind, -1, 0)))
                out.append(("x-", FULL, (kind, 1, 0)))
            elif xo == -1:
                out.append(("x+", UPPER, (kind, 2, 0)))
            elif xo == 1:
                out.append(("x-", LOWER, (kind, 2, 0)))
        if zo <= 0 and (zo > -3 or xo in (0, 2)):
            out.append(("z+", FULL, (kind, xo, zo - 1 if zo > -3 else 4)))
        if 0 <= zo <= 3 and (zo < 3 or xo in (-1, 1)):
            out.append(("z-", FULL, (kind, xo, zo + 1)))
    return out


class Plan:
    def __init__(self, releases, width):
        free = dict.fromkeys(OPPOSITE, 0.0)
        events, self.order, self.times, self.pieces = [], [], {}, {}
        self.sends, self.fills, self.source, self.where = {}, {}, {}, {}
        self.slots = dict.fromkeys(releases, 0)

        def leave(key, now):
            self.order.append(key)
            self.times[key] = now
            for n, (d, rows, there) in enumerate(steps_from(key)):
                free[d] = max(free[d], now) + width[key[0]] * rows[1] * 4e-5
                k = len(self.sends)
                self.sends[(key, n)] = k
                self.fills[(there, rows)] = k
                self.source[k] = (key, n)
                self.where[(key, n)] = self.slots[key[0]]
                self.slots[key[0]] += 1
                heapq.heappush(events, (free[d] + 3.0, k, there, (d, rows)))

        for n, kind in enumerate(releases):
            heapq.heappush(events, (releases[kind], n - len(releases), (kind, 0, 0), None))
            if kind in FAR:
                heapq.heappush(events, (FAR[kind], n - len(releases), (kind, 2, 0), None))
        while events:
            now, _, key, piece = heapq.heappop(events)
            if piece is not None:
                self.pieces.setdefault(key, []).append(piece)
            if piece is None or sum(p[1][1] for p in self.pieces[key]) == BLK:
                leave(key, now)
        self.end = max(self.times.values())


IN = Plan({"db": 0.0, "da": 0.0, "p0": 9.0, "p1": 15.0}, WIDTH_IN)
OUT = Plan({"db": 0.0, "da": 0.0, "pb": 25.0, "pa": 25.0}, WIDTH_OUT)
MIDDLE = {"p": (0.0, 4.5, 8.5, 13.0, 18.0, 22.0), "d": (0.0, 4.5, 10.5, 15.5, 23.5, 28.5, 33.0)}
QUAD = 4


def place():
    gx = lax.axis_index("gx")
    yz = lax.axis_index("yz")
    return gx, yz // (Z * YL), (yz // YL) % Z, yz % YL


def flat(x, z, yl):
    return x * (Z * YL) + z * YL + yl


def copy_rows(move):
    def four(g, carry):
        for j in range(QUAD):
            move(g // 4, (g % 4) * 2 + j // 2, j % 2, g, j)
        return carry

    lax.fori_loop(0, 16, four, 0)


def kernel(
    cache_length, prefill_length, dtok, wkv, ptok, wq, wo, cache_hbm,
    prefill_out, decode_out,
    gp0, gp1, gda, gdb, w, wov, wt, cache, tloc, xda, xdb, dsend, drecv,
    accp, accd, give, takep, taked, tok, tokp, backp, s1, r1, r2, qj, qjp, qh,
    kvown, k1, k2, att, heads, dec, dec2, ppa, ppb, pda, pdb, lpa, lpb, lda, ldb,
    opa, opb, oda, odb, psend, precv, dsend2, drecv2, pfin, pland,
    local, esend, erecv, send, recv, gsend, grecv, asend, arecv, ksend, krecv, qsend, qrecv, hsend, hrecv,
    osend, orecv, fsend, frecv,
):
    gx, x, z, yl = place()
    yz = lax.axis_index("yz")
    core, y_hi = gx % 2, gx // 2
    own = {"da": xda, "db": xdb}
    got = dict(zip(KINDS_IN, (gp0, gp1, gda, gdb)))
    result = dict(zip(KINDS, (opa, opb, oda, odb)))
    held = dict(zip(KINDS, (ppa, ppb, pda, pdb)))
    landing = dict(zip(KINDS, (lpa, lpb, lda, ldb)))
    acc = {"p": accp, "d": accd}
    take = {"p": takep, "d": taked}
    pending = []

    def near(d):
        dx = {"x+": 1, "x-": X - 1}.get(d, 0)
        dz = {"z+": 1, "z-": Z - 1}.get(d, 0)
        return (gx, flat((x + dx) % X, (z + dz) % Z, yl))

    g_peers = [((gx + s) % GX, yz) for s in range(1, GX)]
    there = 1 - y_hi
    across = [(2 * there + o, flat(x, z, 1 - yl)) for o in range(2)]
    z_peers = [(gx, flat(x, (z + s) % Z, yl)) for s in range(1, Z)]
    xy_peers = [(gx, flat((x + e // 2) % X, z, (yl + e) % YL)) for e in range(1, X * YL)]
    quad_first = (yz // QUAD) * QUAD
    place_in_quad = yz % QUAD
    quad_peers = [(gx, quad_first + (place_in_quad + s) % QUAD) for s in range(1, QUAD)]
    diagonal = (gx, flat(x, z + 1 - 2 * (z % 2), 1 - yl))

    def remote(src, dst, ssem, rsem, device):
        return pltpu.make_async_remote_copy(
            src_ref=src, dst_ref=dst, send_sem=ssem, recv_sem=rsem, device_id=device, device_id_type=MESH
        )

    def start(src, dst, ssem, rsem, device):
        c = remote(src, dst, ssem, rsem, device)
        c.start()
        pending.append(c)

    def arrive(dst, ssem, rsem):
        remote(dst, dst, ssem, rsem, near("x+")).wait_recv()

    barrier = pltpu.get_barrier_semaphore()
    peers = z_peers + xy_peers + [diagonal] + g_peers + across
    keeper = (x, flat(gx, z, yl))
    turned = x != gx

    for peer in peers:
        pl.semaphore_signal(barrier, inc=1, device_id=peer, device_id_type=MESH)

    @pl.when(turned)
    def _():
        pl.semaphore_signal(barrier, inc=1, device_id=keeper, device_id_type=MESH)

    group = wq.shape[1]
    loads = []

    def load(src, dst):
        c = pltpu.make_async_copy(src, dst, local.at[len(loads)])
        c.start()
        loads.append(c)
        return c

    dsend[:72, :256] = dtok[0]
    dsend[:72, 256:] = dtok[1]
    dsend[72:, :] = jnp.zeros((8, TOK), BF16)
    pl.semaphore_wait(barrier, len(peers) + turned.astype(jnp.int32))

    partner = (gx, flat(x, z, 1 - yl))
    start(dsend, drecv, esend.at[2], erecv.at[2], partner)
    for c in range(2):

        @pl.when(core == c)
        def _(c=c):
            for far in range(2):
                xx = (x + 2 * far) % X
                for o in range(2):
                    lane = pl.multiple_of((2 * there + o) * group + xx * SPAN, 128)
                    remote(
                        ptok.at[:, pl.ds(lane, SPAN)],
                        got["p%d" % c].at[xx],
                        esend.at[4 * far + o],
                        erecv.at[4 * far + c],
                        across[o],
                    ).start()

    w_load = load(wq, w.at[pl.ds(0, COLS)])
    mine_load = load(ptok.at[:, pl.ds(pl.multiple_of(gx * group, 128), group)], tloc.at[0])
    sibling_gx = gx + 1 - 2 * core
    start(
        ptok.at[:, pl.ds(pl.multiple_of(sibling_gx * group, 128), group)],
        tloc.at[1],
        esend.at[3],
        erecv.at[3],
        (sibling_gx, yz),
    )
    wo_load = load(wo, wov)
    cache_load = load(cache_hbm, cache)
    for ref in (tok, tokp, qj):
        ref[...] = jnp.zeros(ref.shape, F32)

    def slot(key, rows):
        kind, xo, zo = key
        if kind[0] == "p":
            return got[kind].at[(x + xo) % X]
        return got[kind].at[((x + xo) % X) * Z + (z + zo) % Z, pl.ds(rows[0], rows[1])]

    seen = {}

    def multiply(kind, xo):
        xx = (x + xo) % X
        part_of_w = w[:, pl.ds(pl.multiple_of(xx * SPAN, 128), SPAN)]
        if kind[0] == "p":
            part = lax.dot_general(
                part_of_w, got[kind][xx], (((1,), (1,)), ((), ())), preferred_element_type=F32
            )
            lanes = pl.ds(pl.multiple_of((2 * there + int(kind[1])) * 128, 128), 128)
        else:
            block = got[kind][pl.ds(xx * Z, Z)].reshape(SPAN, WIDTH_IN[kind])
            part = jnp.dot(part_of_w, block, preferred_element_type=F32)
            lanes = slice(START_IN[kind], START_IN[kind] + WIDTH_IN[kind])
        if kind in seen:
            acc[kind[0]][:, lanes] += part
        else:
            acc[kind[0]][:, lanes] = part
            seen[kind] = True

    def multiply_near(n):
        lanes = pl.ds(pl.multiple_of((gx if n == 0 else sibling_gx) * 128, 128), 128)
        acc["p"][:, lanes] = lax.dot_general(
            w[...], tloc[n], (((1,), (1,)), ((), ())), preferred_element_type=F32
        )

    def gather_node(key):
        kind, xo, zo = key
        mine = (xo, zo) == (0, 0)
        if xo == 2 and kind in FAR:
            c = 4 + int(kind[1])
            arrive(slot(key, FULL), esend.at[c], erecv.at[c])
        elif not mine:
            for _, rows in IN.pieces[key]:
                k = IN.fills[(key, rows)]
                arrive(slot(key, rows), send.at[KINDS_IN.index(kind)], recv.at[k])
        elif kind[0] == "p":
            c = int(kind[1])
            arrive(slot(key, FULL), esend.at[c], erecv.at[c])
        elif kind == "db":
            arrive(drecv, esend.at[2], erecv.at[2])
            one, two = dsend[:72].astype(F32), drecv[:72].astype(F32)
            both = jnp.where(
                yl == 0, jnp.concatenate([one, two], axis=0), jnp.concatenate([two, one], axis=0)
            ).astype(BF16)
            xda[...] = both[:, : WIDTH_IN["da"]]
            xdb[...] = both[:, WIDTH_IN["da"] :]
        for n, (d, rows, there) in enumerate(steps_from(key)):
            k = IN.sends[(key, n)]
            remote(
                own[kind] if mine and kind in own else slot(key, rows),
                slot(key, rows),
                send.at[KINDS_IN.index(kind)],
                recv.at[k],
                near(d),
            ).start()
        if mine and kind in own:
            got[kind][x * Z + z] = own[kind][...]
        seen[(kind, xo)] = seen.get((kind, xo), 0) + 1
        if seen[(kind, xo)] == (1 if kind[0] == "p" else Z):
            multiply(kind, xo)

    def sum_start(f):
        if f == "d":
            rows = accd[...]
            for g in range(GX):
                accd[:, g * 128 : g * 128 + 64] = rows[:, g * 64 : g * 64 + 64]
                accd[:, g * 128 + 64 : g * 128 + 128] = rows[:, 256 + g * 64 : 320 + g * 64]
        for g in range(GX):
            give[n_of[f], g] = acc[f][:, g * 128 : g * 128 + 128].astype(BF16)
        for s in range(1, GX):
            start(
                give.at[n_of[f], (gx + s) % GX],
                take[f].at[s - 1],
                gsend.at[n_of[f], s],
                grecv.at[n_of[f], s],
                g_peers[s - 1],
            )

    n_of = {"p": 0, "d": 1}

    def exchange_z(i):
        for s in range(1, Z):
            start(
                s1.at[i, :, (z + s) % Z],
                r1.at[i, :, z],
                asend.at[i, s],
                arecv.at[i, s],
                z_peers[s - 1],
            )
        r1[i, :, z] = s1[i, :, z]

    def exchange_xy(i):
        for s in range(1, Z):
            arrive(r1.at[i, :, (z + Z - s) % Z], asend.at[i, s], arecv.at[i, s])
        for e in range(1, X * YL):
            start(
                r1.at[i, (x + e // 2) % X, :, (yl + e) % YL],
                r2.at[i, x, :, yl],
                asend.at[i, Z + e],
                arecv.at[i, Z + e],
                xy_peers[e - 1],
            )
        r2[i, x, :, yl] = r1[i, x, :, yl]

    def exchange_end(i):
        for e in range(1, X * YL):
            arrive(
                r2.at[i, (x + X - e // 2) % X, :, (yl + e) % YL], asend.at[i, Z + e], arecv.at[i, Z + e]
            )

    def queries_start(f):
        for s in range(1, GX):
            arrive(take[f].at[s - 1], gsend.at[n_of[f], s], grecv.at[n_of[f], s])
        lane = pl.multiple_of(gx * 128, 128)
        total = acc[f][:, pl.ds(lane, 128)]
        for s in range(1, GX):
            total = total + take[f][s - 1].astype(F32)
        total = total.astype(BF16).astype(F32)
        if f == "p":
            tokp[:, :ROWS1] = total.T
            for s in range(1, QUAD):
                to = (place_in_quad + s) % QUAD
                start(
                    tokp.at[pl.ds(pl.multiple_of(32 * to, 32), 32)],
                    qjp.at[place_in_quad],
                    qsend.at[0, s],
                    qrecv.at[0, s],
                    quad_peers[s - 1],
                )
            qjp[place_in_quad] = tokp[pl.ds(pl.multiple_of(32 * place_in_quad, 32), 32), :]
            kvown[...] = total[COLS : COLS + KVC]
            for s in range(1, Z):
                start(kvown, k1.at[z], ksend.at[s], krecv.at[s], z_peers[s - 1])
            k1[z] = kvown[...]
            return
        tok[:, :ROWS1] = total.T

        def pack(xx, zz, yy, g, j):
            r = flat(xx, zz, yy)
            for t in range(2):
                s1[0, xx, zz, yy, pl.ds(t, 1), :] = tok[pl.ds(t * 64 + r, 1), :]

        copy_rows(pack)
        exchange_z(0)

    def queries_pass(f):
        if f == "d":
            exchange_xy(0)
            return
        for s in range(1, Z):
            arrive(k1.at[(z + Z - s) % Z], ksend.at[s], krecv.at[s])
        for e in range(1, X * YL):
            start(k1, k2.at[x, :, yl], ksend.at[Z + e], krecv.at[Z + e], xy_peers[e - 1])
        k2[x, :, yl] = k1[...]

    nt = (((1,), (1,)), ((), ()))
    scale = HD ** (-0.5)

    def attend(f):
        if f == "p":
            for s in range(1, QUAD):
                arrive(
                    qjp.at[(place_in_quad + QUAD - s) % QUAD], qsend.at[0, s], qrecv.at[0, s]
                )
            piece = qjp
        else:
            exchange_end(0)

            def unpack(xx, zz, yy, g, j):
                for t in range(2):
                    qj[j, pl.ds(t * 16 + g, 1), :] = r2[0, xx, zz, yy, pl.ds(t, 1), :]

            copy_rows(unpack)
            piece = qj
        qh[0:32, :192] = piece[0, :, :192]
        qh[0:32, 192:] = piece[1, :, :64]
        qh[32:64, :128] = piece[1, :, 64:192]
        qh[32:64, 128:] = piece[2, :, :128]
        qh[64:96, :64] = piece[2, :, 128:192]
        qh[64:96, 64:] = piece[3, :, :192]
        q32 = qh[...]
        q = q32.astype(BF16)
        if f == "p":
            for e in range(1, X * YL):
                arrive(k2.at[(x + X - e // 2) % X, :, (yl + e) % YL], ksend.at[Z + e], krecv.at[Z + e])
            kvt = k2[...].reshape(2 * HD, PLEN).astype(BF16)
            s = jnp.dot(q, kvt[:HD], preferred_element_type=F32) * scale
            query = 32 * place_in_quad + lax.broadcasted_iota(jnp.int32, s.shape, 0) % 32
            pos = lax.broadcasted_iota(jnp.int32, s.shape, 1)
            s = jnp.where((pos <= query) & (pos < prefill_length[0]), s, -1e30)
            e = jnp.exp(s - jnp.max(s, axis=1, keepdims=True))
            probs = (e / jnp.sum(e, axis=1, keepdims=True)).astype(BF16)
            out = lax.dot_general(probs, kvt[HD:], nt, preferred_element_type=F32)
        else:
            row = lax.broadcasted_iota(jnp.int32, (KVC, 2 * HD), 0)
            lane = lax.broadcasted_iota(jnp.int32, (KVC, 2 * HD), 1)
            spread = (lane % KVC == row).astype(BF16)
            group = lax.broadcasted_iota(jnp.int32, (32, 2 * HD), 0) % 16
            holder = lax.broadcasted_iota(jnp.int32, (32, 2 * HD), 1) // KVC
            new = jnp.zeros((32, 2 * HD), F32)
            for j in range(4):
                wide = jnp.dot(
                    qj[j, :, COLS : COLS + KVC].astype(BF16), spread, preferred_element_type=F32
                )
                new = new + jnp.where(holder == 4 * group + j, wide, 0.0)
            new0 = jnp.sum(new[:16], axis=0, keepdims=True)
            new1 = jnp.sum(new[16:], axis=0, keepdims=True)
            s = lax.dot_general(q, cache[:, :HD], nt, preferred_element_type=F32) * scale
            pos = lax.broadcasted_iota(jnp.int32, s.shape, 1)
            s = jnp.where(pos < cache_length[0], s, -1e30)
            f0 = jnp.sum(q32 * new0[:, :HD], axis=1, keepdims=True) * scale
            f1 = jnp.sum(q32 * new1[:, :HD], axis=1, keepdims=True) * scale
            step = (lax.broadcasted_iota(jnp.int32, f1.shape, 0) // 16) % 2
            f1 = jnp.where(step == 1, f1, -1e30)
            peak = jnp.maximum(jnp.max(s, axis=1, keepdims=True), jnp.maximum(f0, f1))
            es, e0, e1 = jnp.exp(s - peak), jnp.exp(f0 - peak), jnp.exp(f1 - peak)
            total = jnp.sum(es, axis=1, keepdims=True) + e0 + e1
            out = jnp.dot((es / total).astype(BF16), cache[:, HD:], preferred_element_type=F32)
            out = out + (e0 / total).astype(BF16).astype(F32) * new0[:, HD:]
            out = out + (e1 / total).astype(BF16).astype(F32) * new1[:, HD:]
        qh[...] = out.astype(BF16).astype(F32)
        piece[0, :, :192] = qh[0:32, :192]
        piece[1, :, :64] = qh[0:32, 192:]
        piece[1, :, 64:192] = qh[32:64, :128]
        piece[2, :, :128] = qh[32:64, 128:]
        piece[2, :, 128:192] = qh[64:96, :64]
        piece[3, :, :192] = qh[64:96, 64:]

        if f == "p":
            for s in range(1, QUAD):
                start(
                    piece.at[(place_in_quad + s) % QUAD],
                    backp.at[pl.ds(pl.multiple_of(32 * place_in_quad, 32), 32)],
                    qsend.at[1, s],
                    qrecv.at[1, s],
                    quad_peers[s - 1],
                )
            backp[pl.ds(pl.multiple_of(32 * place_in_quad, 32), 32), :] = piece[place_in_quad]
            return

        def pack(xx, zz, yy, g, j):
            for t in range(2):
                s1[1, xx, zz, yy, pl.ds(t, 1), :] = qj[j, pl.ds(t * 16 + g, 1), :]

        copy_rows(pack)
        exchange_z(1)

    def attended_pass(f):
        exchange_xy(1)

    def attended_share(f):
        n = n_of[f]
        if f == "p":
            for s in range(1, QUAD):
                first = 32 * ((place_in_quad + QUAD - s) % QUAD)
                arrive(
                    backp.at[pl.ds(pl.multiple_of(first, 32), 32)], qsend.at[1, s], qrecv.at[1, s]
                )
            att[n] = backp[...].T[:COLS].astype(BF16)
        else:
            exchange_end(1)

            def unpack(xx, zz, yy, g, j):
                r = flat(xx, zz, yy)
                for t in range(2):
                    tok[pl.ds(t * 64 + r, 1), :] = r2[1, xx, zz, yy, pl.ds(t, 1), :]

            copy_rows(unpack)
            att[n] = tok[...].T[:COLS].astype(BF16)
        for s in range(1, GX):
            start(att.at[n], heads.at[n, s], hsend.at[n, s], hrecv.at[n, s], g_peers[s - 1])
        heads[n, 0] = att[n]

    def attended_end(f):
        n = n_of[f]
        for s in range(1, GX):
            arrive(heads.at[n, s], hsend.at[n, s], hrecv.at[n, s])
        if f == "d":
            for s in range(GX):
                lane = pl.multiple_of(((gx - s + GX) % GX) * 128, 128)
                dec2[:, pl.ds(lane, 128)] = heads[n, s]
            for g in range(GX):
                for t in range(2):
                    dec[:, t * 256 + g * 64 : t * 256 + g * 64 + 64] = dec2[
                        :, g * 128 + t * 64 : g * 128 + t * 64 + 64
                    ]

    def terms(key):
        kind, xo, zo = key
        xx, zz = (x + xo) % X, (z + zo) % Z
        if kind[0] == "d":
            first = pl.multiple_of((xx * Z + zz) * BLK, 16)
            lanes = slice(START[kind], START[kind] + WIDTH_OUT[kind])
            return jnp.dot(wt[pl.ds(first, BLK), :], dec[:, lanes], preferred_element_type=F32)
        group = heads[0, (gx - xx + GX) % GX]
        parts = []
        for q in range(START[kind] // 128, (START[kind] + WIDTH_OUT[kind]) // 128):
            first = pl.multiple_of(zz * (4 * BLK) + q * BLK, 16)
            parts.append(jnp.dot(wt[pl.ds(first, BLK), :], group, preferred_element_type=F32))
        return jnp.concatenate(parts, axis=1)

    def scatter_node(key):
        kind, xo, zo = key
        last = (xo, zo) == (0, 0)
        at = ((x + xo) % X) * Z + (z + zo) % Z
        local = terms(key)
        steps = steps_from(key)
        for n, (d, rows, there) in enumerate(steps):
            k = OUT.sends[(key, n)]
            spot = landing[kind].at[OUT.where[(key, n)], pl.ds(rows[0], rows[1])]
            arrive(spot, osend.at[KINDS.index(kind)], orecv.at[k])
        halves = [local[:80], local[80:]]
        for n, (d, rows, there) in enumerate(steps):
            for i, (r0, rn) in enumerate((UPPER, LOWER)):
                if rows[0] <= r0 and r0 + rn <= rows[0] + rows[1]:
                    halves[i] = halves[i] + landing[kind][OUT.where[(key, n)], r0 : r0 + rn].astype(F32)
        for i, (r0, rn) in enumerate((UPPER, LOWER)):
            if last:
                result[kind][r0 : r0 + rn] = halves[i]
            else:
                held[kind][at, r0 : r0 + rn] = halves[i].astype(BF16)
        if not last:
            for d, rows in OUT.pieces[key]:
                k = OUT.fills[(key, rows)]
                remote(
                    held[kind].at[at, pl.ds(rows[0], rows[1])],
                    landing[kind].at[OUT.where[OUT.source[k]], pl.ds(rows[0], rows[1])],
                    osend.at[KINDS.index(kind)],
                    orecv.at[k],
                    near(OPPOSITE[d]),
                ).start()

    def prefill_halves():
        psend[...] = jnp.where(yl == 0, opb[...], opa[...]).astype(BF16)
        start(psend, precv, fsend.at[0], frecv.at[0], partner)

    def prefill_turn():
        arrive(precv, fsend.at[0], frecv.at[0])
        pre_sum = jnp.where(yl == 0, opa[...], opb[...]) + precv[...].astype(F32)
        for q in range(2):
            pfin[q * BLK : q * BLK + BLK] = pre_sum[:, q * 128 : q * 128 + 128].astype(BF16)

        @pl.when(turned)
        def _():
            remote(pfin, pland, fsend.at[2], frecv.at[2], keeper).start()

    def prefill_end():
        @pl.when(turned)
        def _():
            remote(pfin, pland, fsend.at[2], frecv.at[2], keeper).wait()
            prefill_out[...] = pland[...]

        @pl.when(x == gx)
        def _():
            prefill_out[...] = pfin[...]

    def weights():
        w_load.wait()
        w[COLS:, :] = jnp.concatenate([wkv[...].astype(F32), jnp.zeros((8, group), F32)]).astype(BF16)
        mine_load.wait()
        multiply_near(0)

    def turn_weights():
        wo_load.wait()
        for n in range(group // 512):
            wt[pl.ds(512 * n, 512), :] = wov[:, 512 * n : 512 * n + 512].T

    def sibling():
        arrive(tloc.at[1], esend.at[3], erecv.at[3])
        multiply_near(1)
        cache_load.wait()

    middle = {
        "p": (sum_start, queries_start, queries_pass, attend, attended_share, attended_end),
        "d": (
            sum_start,
            queries_start,
            queries_pass,
            attend,
            attended_pass,
            attended_share,
            attended_end,
        ),
    }
    todo = [(IN.times[key], gather_node, key) for key in IN.order]
    todo.append((1.5, lambda _: weights(), None))
    todo.append((9.0, lambda _: sibling(), None))
    ends = {}
    for f in "pd":
        ready = max(IN.times[key] for key in IN.order if key[0][0] == f) + 0.5
        todo += [(ready + after, step, f) for after, step in zip(MIDDLE[f], middle[f])]
        ends[f] = ready + MIDDLE[f][-1]
        if f == "p":
            todo.append((ready + MIDDLE["p"][1] + 0.1, lambda _: turn_weights(), None))
    begin = ends["p"] + 0.1
    out_times = {key: begin + OUT.end - OUT.times[key] for key in OUT.order}
    first_d = min(t for key, t in out_times.items() if key[0][0] == "d")
    shift = max(0.0, ends["d"] + 0.1 - first_d)
    for key in reversed(OUT.order):
        todo.append((out_times[key] + (shift if key[0][0] == "d" else 0.0), scatter_node, key))
    last_p = max(t for key, t in out_times.items() if key[0][0] == "p")
    todo.append((last_p + 0.1, lambda _: prefill_halves(), None))
    todo.append((last_p + 6.0, lambda _: prefill_turn(), None))
    for _, step, what in sorted(todo, key=lambda entry: entry[0]):
        step(what)

    dec_sum = jnp.concatenate([oda[...], odb[...]], axis=1)
    dsend2[:72] = jnp.where(yl == 0, dec_sum[72:], dec_sum[:72]).astype(BF16)
    dsend2[72:] = jnp.zeros((8, TOK), BF16)
    start(dsend2, drecv2, fsend.at[1], frecv.at[1], partner)
    prefill_end()
    arrive(drecv2, fsend.at[1], frecv.at[1])
    dec_sum = jnp.where(yl == 0, dec_sum[:72], dec_sum[72:]) + drecv2[:72].astype(F32)
    for t in range(2):
        decode_out[t] = dec_sum[:, t * 256 : t * 256 + 256].astype(BF16)

    for n, kind in enumerate(KINDS_IN):
        sent = got[kind].at[pl.ds(0, 2 if kind[0] == "p" else X * Z - 1)]
        remote(sent, sent, send.at[n], recv.at[0], partner).wait_send()
    for n, kind in enumerate(KINDS):
        sent = held[kind].at[pl.ds(0, X * Z - 1)]
        remote(sent, sent, osend.at[n], orecv.at[0], partner).wait_send()
    for o in (0, 1, 4, 5):
        sent = got["p0"].at[0]
        remote(sent, sent, esend.at[o], erecv.at[o], partner).wait_send()
    for c in pending:
        c.wait_send()


def run(cache_length, prefill_length, dtok, wkv, ptok, wq, wo, cache):
    vmem = pl.BlockSpec(memory_space=pltpu.VMEM)
    hbm = pl.BlockSpec(memory_space=pl.ANY)
    dma = pltpu.SemaphoreType.DMA
    group = wq.shape[1]

    def scratch(*shape, dtype=BF16):
        return pltpu.VMEM(shape, dtype)

    return pl.pallas_call(
        kernel,
        out_shape=(
            jax.ShapeDtypeStruct((2 * BLK, PLEN), BF16),
            jax.ShapeDtypeStruct((2, 72, 256), BF16),
        ),
        in_specs=[pl.BlockSpec(memory_space=pltpu.SMEM)] * 2 + [vmem, vmem, hbm, hbm, hbm, hbm],
        out_specs=(vmem, vmem),
        scratch_shapes=[
            scratch(X, PLEN, SPAN),
            scratch(X, PLEN, SPAN),
            scratch(X * Z, BLK, WIDTH_IN["da"]),
            scratch(X * Z, BLK, WIDTH_IN["db"]),
            scratch(ROWS1, group),
            scratch(COLS, group),
            scratch(group, COLS),
            scratch(*cache.shape),
            scratch(2, PLEN, group),
            scratch(BLK, WIDTH_IN["da"]),
            scratch(BLK, WIDTH_IN["db"]),
            scratch(80, TOK),
            scratch(80, TOK),
            scratch(ROWS1, TOK, dtype=F32),
            scratch(ROWS1, TOK, dtype=F32),
            scratch(2, GX, ROWS1, 128),
            scratch(GX - 1, ROWS1, 128),
            scratch(GX - 1, ROWS1, 128),
            scratch(128, 256, dtype=F32),
            scratch(128, 256, dtype=F32),
            scratch(128, 256, dtype=F32),
            scratch(2, X, Z, YL, 2, 256, dtype=F32),
            scratch(2, X, Z, YL, 2, 256, dtype=F32),
            scratch(2, X, Z, YL, 2, 256, dtype=F32),
            scratch(QUAD, 32, 256, dtype=F32),
            scratch(QUAD, 32, 256, dtype=F32),
            scratch(96, 256, dtype=F32),
            scratch(KVC, PLEN, dtype=F32),
            scratch(Z, KVC, PLEN, dtype=F32),
            scratch(X, Z, YL, KVC, PLEN, dtype=F32),
            scratch(2, COLS, 128),
            scratch(2, GX, COLS, 128),
            scratch(COLS, TOK),
            scratch(COLS, TOK),
        ]
        + [scratch(X * Z, BLK, WIDTH_OUT[k]) for k in KINDS]
        + [scratch(OUT.slots[k], BLK, WIDTH_OUT[k]) for k in KINDS]
        + [scratch(BLK, WIDTH_OUT[k], dtype=F32) for k in KINDS]
        + [
            scratch(BLK, 256),
            scratch(BLK, 256),
            scratch(80, TOK),
            scratch(80, TOK),
            scratch(2 * BLK, PLEN),
            scratch(2 * BLK, PLEN),
            dma((4,)),
            dma((6,)),
            dma((6,)),
            dma((4,)),
            dma((len(IN.sends),)),
            dma((2, GX)),
            dma((2, GX)),
            dma((2, 16)),
            dma((2, 16)),
            dma((16,)),
            dma((16,)),
            dma((2, QUAD)),
            dma((2, QUAD)),
            dma((2, GX)),
            dma((2, GX)),
            dma((4,)),
            dma((len(OUT.sends),)),
            dma((3,)),
            dma((3,)),
        ],
        compiler_params=pltpu.CompilerParams(
            collective_id=0, has_side_effects=True, vmem_limit_bytes=56 * 2**20
        ),
        name="attention_block",
    )(cache_length, prefill_length, dtok, wkv, ptok, wq, wo, cache)


def body(
    prefill_tokens,
    prefill_lengths,
    decode_tokens,
    cache_lengths,
    cache_keyvals,
    query_weight,
    keyval_weight,
    out_weight,
):
    prefill_out, decode_out = run(
        cache_lengths,
        prefill_lengths,
        decode_tokens.transpose(0, 2, 1),
        keyval_weight.T,
        prefill_tokens,
        query_weight.T,
        out_weight,
        cache_keyvals[0],
    )
    return (prefill_out.T, decode_out.transpose(0, 2, 1))


def solution(mesh):
    in_specs = (
        P("gx", None),
        P("gx"),
        P(None, None, ("gx", "yz")),
        P(("gx", "yz")),
        P(("gx", "yz"), None, None),
        P("gx", "yz"),
        P("gx", "yz"),
        P("yz", "gx"),
    )
    out_specs = (P("gx", "yz"), P(None, None, ("gx", "yz")))
    return jax.shard_map(body, mesh=mesh, in_specs=in_specs, out_specs=out_specs, check_vma=False)
```
